32 devices in a mesh: groups: 2 (over x), tiles: 16 (over z, y, core).
Axes of the slice: x: 2, y: 2, z: 4, core: 2. Of those that a mesh axis runs over, the one named last changes fastest.
Arguments:
- obs_position: float32 [2, 65536], P(None, ('groups', 'tiles')), parts along dimension 1, may hold values from 0 to 24, as said below
- obs_sd: float32 [65536], P(('groups', 'tiles')), parts along dimension 0, may hold values from 0.5 to 2
- obs_var: float32 [65536], P(('groups', 'tiles')), parts along dimension 0, may hold values from 0.5 to 2
- innovations: float32 [8, 65536], P(None, ('groups', 'tiles')), parts along dimension 1, may hold values from -12 to 12
- obs_target: int32 [65536], P(('groups', 'tiles')), parts along dimension 0, may hold values from 0 to 32767, as said below
- pair_table: int32 [32, 4, 2], P(('groups', 'tiles')), parts along dimension 0, may hold values from 0 to 15, as said below
- pair_count: int32 [32], P(('groups', 'tiles')), parts along dimension 0, may hold values from 1 to 4, as said below
Outputs:
- solution_field: float32 [8, 65536], P(None, ('groups', 'tiles')), parts along dimension 1
- residual: float32 [8, 65536], P(None, ('groups', 'tiles')), parts along dimension 1
The draws below stay inside these ranges and needn't reach their ends.
There are 2 independent parts, one for each index of `groups`. The reference program is written for one: setup_inputs(seed, part) draws one part's arguments, and reference() takes and returns one part's arrays. A program takes and returns all parts, laid end to end along the dimension named above; each array names one. Nothing has to cross between parts.
Inputs may be any that keep to these rules, and one draw needn't show every extreme that they name: A permutation; the tile of an observation is obs_target // 2048; of the rows of one device at most 192 go to any one tile, and exactly 192 to some tile. `pair_table`: row d holds (d, d), (d, d + 1), ..., (d, d + pair_count[d] - 1) in its first slots and (d, d) in the others; blocks of pairs that are not listed are zero. `pair_count`: equals 4 on some row. `obs_position`: the first coordinates of tile t lie between bounds of their own that rise with t; the second coordinate lies in 0 to 8.
All inputs are finite; a program needn't handle non-finite values.
Results may differ from the reference program's by a relative error of at most 0.0003.
Values sent between devices are 32-bit elements; how exact they have to be, the bound alone decides.
No kernel may reach another device: no remote copies, remote signals or barrier semaphores. Data moves between devices by JAX's collectives and lax.ppermute only.
A program may use at most 64 MiB of HBM per device.

```python
import math
import jax
import jax.numpy as jnp
from jax import lax

TILE = 2048
K = 8
ITERS = 2
PMAX = 4
TILES = 16
NOBS = 32768


def layout(key):
    tile_ids = jnp.arange(TILES, dtype=jnp.int32)
    widths = jax.random.randint(jax.random.fold_in(key, 11), (TILES,), 7, 29)
    chosen = jax.random.randint(jax.random.fold_in(key, 12), (), 0, TILES - 3)
    widths = jnp.where((tile_ids == chosen + 1) | (tile_ids == chosen + 2), 7, widths)
    bounds = jnp.cumsum(widths) - widths
    sign_list = jnp.where(jax.random.permutation(jax.random.fold_in(key, 13), TILES) < TILES // 2, 1, -1)
    base_load = TILE // TILES
    send_counts = base_load + base_load // 2 * sign_list[(tile_ids[None, :] - tile_ids[:, None]) % TILES]
    upper_ends = jnp.cumsum(send_counts, axis=1)
    before = jnp.cumsum(send_counts, axis=0) - send_counts
    slot_ids = jnp.arange(TILE, dtype=jnp.int32)
    scores = jax.random.randint(jax.random.fold_in(key, 14), (TILES, TILE), 0, 2 ** 18) * TILE + slot_ids[None, :]
    rank_order = jnp.argsort(scores, axis=1).astype(jnp.int32)
    owners = jnp.sum((upper_ends[:, None, :] <= rank_order[:, :, None]).astype(jnp.int32), axis=2)
    within = rank_order - jnp.take_along_axis(upper_ends - send_counts, owners, axis=1)
    offsets = before[tile_ids[:, None], owners]
    other_scores = jax.random.randint(jax.random.fold_in(key, 15), (TILES, TILE), 0, 2 ** 18) * TILE + slot_ids[None, :]
    places = jnp.argsort(other_scores, axis=1).astype(jnp.int32)
    slot_pick = places[owners, offsets + within]
    target = (owners * TILE + slot_pick).reshape(-1)
    return (widths, bounds, target)


def pair_grid(key):
    widths, bounds, target = layout(key)
    tile_ids = jnp.arange(TILES, dtype=jnp.int32)
    slot_ids = jnp.arange(PMAX, dtype=jnp.int32)
    partner = tile_ids[:, None] + slot_ids[None, :]
    end_edges = bounds + widths
    gap_units = bounds[jnp.minimum(partner, TILES - 1)] - end_edges[:, None]
    listed = (slot_ids[None, :] == 0) | (partner < TILES) & (gap_units < 20)
    return (tile_ids, partner, listed)


def draw_obs_target(key, part):
    widths, bounds, target = layout(key)
    return target.astype(jnp.int32)


def draw_pair_table(key, part):
    tile_ids, partner, listed = pair_grid(key)
    second = jnp.where(listed, partner, tile_ids[:, None])
    first_ids = jnp.broadcast_to(tile_ids[:, None], second.shape)
    return jnp.stack([first_ids, second], axis=-1).astype(jnp.int32)


def draw_pair_count(key, part):
    tile_ids, partner, listed = pair_grid(key)
    return jnp.sum(listed.astype(jnp.int32), axis=1).astype(jnp.int32)


def draw_obs_position(key, part):
    widths, bounds, target = layout(key)
    owner_tile = target // TILE
    across = jax.random.uniform(jax.random.fold_in(key, 21), (NOBS,), jnp.float32)
    upward = jax.random.uniform(jax.random.fold_in(key, 22), (NOBS,), jnp.float32)
    first_coord = (bounds[owner_tile].astype(jnp.float32) + widths[owner_tile].astype(jnp.float32) * across) / 20.0
    return jnp.stack([first_coord, 8.0 * upward]).astype(jnp.float32)


def draw_innovations(key, part):
    widths, bounds, target = layout(key)
    owner_tile = (target // TILE).astype(jnp.float32)
    rising = 3.0 ** (0.5 * owner_tile / (TILES - 1))
    values = jnp.clip(jax.random.normal(jax.random.fold_in(key, 31), (K, NOBS), jnp.float32), -6.0, 6.0)
    return (values * rising[None, :]).astype(jnp.float32)


def block_levels(rng, shape, split, smallest, largest):
    loudness = 1.0
    for position, blocks in split:
        heights = jax.random.uniform(jax.random.fold_in(jax.random.fold_in(rng, 6), position), (blocks,), jnp.float32, smallest / len(split), largest / len(split))
        loudness = loudness * jnp.repeat(jnp.exp(heights), shape[position] // blocks).reshape((-1,) + (1,) * (len(shape) - 1 - position))
    return loudness


def setup_inputs(seed: int = 0, part: int = 0) -> dict:
    seeds = jax.random.split(jax.random.key(seed), 8)
    part_splits = jax.random.split(jax.random.fold_in(seeds[7], part), 8)
    obs_position = draw_obs_position(jax.random.fold_in(jax.random.fold_in(seeds[7], part), 71), part)
    obs_sd = jnp.clip(jnp.exp(math.log(2.0) - 1.3862944 * jax.random.uniform(part_splits[1], (NOBS,), jnp.float32) ** block_levels(part_splits[1], (NOBS,), ((0, 16),), -0.2, 0.2)), 0.5, 2.0)
    obs_var = jnp.clip(jnp.exp(math.log(2.0) - 1.3862944 * jax.random.uniform(part_splits[2], (NOBS,), jnp.float32) ** block_levels(part_splits[2], (NOBS,), ((0, 16),), -0.2, 0.2)), 0.5, 2.0)
    innovations = draw_innovations(jax.random.fold_in(jax.random.fold_in(seeds[7], part), 71), part)
    obs_target = draw_obs_target(jax.random.fold_in(jax.random.fold_in(seeds[7], part), 71), part)
    pair_table = draw_pair_table(jax.random.fold_in(jax.random.fold_in(seeds[7], part), 71), part)
    pair_count = draw_pair_count(jax.random.fold_in(jax.random.fold_in(seeds[7], part), 71), part)
    return dict(obs_position=obs_position, obs_sd=obs_sd, obs_var=obs_var, innovations=innovations, obs_target=obs_target, pair_table=pair_table, pair_count=pair_count)


def wendland_block(row_geo, col_geo):
    delta_x = row_geo[0][:, None] - col_geo[0][None, :]
    delta_y = row_geo[1][:, None] - col_geo[1][None, :]
    distance = jnp.sqrt(delta_x * delta_x + delta_y * delta_y)
    inside = jnp.maximum(1.0 - distance, 0.0)
    squared = inside * inside
    return squared * squared * (4.0 * distance + 1.0) * row_geo[2][:, None] * col_geo[2][None, :]

def reference(obs_position, obs_sd, obs_var, innovations, obs_target, pair_table, pair_count):
    obs_total = obs_target.shape[0]
    placing = jnp.zeros((obs_total,), jnp.int32).at[obs_target].set(jnp.arange(obs_total, dtype=jnp.int32))
    geometry = jnp.concatenate([obs_position[:, placing], obs_sd[placing][None, :]], axis=0)
    variance = obs_var[placing]
    right_side = innovations[:, placing]
    slot_count = pair_table.shape[1]
    firsts = pair_table[:, :, 0].reshape(-1)
    seconds = pair_table[:, :, 1].reshape(-1)
    listed = (jnp.arange(slot_count, dtype=jnp.int32)[None, :] < pair_count[:, None]).reshape(-1)

    def operate(direction):

        def one_pair(image, item):
            first_tile, second_tile, present = item
            row_start = (first_tile * TILE).astype(jnp.int32)
            col_start = (second_tile * TILE).astype(jnp.int32)
            geo_first = lax.dynamic_slice_in_dim(geometry, row_start, TILE, 1)
            geo_second = lax.dynamic_slice_in_dim(geometry, col_start, TILE, 1)
            dir_first = lax.dynamic_slice_in_dim(direction, row_start, TILE, 1)
            dir_second = lax.dynamic_slice_in_dim(direction, col_start, TILE, 1)
            block_corr = wendland_block(geo_first, geo_second) * jnp.where(present, 1.0, 0.0)
            into_first = lax.dot_general(dir_second, block_corr, (((1,), (1,)), ((), ())), precision=lax.Precision.HIGHEST, preferred_element_type=jnp.float32)
            into_second = jnp.dot(dir_first, block_corr, precision=lax.Precision.HIGHEST, preferred_element_type=jnp.float32)
            into_second = into_second * jnp.where(first_tile != second_tile, 1.0, 0.0)
            current = lax.dynamic_slice_in_dim(image, row_start, TILE, 1)
            image = lax.dynamic_update_slice_in_dim(image, current + into_first, row_start, 1)
            current = lax.dynamic_slice_in_dim(image, col_start, TILE, 1)
            image = lax.dynamic_update_slice_in_dim(image, current + into_second, col_start, 1)
            return (image, None)
        image, unused = lax.scan(one_pair, variance[None, :] * direction, (firsts, seconds, listed))
        return image
    solution_field = jnp.zeros_like(right_side)
    residual = right_side
    direction = right_side
    norm_now = lax.optimization_barrier(jnp.sum(residual * residual, axis=1))
    for iteration in range(ITERS):
        image = operate(direction)
        alpha = norm_now / lax.optimization_barrier(jnp.sum(direction * image, axis=1))
        solution_field = solution_field + alpha[:, None] * direction
        residual = residual - alpha[:, None] * image
        norm_next = lax.optimization_barrier(jnp.sum(residual * residual, axis=1))
        direction = residual + (norm_next / norm_now)[:, None] * direction
        norm_now = norm_next
    return (solution_field, residual)
```

```python
import functools

import jax
import jax.numpy as jnp
from jax import lax
from jax.experimental import pallas as pl
from jax.experimental.pallas import tpu as pltpu
from jax.sharding import PartitionSpec as P

f32, bf16, i32 = jnp.float32, jnp.bfloat16, jnp.int32
LANES = 128
FIELDS = 16
BINS = 128
BATCH = 4
TRANSPOSED = (((1,), (1,)), ((), ()))
VMEM = pl.BlockSpec(memory_space=pltpu.VMEM)
SMEM = pl.BlockSpec(memory_space=pltpu.SMEM)
LIMIT = 40 * 2**20


def iota(shape, axis):
    return lax.broadcasted_iota(i32, shape, axis)


def running_sum_weights():
    shape = (LANES, 2 * LANES)
    row, col = iota(shape, 0), iota(shape, 1)
    return jnp.where((row <= col) | (col >= LANES), 1.0, 0.0).astype(bf16)


def dot(a, b):
    return jnp.dot(a, b, preferred_element_type=f32)


def dot_t(a, b):
    return lax.dot_general(a, b, TRANSPOSED, preferred_element_type=f32)


def invert(places, count):
    chunk_rows, lane_rows, here_rows, low_rows = [], [], [], []
    for chunk, place in enumerate(places):
        high = jnp.right_shift(place, 7)
        here = jnp.where(high == iota((count, LANES), 0), 1.0, 0.0)
        here_rows.append(here.astype(bf16))
        chunk_rows.append((here * float(chunk)).astype(bf16))
        lane_rows.append((here * iota((count, LANES), 1).astype(f32)).astype(bf16))
        low = jnp.bitwise_and(place, LANES - 1)
        low_rows.append(jnp.where(low == iota((LANES, LANES), 0), 1.0, 0.0).astype(bf16))
    left = jnp.concatenate(
        [jnp.concatenate(rows, axis=1) for rows in (chunk_rows, lane_rows, here_rows)], axis=0
    )
    found = dot_t(left, jnp.concatenate(low_rows, axis=1))
    chunk = found[:count].astype(i32)
    lane = found[count : 2 * count].astype(i32)
    return chunk, lane, found[2 * count :] > 0.5


def pick(load, sources, chunk, lane, here):
    total = None
    for source in range(sources):
        value = load(source)
        index = jnp.broadcast_to(lane, value.shape)
        value = jnp.take_along_axis(value, index, axis=1)
        total = value if total is None else jnp.where(chunk == source, value, total)
    return jnp.where(here, total, 0.0)


def outbox_kernel(
    tiles, width, pos_ref, sd_ref, var_ref, innov_ref, target_ref, out_ref, fields, inv_chunk, inv_lane, inv_here
):
    rows = pos_ref.shape[1]
    chunks = rows // LANES
    fields[...] = jnp.zeros_like(fields)
    fields[0:2, :] = pos_ref[...]
    fields[2:3, :] = sd_ref[...]
    fields[3:4, :] = var_ref[...]
    target = target_ref[...]
    owner = target // rows
    fields[12:13, :] = (target - owner * rows + 1).astype(f32)
    fields[4:12, :] = innov_ref[...]
    mine = [
        jnp.where(owner[:, c * LANES : (c + 1) * LANES] == iota((tiles, LANES), 0), 1.0, 0.0)
        for c in range(chunks)
    ]
    sums = dot(jnp.concatenate([m.astype(bf16) for m in mine], axis=0), running_sum_weights())
    before = (iota((tiles, LANES), 0) * width - 1).astype(f32)
    places = []
    for c in range(chunks):
        part = sums[c * tiles : (c + 1) * tiles]
        place = jnp.sum(mine[c] * (part[:, :LANES] + before), axis=0, keepdims=True)
        places.append(place.astype(i32))
        before = before + part[:, LANES:]
    count = tiles * width // LANES
    chunk, lane, here = invert(places, count)
    inv_chunk[...] = chunk
    inv_lane[...] = lane
    inv_here[...] = jnp.where(here, 1, 0)
    per_tile = width // LANES
    for d in range(count):
        out_ref[d // per_tile, :, (d % per_tile) * LANES : (d % per_tile + 1) * LANES] = pick(
            lambda s: fields[:, s * LANES : (s + 1) * LANES],
            chunks,
            inv_chunk[d : d + 1, :],
            inv_lane[d : d + 1, :],
            inv_here[d : d + 1, :] > 0,
        )


def sort_kernel(in_ref, count_ref, share_ref, own_ref, inv_chunk, inv_lane, rank_scr):
    tiles, _, width = in_ref.shape
    rows = own_ref.shape[1]
    chunks = rows // LANES
    per_tile = width // LANES
    sources = tiles * per_tile

    def load(s):
        return in_ref[s // per_tile, :, (s % per_tile) * LANES : (s % per_tile + 1) * LANES]

    weights = running_sum_weights()
    before = jnp.full((BINS, LANES), -1.0, f32)
    for s in range(sources):
        data = load(s)
        bins = jnp.clip((data[1:2] * (BINS / 8.0)).astype(i32), 0, BINS - 1)
        bins = jnp.where(data[12:13] > 0.5, bins, -1)
        member = jnp.where(bins == iota((BINS, LANES), 0), 1.0, 0.0)
        part = dot(member.astype(bf16), weights)
        rank_scr[s] = member * (part[:, :LANES] + before)
        before = before + part[:, LANES:]
    totals = before + 1.0
    high = jnp.floor(totals * (1.0 / 64.0))
    low = totals - 64.0 * high
    earlier = jnp.where(iota((BINS, BINS), 1) < iota((BINS, BINS), 0), 1.0, 0.0).astype(bf16)
    base = 64.0 * dot(earlier, high.astype(bf16)) + dot(earlier, low.astype(bf16))
    places = []
    for s in range(sources):
        data = load(s)
        bins = jnp.clip((data[1:2] * (BINS / 8.0)).astype(i32), 0, BINS - 1)
        here = data[12:13] > 0.5
        member = jnp.where(bins == iota((BINS, LANES), 0), base, 0.0)
        place = jnp.sum(member + rank_scr[s], axis=0, keepdims=True).astype(i32)
        places.append(jnp.where(here, place, -1))
    chunk, lane, here = invert(places, chunks)
    inv_chunk[...] = chunk
    inv_lane[...] = lane
    for d in range(chunks):
        own_ref[:, d * LANES : (d + 1) * LANES] = pick(
            load, sources, inv_chunk[d : d + 1, :], inv_lane[d : d + 1, :], inv_lane[d : d + 1, :] >= 0
        )
    share_ref[...] = jnp.zeros_like(share_ref)
    share_ref[0:8, :] = own_ref[4:12, :] * (own_ref[2:3, :] * (1.0 / 256.0))
    share_ref[8:10, :] = own_ref[0:2, :] * 4.0
    stat = jnp.zeros((1, LANES), f32)
    for axis in range(2):
        wide = jnp.concatenate(
            [share_ref[8 + axis : 9 + axis, c * LANES : (c + 1) * LANES] for c in range(chunks)], axis=0
        )
        for which, value in ((0, jnp.min(wide, axis=1, keepdims=True)), (1, jnp.max(wide, axis=1, keepdims=True))):
            lanes = iota((chunks, LANES), 1) - chunks * (2 * axis + which)
            stat = stat + jnp.sum(
                jnp.where(lanes == iota((chunks, LANES), 0), value, 0.0), axis=0, keepdims=True
            )
    stat = jnp.where(iota((1, LANES), 1) == 4 * chunks, count_ref[0].astype(f32), stat)
    share_ref[10:11, 0:LANES] = stat


def make_list(hops, tile_ref, shares, list_ref):
    chunks = list_ref.shape[0]
    my_tile = tile_ref[0]
    own = shares[hops][10:11, 0:LANES]
    lane, sub = iota((chunks, LANES), 1), iota((chunks, LANES), 0)
    x_low, x_high, y_low, y_high = [
        jnp.sum(jnp.where(lane == sub + chunks * q, own, 0.0), axis=1, keepdims=True) for q in range(4)
    ]
    own_count = own[:, 4 * chunks : 4 * chunks + 1]
    need = jnp.zeros((chunks, LANES), f32)
    for nb in range(2 * hops + 1):
        hop = nb - hops
        other = shares[nb][10:11, 0:LANES]
        at = [pltpu.roll(other, (nb * chunks - q * chunks) % LANES, 1) for q in range(4)]
        gap_x = jnp.maximum(jnp.maximum(at[0] - x_high, x_low - at[1]), 0.0)
        gap_y = jnp.maximum(jnp.maximum(at[2] - y_high, y_low - at[3]), 0.0)
        near = gap_x * gap_x + gap_y * gap_y < 16.001
        count = own_count if hop >= 0 else other[:, 4 * chunks : 4 * chunks + 1]
        listed = (count > abs(hop) + 0.5) & (my_tile + hop >= 0)
        inside = (lane >= nb * chunks) & (lane < (nb + 1) * chunks)
        need = need + jnp.where(near & listed & inside, 1.0, 0.0)
    total = dot(need.astype(bf16), running_sum_weights())
    slot = jnp.where(need > 0.5, total[:, :LANES] - 1.0, -1.0)
    numbers = jnp.broadcast_to(iota((8, LANES), 1).astype(f32), (8, LANES)).astype(bf16)
    for r in range(chunks):
        match = jnp.where(slot[r : r + 1] == iota((LANES, LANES), 0).astype(f32), 1.0, 0.0)
        found = dot_t(numbers, match.astype(bf16))[0:1]
        amount = total[r : r + 1, LANES:]
        row = jnp.where(iota((1, LANES), 1).astype(f32) < amount, found, float((2 * hops + 1) * chunks))
        row = jnp.where(iota((1, LANES), 1) == LANES - 1, amount, row)
        list_ref[r : r + 1, :] = row.astype(i32)


def load_operands(hops, shares, vectors, where_scr, vec_scr):
    chunks = shares[0].shape[1] // LANES
    for nb in range(2 * hops + 1):
        for c in range(chunks):
            lanes = slice(c * LANES, (c + 1) * LANES)
            where_scr[nb * chunks + c] = shares[nb][8:16, lanes]
            value = vectors[nb][0:8, lanes]
            high = value.astype(bf16)
            low = (value - high.astype(f32)).astype(bf16)
            vec_scr[nb * chunks + c] = jnp.concatenate([high, low], axis=0)
    last = (2 * hops + 1) * chunks
    where_scr[last] = jnp.zeros((8, LANES), f32)
    vec_scr[last] = jnp.zeros((16, LANES), bf16)


def product(hops, list_smem, where_scr, vec_scr, out_ref):
    chunks = out_ref.shape[1] // LANES

    def chunk_rows(r, _):
        column = where_scr[hops * chunks + r].T
        x_col = jnp.broadcast_to(column[:, 0:1], (LANES, LANES))
        y_col = jnp.broadcast_to(column[:, 1:2], (LANES, LANES))

        def batch(b, total):
            highs, lows, vecs = [], [], []
            for j in range(BATCH):
                c = list_smem[r, b * BATCH + j]
                dx = x_col - where_scr[c, 0:1, :]
                dy = y_col - where_scr[c, 1:2, :]
                square = jnp.maximum(dx * dx + dy * dy, 1e-30)
                distance = square * lax.rsqrt(square)
                inside = jnp.maximum(4.0 - distance, 0.0)
                inside = inside * inside
                corr = inside * inside * (distance + 1.0)
                high = corr.astype(bf16)
                highs.append(high)
                lows.append((corr - high.astype(f32)).astype(bf16))
                vecs.append(vec_scr[c])
            return total + dot_t(
                jnp.concatenate(highs + lows, axis=1), jnp.concatenate(vecs + vecs, axis=1)
            )

        steps = (list_smem[r, LANES - 1] + (BATCH - 1)) // BATCH
        total = lax.fori_loop(0, steps, batch, jnp.zeros((LANES, 16), f32))
        flat = total.T
        out_ref[:, pl.ds(pl.multiple_of(r * LANES, LANES), LANES)] = flat[0:8] + flat[8:16]
        return 0

    lax.fori_loop(0, chunks, chunk_rows, 0)


def first_kernel(hops, tile_ref, own_ref, *refs):
    shares = refs[: 2 * hops + 1]
    image_ref, share_ref, dots_ref, list_ref, list_smem, where_scr, vec_scr, sem = refs[2 * hops + 1 :]
    make_list(hops, tile_ref, shares, list_ref)
    copy = pltpu.make_async_copy(list_ref, list_smem, sem)
    copy.start()
    load_operands(hops, shares, shares, where_scr, vec_scr)
    copy.wait()
    product(hops, list_smem, where_scr, vec_scr, image_ref)
    field = own_ref[4:12, :]
    image = own_ref[3:4, :] * field + own_ref[2:3, :] * image_ref[...]
    image_ref[...] = image
    share_ref[...] = image * (own_ref[2:3, :] * (1.0 / 256.0))
    dots_ref[:, 0:128] = jnp.broadcast_to(jnp.sum(field * field, axis=1, keepdims=True), (8, LANES))
    dots_ref[:, 128:256] = jnp.broadcast_to(jnp.sum(field * image, axis=1, keepdims=True), (8, LANES))
    dots_ref[:, 256:384] = jnp.broadcast_to(jnp.sum(image * image, axis=1, keepdims=True), (8, LANES))


def second_kernel(hops, list_smem, own_ref, image_ref, *refs):
    n = 2 * hops + 1
    shares, vectors = refs[:n], refs[n : 2 * n]
    twice_ref, where_scr, vec_scr = refs[2 * n :]
    load_operands(hops, shares, vectors, where_scr, vec_scr)
    product(hops, list_smem, where_scr, vec_scr, twice_ref)
    twice_ref[...] = own_ref[3:4, :] * image_ref[...] + own_ref[2:3, :] * twice_ref[...]


def place_kernel(own_ref, data_ref, out_ref, inv_chunk, inv_lane):
    chunks = own_ref.shape[1] // LANES
    places = [own_ref[12:13, c * LANES : (c + 1) * LANES].astype(i32) - 1 for c in range(chunks)]
    chunk, lane, _ = invert(places, chunks)
    inv_chunk[...] = chunk
    inv_lane[...] = lane
    for d in range(chunks):
        out_ref[:, d * LANES : (d + 1) * LANES] = pick(
            lambda s: data_ref[:, s * LANES : (s + 1) * LANES],
            chunks,
            inv_chunk[d : d + 1, :],
            inv_lane[d : d + 1, :],
            inv_lane[d : d + 1, :] >= 0,
        )


def call(kernel, outs, ins, scratch=()):
    return pl.pallas_call(
        kernel,
        out_shape=[jax.ShapeDtypeStruct(shape, kind) for shape, kind in outs],
        in_specs=ins,
        out_specs=[VMEM] * len(outs),
        scratch_shapes=list(scratch),
        compiler_params=pltpu.CompilerParams(vmem_limit_bytes=LIMIT),
    )


def around(value, hops, tiles):
    got = {0: value}
    for hop in range(1, hops + 1):
        for sign in (1, -1):
            pairs = [(i, (i - sign * hop) % tiles) for i in range(tiles)]
            got[sign * hop] = lax.ppermute(value, "tiles", pairs)
    return [got[hop] for hop in range(-hops, hops + 1)]


def local(obs_position, obs_sd, obs_var, innovations, obs_target, pair_table, pair_count):
    tiles = lax.axis_size("tiles")
    my_tile = lax.axis_index("tiles").astype(i32)
    rows = obs_sd.shape[0]
    chunks = rows // LANES
    hops = pair_table.shape[1] - 1
    held = (2 * hops + 1) * chunks
    capacity = 3 * rows // (2 * tiles)
    width = -(-capacity // LANES) * LANES
    boxes = tiles * width // LANES

    (outbox,) = call(
        functools.partial(outbox_kernel, tiles, width),
        [((tiles, FIELDS, width), f32)],
        [VMEM] * 5,
        [pltpu.VMEM((FIELDS, rows), f32)] + [pltpu.VMEM((boxes, LANES), i32)] * 3,
    )(obs_position, obs_sd[None], obs_var[None], innovations, obs_target[None])
    inbox = lax.all_to_all(outbox, "tiles", split_axis=0, concat_axis=0, tiled=True)
    share, own = call(
        sort_kernel,
        [((FIELDS, rows), f32), ((FIELDS, rows), f32)],
        [VMEM, SMEM],
        [pltpu.VMEM((chunks, LANES), i32)] * 2 + [pltpu.VMEM((boxes, BINS, LANES), f32)],
    )(inbox, pair_count)
    shares = around(share, hops, tiles)
    operands = [pltpu.VMEM((held + 1, 8, LANES), f32), pltpu.VMEM((held + 1, 16, LANES), bf16)]
    image, image_share, dots, near = call(
        functools.partial(first_kernel, hops),
        [((8, rows), f32), ((8, rows), f32), ((8, 3 * LANES), f32), ((chunks, LANES), i32)],
        [SMEM] + [VMEM] * (2 * hops + 2),
        [pltpu.SMEM((chunks, LANES), i32)] + operands + [pltpu.SemaphoreType.DMA],
    )(my_tile[None], own, *shares)
    vectors = around(image_share, hops, tiles)
    (twice,) = call(
        functools.partial(second_kernel, hops),
        [((8, rows), f32)],
        [SMEM] + [VMEM] * (4 * hops + 4),
        operands,
    )(near, own, image, *shares, *vectors)

    sums = jnp.sum(lax.all_gather(dots, "tiles"), axis=0)
    norm, power, size = sums[:, 0:1], sums[:, 128:129], sums[:, 256:257]
    field = own[4:12]
    alpha = norm / power
    beta = (alpha * alpha * size - norm) / norm
    residual = field - alpha * image
    direction = residual + beta * field
    moved = (1.0 + beta) * image - alpha * twice
    parts = jnp.concatenate(
        [
            jnp.broadcast_to(jnp.sum(residual * residual, axis=1, keepdims=True), (8, 64)),
            jnp.broadcast_to(jnp.sum(direction * moved, axis=1, keepdims=True), (8, 64)),
        ],
        axis=1,
    )
    both = lax.all_to_all(
        jnp.broadcast_to(parts[None], (tiles, 8, LANES)), "tiles", split_axis=0, concat_axis=0, tiled=True
    )
    both = jnp.sum(both, axis=0)
    alpha_next = both[:, 0:1] / both[:, 64:65]
    data = jnp.concatenate(
        [alpha * field + alpha_next * direction, residual - alpha_next * moved], axis=0
    )
    (placed,) = call(
        place_kernel, [((16, rows), f32)], [VMEM, VMEM], [pltpu.VMEM((chunks, LANES), i32)] * 2
    )(own, data)
    return (placed[0:8], placed[8:16])


def solution(mesh):
    both = ("groups", "tiles")
    placed = (P(None, both), P(both), P(both), P(None, both), P(both), P(both, None, None), P(both))
    return jax.shard_map(
        local,
        mesh=mesh,
        in_specs=placed,
        out_specs=(P(None, both), P(None, both)),
        check_vma=False,
    )
```

```python
import functools

import jax
import jax.numpy as jnp
from jax import lax
from jax.experimental import pallas as pl
from jax.experimental.pallas import tpu as pltpu
from jax.sharding import PartitionSpec as P

f32, bf16, i32 = jnp.float32, jnp.bfloat16, jnp.int32
LANES = 128
FIELDS = 16
BINS = 128
BATCH = 16
TRANSPOSED = (((1,), (1,)), ((), ()))
VMEM = pl.BlockSpec(memory_space=pltpu.VMEM)
SMEM = pl.BlockSpec(memory_space=pltpu.SMEM)
LIMIT = 40 * 2**20


def iota(shape, axis):
    return lax.broadcasted_iota(i32, shape, axis)


def running_sum_weights():
    shape = (LANES, 2 * LANES)
    row, col = iota(shape, 0), iota(shape, 1)
    return jnp.where((row <= col) | (col >= LANES), 1.0, 0.0).astype(bf16)


def dot(a, b):
    return jnp.dot(a, b, preferred_element_type=f32)


def dot_t(a, b):
    return lax.dot_general(a, b, TRANSPOSED, preferred_element_type=f32)


def invert(places, count):
    chunk_rows, lane_rows, here_rows, low_rows = [], [], [], []
    for chunk, place in enumerate(places):
        high = jnp.right_shift(place, 7)
        here = jnp.where(high == iota((count, LANES), 0), 1.0, 0.0)
        here_rows.append(here.astype(bf16))
        chunk_rows.append((here * float(chunk)).astype(bf16))
        lane_rows.append((here * iota((count, LANES), 1).astype(f32)).astype(bf16))
        low = jnp.bitwise_and(place, LANES - 1)
        low_rows.append(jnp.where(low == iota((LANES, LANES), 0), 1.0, 0.0).astype(bf16))
    left = jnp.concatenate(
        [jnp.concatenate(rows, axis=1) for rows in (chunk_rows, lane_rows, here_rows)], axis=0
    )
    found = dot_t(left, jnp.concatenate(low_rows, axis=1))
    chunk = found[:count].astype(i32)
    lane = found[count : 2 * count].astype(i32)
    return chunk, lane, found[2 * count :] > 0.5


def pick(load, sources, chunk, lane, here):
    total = None
    for source in range(sources):
        value = load(source)
        index = jnp.broadcast_to(lane, value.shape)
        value = jnp.take_along_axis(value, index, axis=1)
        total = value if total is None else jnp.where(chunk == source, value, total)
    return jnp.where(here, total, 0.0)


def outbox_kernel(
    tiles,
    width,
    pos_ref,
    sd_ref,
    var_ref,
    innov_ref,
    target_ref,
    out_ref,
    fields,
    pos_scr,
    sd_scr,
    var_scr,
    innov_scr,
    target_scr,
    inv_chunk,
    inv_lane,
    inv_here,
    sems,
):
    rows = pos_ref.shape[1]
    chunks = rows // LANES
    copies = [
        pltpu.make_async_copy(source, target, sems.at[k])
        for k, (source, target) in enumerate(
            (
                (target_ref, target_scr),
                (pos_ref, pos_scr),
                (sd_ref, sd_scr),
                (var_ref, var_scr),
                (innov_ref, innov_scr),
            )
        )
    ]
    for copy in copies:
        copy.start()
    fields[...] = jnp.zeros_like(fields)
    for copy in copies:
        copy.wait()
    fields[0:2, :] = pos_scr[...]
    fields[2:3, :] = sd_scr[...]
    fields[3:4, :] = var_scr[...]
    target = target_scr[...]
    owner = target // rows
    fields[12:13, :] = (target - owner * rows + 1).astype(f32)
    fields[4:12, :] = innov_scr[...]
    mine = [
        jnp.where(owner[:, c * LANES : (c + 1) * LANES] == iota((tiles, LANES), 0), 1.0, 0.0)
        for c in range(chunks)
    ]
    sums = dot(jnp.concatenate([m.astype(bf16) for m in mine], axis=0), running_sum_weights())
    before = (iota((tiles, LANES), 0) * width - 1).astype(f32)
    places = []
    for c in range(chunks):
        part = sums[c * tiles : (c + 1) * tiles]
        place = jnp.sum(mine[c] * (part[:, :LANES] + before), axis=0, keepdims=True)
        places.append(place.astype(i32))
        before = before + part[:, LANES:]
    count = tiles * width // LANES
    chunk, lane, here = invert(places, count)
    inv_chunk[...] = chunk
    inv_lane[...] = lane
    inv_here[...] = jnp.where(here, 1, 0)
    per_tile = width // LANES
    for d in range(count):
        out_ref[d // per_tile, :, (d % per_tile) * LANES : (d % per_tile + 1) * LANES] = pick(
            lambda s: fields[:, s * LANES : (s + 1) * LANES],
            chunks,
            inv_chunk[d : d + 1, :],
            inv_lane[d : d + 1, :],
            inv_here[d : d + 1, :] > 0,
        )


def sort_kernel(in_ref, count_ref, share_ref, own_ref, inv_chunk, inv_lane, rank_scr):
    tiles, _, width = in_ref.shape
    rows = own_ref.shape[1]
    chunks = rows // LANES
    per_tile = width // LANES
    sources = tiles * per_tile

    def load(s):
        return in_ref[s // per_tile, :, (s % per_tile) * LANES : (s % per_tile + 1) * LANES]

    weights = running_sum_weights()
    before = jnp.full((BINS, LANES), -1.0, f32)
    for s in range(sources):
        data = load(s)
        bins = jnp.clip((data[1:2] * (BINS / 8.0)).astype(i32), 0, BINS - 1)
        bins = jnp.where(data[12:13] > 0.5, bins, -1)
        member = jnp.where(bins == iota((BINS, LANES), 0), 1.0, 0.0)
        part = dot(member.astype(bf16), weights)
        rank_scr[s] = member * (part[:, :LANES] + before)
        before = before + part[:, LANES:]
    totals = before + 1.0
    high = jnp.floor(totals * (1.0 / 64.0))
    low = totals - 64.0 * high
    earlier = jnp.where(iota((BINS, BINS), 1) < iota((BINS, BINS), 0), 1.0, 0.0).astype(bf16)
    base = 64.0 * dot(earlier, high.astype(bf16)) + dot(earlier, low.astype(bf16))
    places = []
    for s in range(sources):
        data = load(s)
        bins = jnp.clip((data[1:2] * (BINS / 8.0)).astype(i32), 0, BINS - 1)
        here = data[12:13] > 0.5
        member = jnp.where(bins == iota((BINS, LANES), 0), base, 0.0)
        place = jnp.sum(member + rank_scr[s], axis=0, keepdims=True).astype(i32)
        places.append(jnp.where(here, place, -1))
    chunk, lane, here = invert(places, chunks)
    inv_chunk[...] = chunk
    inv_lane[...] = lane
    for d in range(chunks):
        own_ref[:, d * LANES : (d + 1) * LANES] = pick(
            load, sources, inv_chunk[d : d + 1, :], inv_lane[d : d + 1, :], inv_lane[d : d + 1, :] >= 0
        )
    share_ref[...] = jnp.zeros_like(share_ref)
    share_ref[0:8, :] = own_ref[4:12, :] * (own_ref[2:3, :] * (1.0 / 256.0))
    share_ref[8:10, :] = own_ref[0:2, :] * 4.0
    stat = jnp.zeros((1, LANES), f32)
    for axis in range(2):
        wide = jnp.concatenate(
            [share_ref[8 + axis : 9 + axis, c * LANES : (c + 1) * LANES] for c in range(chunks)], axis=0
        )
        for which, value in ((0, jnp.min(wide, axis=1, keepdims=True)), (1, jnp.max(wide, axis=1, keepdims=True))):
            lanes = iota((chunks, LANES), 1) - chunks * (2 * axis + which)
            stat = stat + jnp.sum(
                jnp.where(lanes == iota((chunks, LANES), 0), value, 0.0), axis=0, keepdims=True
            )
    stat = jnp.where(iota((1, LANES), 1) == 4 * chunks, count_ref[0].astype(f32), stat)
    share_ref[10:11, 0:LANES] = stat


def make_list(hops, tile_ref, shares, list_ref):
    chunks = list_ref.shape[0]
    my_tile = tile_ref[0]
    own = shares[hops][10:11, 0:LANES]
    lane, sub = iota((chunks, LANES), 1), iota((chunks, LANES), 0)
    x_low, x_high, y_low, y_high = [
        jnp.sum(jnp.where(lane == sub + chunks * q, own, 0.0), axis=1, keepdims=True) for q in range(4)
    ]
    own_count = own[:, 4 * chunks : 4 * chunks + 1]
    need = jnp.zeros((chunks, LANES), f32)
    for nb in range(2 * hops + 1):
        hop = nb - hops
        other = shares[nb][10:11, 0:LANES]
        at = [pltpu.roll(other, (nb * chunks - q * chunks) % LANES, 1) for q in range(4)]
        gap_x = jnp.maximum(jnp.maximum(at[0] - x_high, x_low - at[1]), 0.0)
        gap_y = jnp.maximum(jnp.maximum(at[2] - y_high, y_low - at[3]), 0.0)
        near = gap_x * gap_x + gap_y * gap_y < 16.001
        count = own_count if hop >= 0 else other[:, 4 * chunks : 4 * chunks + 1]
        listed = (count > abs(hop) + 0.5) & (my_tile + hop >= 0)
        inside = (lane >= nb * chunks) & (lane < (nb + 1) * chunks)
        need = need + jnp.where(near & listed & inside, 1.0, 0.0)
    total = dot(need.astype(bf16), running_sum_weights())
    slot = jnp.where(need > 0.5, total[:, :LANES] - 1.0, -1.0)
    numbers = jnp.broadcast_to(iota((8, LANES), 1).astype(f32), (8, LANES)).astype(bf16)
    for r in range(chunks):
        match = jnp.where(slot[r : r + 1] == iota((LANES, LANES), 0).astype(f32), 1.0, 0.0)
        found = dot_t(numbers, match.astype(bf16))[0:1]
        amount = total[r : r + 1, LANES:]
        row = jnp.where(iota((1, LANES), 1).astype(f32) < amount, found, float((2 * hops + 1) * chunks))
        row = jnp.where(iota((1, LANES), 1) == LANES - 1, amount, row)
        list_ref[r : r + 1, :] = row.astype(i32)


def load_operands(hops, shares, vectors, where_scr, vec_scr):
    chunks = shares[0].shape[1] // LANES
    for nb in range(2 * hops + 1):
        for c in range(chunks):
            lanes = slice(c * LANES, (c + 1) * LANES)
            where_scr[nb * chunks + c] = shares[nb][8:16, lanes]
            value = vectors[nb][0:8, lanes]
            high = value.astype(bf16)
            low = (value - high.astype(f32)).astype(bf16)
            vec_scr[nb * chunks + c] = jnp.concatenate([high, low], axis=0)
    last = (2 * hops + 1) * chunks
    where_scr[last] = jnp.zeros((8, LANES), f32)
    vec_scr[last] = jnp.zeros((16, LANES), bf16)


def product(hops, list_smem, where_scr, vec_scr, out_ref):
    chunks = out_ref.shape[1] // LANES

    def chunk_rows(r, _):
        column = where_scr[hops * chunks + r].T
        x_col = jnp.broadcast_to(column[:, 0:1], (LANES, LANES))
        y_col = jnp.broadcast_to(column[:, 1:2], (LANES, LANES))

        def batch(start, size, total):
            highs, lows, vecs = [], [], []
            for j in range(size):
                c = list_smem[r, start + j]
                dx = x_col - where_scr[c, 0:1, :]
                dy = y_col - where_scr[c, 1:2, :]
                square = jnp.maximum(dx * dx + dy * dy, 1e-30)
                distance = square * lax.rsqrt(square)
                inside = jnp.maximum(4.0 - distance, 0.0)
                inside = inside * inside
                corr = inside * inside * (distance + 1.0)
                high = corr.astype(bf16)
                highs.append(high)
                lows.append((corr - high.astype(f32)).astype(bf16))
                vecs.append(vec_scr[c])
            vec = jnp.concatenate(vecs, axis=1)
            total = total + dot_t(vec, jnp.concatenate(highs, axis=1))
            return total + dot_t(vec, jnp.concatenate(lows, axis=1))

        amount = list_smem[r, LANES - 1]
        full = amount // BATCH
        total = lax.fori_loop(
            0, full, lambda b, t: batch(b * BATCH, BATCH, t), jnp.zeros((16, LANES), f32)
        )
        left = (amount - full * BATCH + 3) // 4
        for size in range(4, BATCH + 1, 4):
            total = lax.cond(
                left == size // 4, lambda t, size=size: batch(full * BATCH, size, t), lambda t: t, total
            )
        out_ref[:, pl.ds(pl.multiple_of(r * LANES, LANES), LANES)] = total[0:8] + total[8:16]
        return 0

    lax.fori_loop(0, chunks, chunk_rows, 0)


def first_kernel(hops, tile_ref, own_ref, *refs):
    shares = refs[: 2 * hops + 1]
    image_ref, share_ref, dots_ref, list_ref, list_smem, where_scr, vec_scr, sem = refs[2 * hops + 1 :]
    make_list(hops, tile_ref, shares, list_ref)
    copy = pltpu.make_async_copy(list_ref, list_smem, sem)
    copy.start()
    load_operands(hops, shares, shares, where_scr, vec_scr)
    copy.wait()
    product(hops, list_smem, where_scr, vec_scr, image_ref)
    field = own_ref[4:12, :]
    image = own_ref[3:4, :] * field + own_ref[2:3, :] * image_ref[...]
    image_ref[...] = image
    share_ref[...] = image * (own_ref[2:3, :] * (1.0 / 256.0))
    lane = iota((8, LANES), 1)
    dots = jnp.where(
        lane == 0,
        jnp.sum(field * field, axis=1, keepdims=True),
        jnp.where(
            lane == 1,
            jnp.sum(field * image, axis=1, keepdims=True),
            jnp.sum(image * image, axis=1, keepdims=True),
        ),
    )
    dots_ref[...] = jnp.broadcast_to(dots[None], dots_ref.shape)


def second_kernel(hops, list_smem, own_ref, image_ref, *refs):
    n = 2 * hops + 1
    shares, vectors = refs[:n], refs[n : 2 * n]
    twice_ref, where_scr, vec_scr = refs[2 * n :]
    load_operands(hops, shares, vectors, where_scr, vec_scr)
    product(hops, list_smem, where_scr, vec_scr, twice_ref)
    twice_ref[...] = own_ref[3:4, :] * image_ref[...] + own_ref[2:3, :] * twice_ref[...]


def place_kernel(
    own_ref, both_ref, alpha_ref, direction_ref, residual_ref, moved_ref, field_out, residual_out, inv_chunk, inv_lane, data_scr
):
    chunks = own_ref.shape[1] // LANES
    sums = both_ref[0]
    for t in range(1, both_ref.shape[0]):
        sums = sums + both_ref[t]
    alpha_next = sums[:, 0:1] / sums[:, 1:2]
    data_scr[0:8, :] = alpha_ref[:, 0:1] * own_ref[4:12, :] + alpha_next * direction_ref[...]
    data_scr[8:16, :] = residual_ref[...] - alpha_next * moved_ref[...]
    places = [own_ref[12:13, c * LANES : (c + 1) * LANES].astype(i32) - 1 for c in range(chunks)]
    chunk, lane, _ = invert(places, chunks)
    inv_chunk[...] = chunk
    inv_lane[...] = lane
    for d in range(chunks):
        value = pick(
            lambda s: data_scr[:, s * LANES : (s + 1) * LANES],
            chunks,
            inv_chunk[d : d + 1, :],
            inv_lane[d : d + 1, :],
            inv_lane[d : d + 1, :] >= 0,
        )
        field_out[:, d * LANES : (d + 1) * LANES] = value[0:8]
        residual_out[:, d * LANES : (d + 1) * LANES] = value[8:16]


def call(kernel, outs, ins, scratch=(), limit=LIMIT):
    return pl.pallas_call(
        kernel,
        out_shape=[jax.ShapeDtypeStruct(shape, kind) for shape, kind in outs],
        in_specs=ins,
        out_specs=[VMEM] * len(outs),
        scratch_shapes=list(scratch),
        compiler_params=pltpu.CompilerParams(vmem_limit_bytes=limit),
    )


def around(value, hops, tiles):
    got = {0: value}
    for hop in range(1, hops + 1):
        for sign in (1, -1):
            pairs = [(i, (i - sign * hop) % tiles) for i in range(tiles)]
            got[sign * hop] = lax.ppermute(value, "tiles", pairs)
    return [got[hop] for hop in range(-hops, hops + 1)]


def local(obs_position, obs_sd, obs_var, innovations, obs_target, pair_table, pair_count):
    tiles = lax.axis_size("tiles")
    my_tile = lax.axis_index("tiles").astype(i32)
    rows = obs_sd.shape[0]
    chunks = rows // LANES
    hops = pair_table.shape[1] - 1
    held = (2 * hops + 1) * chunks
    capacity = 3 * rows // (2 * tiles)
    width = -(-capacity // LANES) * LANES
    boxes = tiles * width // LANES

    (outbox,) = call(
        functools.partial(outbox_kernel, tiles, width),
        [((tiles, FIELDS, width), f32)],
        [pl.BlockSpec(memory_space=pltpu.HBM)] * 5,
        [
            pltpu.VMEM((FIELDS, rows), f32),
            pltpu.VMEM((2, rows), f32),
            pltpu.VMEM((1, rows), f32),
            pltpu.VMEM((1, rows), f32),
            pltpu.VMEM((8, rows), f32),
            pltpu.VMEM((1, rows), i32),
        ]
        + [pltpu.VMEM((boxes, LANES), i32)] * 3
        + [pltpu.SemaphoreType.DMA((5,))],
        64 * 2**20 - 2**16,
    )(obs_position, obs_sd[None], obs_var[None], innovations, obs_target[None])
    inbox = lax.all_to_all(outbox, "tiles", split_axis=0, concat_axis=0, tiled=True)
    share, own = call(
        sort_kernel,
        [((FIELDS, rows), f32), ((FIELDS, rows), f32)],
        [VMEM, SMEM],
        [pltpu.VMEM((chunks, LANES), i32)] * 2 + [pltpu.VMEM((boxes, BINS, LANES), f32)],
    )(inbox, pair_count)
    shares = around(share, hops, tiles)
    operands = [pltpu.VMEM((held + 1, 8, LANES), f32), pltpu.VMEM((held + 1, 16, LANES), bf16)]
    image, image_share, dots, near = call(
        functools.partial(first_kernel, hops),
        [((8, rows), f32), ((8, rows), f32), ((tiles, 8, LANES), f32), ((chunks, LANES), i32)],
        [SMEM] + [VMEM] * (2 * hops + 2),
        [pltpu.SMEM((chunks, LANES), i32)] + operands + [pltpu.SemaphoreType.DMA],
    )(my_tile[None], own, *shares)
    vectors = around(image_share, hops, tiles)
    (twice,) = call(
        functools.partial(second_kernel, hops),
        [((8, rows), f32)],
        [SMEM] + [VMEM] * (4 * hops + 4),
        operands,
    )(near, own, image, *shares, *vectors)

    sums = jnp.sum(
        lax.all_to_all(dots, "tiles", split_axis=0, concat_axis=0, tiled=True), axis=0
    )
    norm, power, size = sums[:, 0:1], sums[:, 1:2], sums[:, 2:3]
    field = own[4:12]
    alpha = norm / power
    beta = (alpha * alpha * size - norm) / norm
    residual = field - alpha * image
    direction = residual + beta * field
    moved = (1.0 + beta) * image - alpha * twice
    parts = jnp.where(
        jnp.arange(LANES)[None] == 0,
        jnp.sum(residual * residual, axis=1, keepdims=True),
        jnp.sum(direction * moved, axis=1, keepdims=True),
    )
    both = lax.all_to_all(
        jnp.broadcast_to(parts[None], (tiles, 8, LANES)), "tiles", split_axis=0, concat_axis=0, tiled=True
    )
    return tuple(
        call(
            place_kernel,
            [((8, rows), f32)] * 2,
            [VMEM] * 6,
            [pltpu.VMEM((chunks, LANES), i32)] * 2 + [pltpu.VMEM((16, rows), f32)],
        )(own, both, jnp.broadcast_to(alpha, (8, LANES)), direction, residual, moved)
    )


def solution(mesh):
    both = ("groups", "tiles")
    placed = (P(None, both), P(both), P(both), P(None, both), P(both), P(both, None, None), P(both))
    return jax.shard_map(
        local,
        mesh=mesh,
        in_specs=placed,
        out_specs=(P(None, both), P(None, both)),
        check_vma=False,
    )
```

```python
import functools

import jax
import jax.numpy as jnp
from jax import lax
from jax.experimental import pallas as pl
from jax.experimental.pallas import tpu as pltpu
from jax.sharding import PartitionSpec as P

f32, bf16, i32 = jnp.float32, jnp.bfloat16, jnp.int32
LANES = 128
FIELDS = 16
BINS = 128
GROUP = 4
LARGEST = 8
UNIT = 8
RING = 4
CACHED = 25
TRANSPOSED = (((1,), (1,)), ((), ()))
VMEM = pl.BlockSpec(memory_space=pltpu.VMEM)
SMEM = pl.BlockSpec(memory_space=pltpu.SMEM)
HBM = pl.BlockSpec(memory_space=pltpu.HBM)
LIMIT = 40 * 2**20


def iota(shape, axis):
    return lax.broadcasted_iota(i32, shape, axis)


def running_sum_weights():
    shape = (LANES, 2 * LANES)
    row, col = iota(shape, 0), iota(shape, 1)
    return jnp.where((row <= col) | (col >= LANES), 1.0, 0.0).astype(bf16)


def dot(a, b):
    return jnp.dot(a, b, preferred_element_type=f32)


def dot_t(a, b):
    return lax.dot_general(a, b, TRANSPOSED, preferred_element_type=f32)


def invert(places, count):
    chunk_rows, lane_rows, here_rows, low_rows = [], [], [], []
    for chunk, place in enumerate(places):
        high = jnp.right_shift(place, 7)
        here = jnp.where(high == iota((count, LANES), 0), 1.0, 0.0)
        here_rows.append(here.astype(bf16))
        chunk_rows.append((here * float(chunk)).astype(bf16))
        lane_rows.append((here * iota((count, LANES), 1).astype(f32)).astype(bf16))
        low = jnp.bitwise_and(place, LANES - 1)
        low_rows.append(jnp.where(low == iota((LANES, LANES), 0), 1.0, 0.0).astype(bf16))
    left = jnp.concatenate(
        [jnp.concatenate(rows, axis=1) for rows in (chunk_rows, lane_rows, here_rows)], axis=0
    )
    found = dot_t(left, jnp.concatenate(low_rows, axis=1))
    chunk = found[:count].astype(i32)
    lane = found[count : 2 * count].astype(i32)
    return chunk, lane, found[2 * count :] > 0.5


def pick(load, sources, chunk, lane, here):
    total = None
    for source in range(sources):
        value = load(source)
        index = jnp.broadcast_to(lane, value.shape)
        value = jnp.take_along_axis(value, index, axis=1)
        total = value if total is None else jnp.where(chunk == source, value, total)
    return jnp.where(here, total, 0.0)


def outbox_kernel(
    tiles,
    width,
    pos_ref,
    sd_ref,
    var_ref,
    innov_ref,
    target_ref,
    out_ref,
    fields,
    pos_scr,
    sd_scr,
    var_scr,
    innov_scr,
    target_scr,
    inv_chunk,
    inv_lane,
    inv_here,
    sems,
):
    rows = pos_ref.shape[1]
    chunks = rows // LANES
    copies = [
        pltpu.make_async_copy(source, target, sems.at[k])
        for k, (source, target) in enumerate(
            (
                (target_ref, target_scr),
                (pos_ref, pos_scr),
                (sd_ref, sd_scr),
                (var_ref, var_scr),
                (innov_ref, innov_scr),
            )
        )
    ]
    for copy in copies:
        copy.start()
    fields[...] = jnp.zeros_like(fields)
    for copy in copies:
        copy.wait()
    fields[0:2, :] = pos_scr[...]
    fields[2:3, :] = sd_scr[...]
    fields[3:4, :] = var_scr[...]
    target = target_scr[...]
    owner = target // rows
    fields[12:13, :] = (target - owner * rows + 1).astype(f32)
    fields[4:12, :] = innov_scr[...]
    mine = [
        jnp.where(owner[:, c * LANES : (c + 1) * LANES] == iota((tiles, LANES), 0), 1.0, 0.0)
        for c in range(chunks)
    ]
    sums = dot(jnp.concatenate([m.astype(bf16) for m in mine], axis=0), running_sum_weights())
    before = (iota((tiles, LANES), 0) * width - 1).astype(f32)
    places = []
    for c in range(chunks):
        part = sums[c * tiles : (c + 1) * tiles]
        place = jnp.sum(mine[c] * (part[:, :LANES] + before), axis=0, keepdims=True)
        places.append(place.astype(i32))
        before = before + part[:, LANES:]
    count = tiles * width // LANES
    chunk, lane, here = invert(places, count)
    inv_chunk[...] = chunk
    inv_lane[...] = lane
    inv_here[...] = jnp.where(here, 1, 0)
    per_tile = width // LANES
    for d in range(count):
        out_ref[d // per_tile, :, (d % per_tile) * LANES : (d % per_tile + 1) * LANES] = pick(
            lambda s: fields[:, s * LANES : (s + 1) * LANES],
            chunks,
            inv_chunk[d : d + 1, :],
            inv_lane[d : d + 1, :],
            inv_here[d : d + 1, :] > 0,
        )


def sort_kernel(in_ref, count_ref, share_ref, own_ref, inv_chunk, inv_lane, rank_scr):
    tiles, _, width = in_ref.shape
    rows = own_ref.shape[1]
    chunks = rows // LANES
    per_tile = width // LANES
    sources = tiles * per_tile

    def load(s):
        return in_ref[s // per_tile, :, (s % per_tile) * LANES : (s % per_tile + 1) * LANES]

    weights = running_sum_weights()
    before = jnp.full((BINS, LANES), -1.0, f32)
    for s in range(sources):
        data = load(s)
        bins = jnp.clip((data[1:2] * (BINS / 8.0)).astype(i32), 0, BINS - 1)
        bins = jnp.where(data[12:13] > 0.5, bins, -1)
        member = jnp.where(bins == iota((BINS, LANES), 0), 1.0, 0.0)
        part = dot(member.astype(bf16), weights)
        rank_scr[s] = member * (part[:, :LANES] + before)
        before = before + part[:, LANES:]
    totals = before + 1.0
    high = jnp.floor(totals * (1.0 / 64.0))
    low = totals - 64.0 * high
    earlier = jnp.where(iota((BINS, BINS), 1) < iota((BINS, BINS), 0), 1.0, 0.0).astype(bf16)
    base = 64.0 * dot(earlier, high.astype(bf16)) + dot(earlier, low.astype(bf16))
    places = []
    for s in range(sources):
        data = load(s)
        bins = jnp.clip((data[1:2] * (BINS / 8.0)).astype(i32), 0, BINS - 1)
        here = data[12:13] > 0.5
        member = jnp.where(bins == iota((BINS, LANES), 0), base, 0.0)
        place = jnp.sum(member + rank_scr[s], axis=0, keepdims=True).astype(i32)
        places.append(jnp.where(here, place, -1))
    chunk, lane, here = invert(places, chunks)
    inv_chunk[...] = chunk
    inv_lane[...] = lane
    for d in range(chunks):
        own_ref[:, d * LANES : (d + 1) * LANES] = pick(
            load, sources, inv_chunk[d : d + 1, :], inv_lane[d : d + 1, :], inv_lane[d : d + 1, :] >= 0
        )
    share_ref[...] = jnp.zeros_like(share_ref)
    share_ref[0:8, :] = own_ref[4:12, :] * (own_ref[2:3, :] * (1.0 / 256.0))
    share_ref[8:10, :] = own_ref[0:2, :] * 4.0
    stat = jnp.zeros((1, LANES), f32)
    for axis in range(2):
        wide = jnp.concatenate(
            [share_ref[8 + axis : 9 + axis, c * LANES : (c + 1) * LANES] for c in range(chunks)], axis=0
        )
        for which, value in ((0, jnp.min(wide, axis=1, keepdims=True)), (1, jnp.max(wide, axis=1, keepdims=True))):
            lanes = iota((chunks, LANES), 1) - chunks * (2 * axis + which)
            stat = stat + jnp.sum(
                jnp.where(lanes == iota((chunks, LANES), 0), value, 0.0), axis=0, keepdims=True
            )
    stat = jnp.where(iota((1, LANES), 1) == 4 * chunks, count_ref[0].astype(f32), stat)
    share_ref[10:11, 0:LANES] = stat


def make_list(hops, tile_ref, shares, list_ref):
    chunks = list_ref.shape[0]
    my_tile = tile_ref[0]
    own = shares[hops][10:11, 0:LANES]
    lane, sub = iota((chunks, LANES), 1), iota((chunks, LANES), 0)
    x_low, x_high, y_low, y_high = [
        jnp.sum(jnp.where(lane == sub + chunks * q, own, 0.0), axis=1, keepdims=True) for q in range(4)
    ]
    own_count = own[:, 4 * chunks : 4 * chunks + 1]
    need = jnp.zeros((chunks, LANES), f32)
    for nb in range(2 * hops + 1):
        hop = nb - hops
        other = shares[nb][10:11, 0:LANES]
        at = [pltpu.roll(other, (nb * chunks - q * chunks) % LANES, 1) for q in range(4)]
        gap_x = jnp.maximum(jnp.maximum(at[0] - x_high, x_low - at[1]), 0.0)
        gap_y = jnp.maximum(jnp.maximum(at[2] - y_high, y_low - at[3]), 0.0)
        near = gap_x * gap_x + gap_y * gap_y < 16.001
        count = own_count if hop >= 0 else other[:, 4 * chunks : 4 * chunks + 1]
        listed = (count > abs(hop) + 0.5) & (my_tile + hop >= 0)
        inside = (lane >= nb * chunks) & (lane < (nb + 1) * chunks)
        need = need + jnp.where(near & listed & inside, 1.0, 0.0)
    total = dot(need.astype(bf16), running_sum_weights())
    slot = jnp.where(need > 0.5, total[:, :LANES] - 1.0, -1.0)
    numbers = jnp.broadcast_to(iota((8, LANES), 1).astype(f32), (8, LANES)).astype(bf16)
    for r in range(chunks):
        match = jnp.where(slot[r : r + 1] == iota((LANES, LANES), 0).astype(f32), 1.0, 0.0)
        found = dot_t(numbers, match.astype(bf16))[0:1]
        amount = total[r : r + 1, LANES:]
        row = jnp.where(iota((1, LANES), 1).astype(f32) < amount, found, float((2 * hops + 1) * chunks))
        row = jnp.where(iota((1, LANES), 1) == LANES - 1, amount, row)
        list_ref[r : r + 1, :] = row.astype(i32)


def load_where(hops, shares, where_scr):
    chunks = shares[0].shape[1] // LANES
    for nb in range(2 * hops + 1):
        for c in range(chunks):
            where_scr[nb * chunks + c] = shares[nb][8:16, c * LANES : (c + 1) * LANES]
    where_scr[(2 * hops + 1) * chunks] = jnp.zeros((8, LANES), f32)


def load_vectors(hops, vectors, vec_scr):
    chunks = vectors[0].shape[1] // LANES
    for nb in range(2 * hops + 1):
        for c in range(chunks):
            value = vectors[nb][0:8, c * LANES : (c + 1) * LANES]
            high = value.astype(bf16)
            low = (value - high.astype(f32)).astype(bf16)
            vec_scr[nb * chunks + c] = jnp.concatenate([high, low], axis=0)
    vec_scr[(2 * hops + 1) * chunks] = jnp.zeros((16, LANES), bf16)


def block(x_col, y_col, x_row, y_row):
    dx = x_col - x_row
    dy = y_col - y_row
    square = jnp.maximum(dx * dx + dy * dy, 1e-30)
    distance = square * lax.rsqrt(square)
    inside = jnp.maximum(4.0 - distance, 0.0)
    inside = inside * inside
    corr = inside * inside * (distance + 1.0)
    high = corr.astype(bf16)
    return high, (corr - high.astype(f32)).astype(bf16)


def group_blocks(list_smem, where_scr, vec_scr, r, start, columns):
    highs, lows, vecs = [], [], []
    for j in range(GROUP):
        c = list_smem[r, start + j]
        high, low = block(*columns, where_scr[c, 0:1, :], where_scr[c, 1:2, :])
        highs.append(high)
        lows.append(low)
        vecs.append(vec_scr[c])
    return highs, lows, vecs


def multiply(total, highs, lows, vecs):
    vec = jnp.concatenate(vecs, axis=1)
    total = total + dot_t(vec, jnp.concatenate(highs, axis=1))
    return total + dot_t(vec, jnp.concatenate(lows, axis=1))


def groups_of(list_smem, r):
    return (list_smem[r, LANES - 1] + (GROUP - 1)) // GROUP


def own_columns(hops, chunks, where_scr, r):
    column = where_scr[hops * chunks + r].T
    return tuple(jnp.broadcast_to(column[:, k : k + 1], (LANES, LANES)) for k in range(2))


def in_batches(count, batch):
    total = lax.fori_loop(
        0, count // LARGEST, lambda b, t: batch(b * LARGEST, LARGEST, t), jnp.zeros((16, LANES), f32)
    )
    size = LARGEST // 2
    while size:
        first = count // (2 * size) * (2 * size)
        total = lax.cond(
            (count // size) % 2 == 1,
            lambda t, first=first, size=size: batch(first, size, t),
            lambda t: t,
            total,
        )
        size //= 2
    return total


def put_rows(out_ref, r, total):
    out_ref[:, pl.ds(pl.multiple_of(r * LANES, LANES), LANES)] = total[0:8] + total[8:16]


def first_touch(number, size):
    return (number + size - 1) // UNIT != (number + UNIT - 1) // UNIT - 1


def unit_of(stage, unit):
    return stage.at[pl.ds((unit % RING) * UNIT, UNIT)]


def product(hops, list_smem, where_scr, vec_scr, out_ref, cache_ref, stage, sems):
    chunks = out_ref.shape[1] // LANES
    room = cache_ref.shape[0] - 1

    def save(unit):
        return pltpu.make_async_copy(
            unit_of(stage, unit), cache_ref.at[jnp.minimum(unit, room)], sems.at[unit % RING]
        )

    def chunk_rows(r, before):
        columns = own_columns(hops, chunks, where_scr, r)
        count = groups_of(list_smem, r)

        def batch(first, size, total):
            number = before + first
            touched = (number + size - 1) // UNIT
            pl.when(first_touch(number, size) & (touched >= RING))(lambda: save(touched - RING).wait())
            highs, lows, vecs = [], [], []
            for g in range(size):
                high, low, vec = group_blocks(
                    list_smem, where_scr, vec_scr, r, (first + g) * GROUP, columns
                )
                highs += high
                lows += low
                vecs += vec
            for g in range(size):
                slot = (number + g) % (RING * UNIT)
                for j in range(GROUP):
                    stage[slot, j] = highs[g * GROUP + j]
                    stage[slot, GROUP + j] = lows[g * GROUP + j]
            total = multiply(total, highs, lows, vecs)
            full = number // UNIT
            pl.when((number + size) // UNIT > full)(lambda: save(full).start())
            return total

        put_rows(out_ref, r, in_batches(count, batch))
        return before + count

    used = lax.fori_loop(0, chunks, chunk_rows, 0)
    pl.when(used % UNIT != 0)(lambda: save(used // UNIT).start())
    units = (used + UNIT - 1) // UNIT
    for k in range(RING):
        last = units - 1 - (units - 1 - k) % RING
        pl.when(units > k)(lambda last=last: save(last).wait())


def product_again(hops, list_smem, where_scr, vec_scr, out_ref, cache_ref, stage, sems, load):
    chunks = out_ref.shape[1] // LANES
    room = (cache_ref.shape[0] - 1) * UNIT

    def sizes(r, state):
        before, kept = state
        after = before + groups_of(list_smem, r)
        return after, jnp.where(after <= room, after, kept)

    used, kept = lax.fori_loop(0, chunks, sizes, (0, 0))
    units = (kept + UNIT - 1) // UNIT

    def fetch(unit):
        return pltpu.make_async_copy(cache_ref.at[unit], unit_of(stage, unit), sems.at[unit % RING])

    for k in range(RING):
        pl.when(k < units)(lambda k=k: fetch(k).start())
    load(used > kept)

    def chunk_rows(r, before):
        count = groups_of(list_smem, r)

        def kept_batch(first, size, total):
            number = before + first
            pl.when(first_touch(number, size))(lambda: fetch((number + size - 1) // UNIT).wait())
            highs, lows, vecs = [], [], []
            for g in range(size):
                slot = (number + g) % (RING * UNIT)
                for j in range(GROUP):
                    highs.append(stage[slot, j])
                    lows.append(stage[slot, GROUP + j])
                    vecs.append(vec_scr[list_smem[r, (first + g) * GROUP + j]])
            total = multiply(total, highs, lows, vecs)
            full = number // UNIT
            pl.when(((number + size) // UNIT > full) & (full + RING < units))(
                lambda: fetch(full + RING).start()
            )
            return total

        def fresh(g, total):
            columns = own_columns(hops, chunks, where_scr, r)
            return multiply(total, *group_blocks(list_smem, where_scr, vec_scr, r, g * GROUP, columns))

        total = lax.cond(
            before + count <= kept,
            lambda: in_batches(count, kept_batch),
            lambda: lax.fori_loop(0, count, fresh, jnp.zeros((16, LANES), f32)),
        )
        put_rows(out_ref, r, total)
        return before + count

    lax.fori_loop(0, chunks, chunk_rows, 0)


def first_kernel(hops, tile_ref, own_ref, *refs):
    shares = refs[: 2 * hops + 1]
    image_ref, share_ref, dots_ref, list_ref, cache_ref = refs[2 * hops + 1 : 2 * hops + 6]
    list_smem, where_scr, vec_scr, stage, sems, sem = refs[2 * hops + 6 :]
    make_list(hops, tile_ref, shares, list_ref)
    copy = pltpu.make_async_copy(list_ref, list_smem, sem)
    copy.start()
    load_where(hops, shares, where_scr)
    load_vectors(hops, shares, vec_scr)
    copy.wait()
    product(hops, list_smem, where_scr, vec_scr, image_ref, cache_ref, stage, sems)
    field = own_ref[4:12, :]
    image = own_ref[3:4, :] * field + own_ref[2:3, :] * image_ref[...]
    image_ref[...] = image
    share_ref[...] = image * (own_ref[2:3, :] * (1.0 / 256.0))
    lane = iota((8, LANES), 1)
    dots = jnp.where(
        lane == 0,
        jnp.sum(field * field, axis=1, keepdims=True),
        jnp.where(
            lane == 1,
            jnp.sum(field * image, axis=1, keepdims=True),
            jnp.sum(image * image, axis=1, keepdims=True),
        ),
    )
    dots_ref[...] = jnp.broadcast_to(dots[None], dots_ref.shape)


def second_kernel(hops, list_smem, own_ref, image_ref, cache_ref, *refs):
    n = 2 * hops + 1
    shares, vectors = refs[:n], refs[n : 2 * n]
    twice_ref, where_scr, vec_scr, stage, sems = refs[2 * n :]

    def load(needed):
        load_vectors(hops, vectors, vec_scr)
        pl.when(needed)(lambda: load_where(hops, shares, where_scr))

    product_again(hops, list_smem, where_scr, vec_scr, twice_ref, cache_ref, stage, sems, load)
    twice_ref[...] = own_ref[3:4, :] * image_ref[...] + own_ref[2:3, :] * twice_ref[...]


def place_kernel(
    own_ref, both_ref, alpha_ref, direction_ref, residual_ref, moved_ref, field_out, residual_out, inv_chunk, inv_lane, data_scr
):
    chunks = own_ref.shape[1] // LANES
    sums = both_ref[0]
    for t in range(1, both_ref.shape[0]):
        sums = sums + both_ref[t]
    alpha_next = sums[:, 0:1] / sums[:, 1:2]
    data_scr[0:8, :] = alpha_ref[:, 0:1] * own_ref[4:12, :] + alpha_next * direction_ref[...]
    data_scr[8:16, :] = residual_ref[...] - alpha_next * moved_ref[...]
    places = [own_ref[12:13, c * LANES : (c + 1) * LANES].astype(i32) - 1 for c in range(chunks)]
    chunk, lane, _ = invert(places, chunks)
    inv_chunk[...] = chunk
    inv_lane[...] = lane
    for d in range(chunks):
        value = pick(
            lambda s: data_scr[:, s * LANES : (s + 1) * LANES],
            chunks,
            inv_chunk[d : d + 1, :],
            inv_lane[d : d + 1, :],
            inv_lane[d : d + 1, :] >= 0,
        )
        field_out[:, d * LANES : (d + 1) * LANES] = value[0:8]
        residual_out[:, d * LANES : (d + 1) * LANES] = value[8:16]


def call(kernel, outs, ins, scratch=(), limit=LIMIT):
    return pl.pallas_call(
        kernel,
        out_shape=[jax.ShapeDtypeStruct(shape, kind) for shape, kind in outs],
        in_specs=ins,
        out_specs=[VMEM if len(shape) < 3 or kind != bf16 else HBM for shape, kind in outs],
        scratch_shapes=list(scratch),
        compiler_params=pltpu.CompilerParams(vmem_limit_bytes=limit),
    )


def around(value, hops, tiles):
    got = {0: value}
    for hop in range(1, hops + 1):
        for sign in (1, -1):
            pairs = [(i, (i - sign * hop) % tiles) for i in range(tiles)]
            got[sign * hop] = lax.ppermute(value, "tiles", pairs)
    return [got[hop] for hop in range(-hops, hops + 1)]


def local(obs_position, obs_sd, obs_var, innovations, obs_target, pair_table, pair_count):
    tiles = lax.axis_size("tiles")
    my_tile = lax.axis_index("tiles").astype(i32)
    rows = obs_sd.shape[0]
    chunks = rows // LANES
    hops = pair_table.shape[1] - 1
    held = (2 * hops + 1) * chunks
    capacity = 3 * rows // (2 * tiles)
    width = -(-capacity // LANES) * LANES
    boxes = tiles * width // LANES

    (outbox,) = call(
        functools.partial(outbox_kernel, tiles, width),
        [((tiles, FIELDS, width), f32)],
        [HBM] * 5,
        [
            pltpu.VMEM((FIELDS, rows), f32),
            pltpu.VMEM((2, rows), f32),
            pltpu.VMEM((1, rows), f32),
            pltpu.VMEM((1, rows), f32),
            pltpu.VMEM((8, rows), f32),
            pltpu.VMEM((1, rows), i32),
        ]
        + [pltpu.VMEM((boxes, LANES), i32)] * 3
        + [pltpu.SemaphoreType.DMA((5,))],
        64 * 2**20 - 2**16,
    )(obs_position, obs_sd[None], obs_var[None], innovations, obs_target[None])
    inbox = lax.all_to_all(outbox, "tiles", split_axis=0, concat_axis=0, tiled=True)
    share, own = call(
        sort_kernel,
        [((FIELDS, rows), f32), ((FIELDS, rows), f32)],
        [VMEM, SMEM],
        [pltpu.VMEM((chunks, LANES), i32)] * 2 + [pltpu.VMEM((boxes, BINS, LANES), f32)],
    )(inbox, pair_count)
    shares = around(share, hops, tiles)
    operands = [
        pltpu.VMEM((held + 1, 8, LANES), f32),
        pltpu.VMEM((held + 1, 16, LANES), bf16),
        pltpu.VMEM((RING * UNIT, 2 * GROUP, LANES, LANES), bf16),
        pltpu.SemaphoreType.DMA((RING,)),
    ]
    kept = (min(CACHED, held * chunks // (GROUP * UNIT)) + 1, UNIT, 2 * GROUP, LANES, LANES)
    image, image_share, dots, near, cache = call(
        functools.partial(first_kernel, hops),
        [((8, rows), f32), ((8, rows), f32), ((tiles, 8, LANES), f32), ((chunks, LANES), i32), (kept, bf16)],
        [SMEM] + [VMEM] * (2 * hops + 2),
        [pltpu.SMEM((chunks, LANES), i32)] + operands + [pltpu.SemaphoreType.DMA],
    )(my_tile[None], own, *shares)
    vectors = around(image_share, hops, tiles)
    (twice,) = call(
        functools.partial(second_kernel, hops),
        [((8, rows), f32)],
        [SMEM] + [VMEM] * 2 + [HBM] + [VMEM] * (4 * hops + 2),
        operands,
    )(near, own, image, cache, *shares, *vectors)

    sums = jnp.sum(
        lax.all_to_all(dots, "tiles", split_axis=0, concat_axis=0, tiled=True), axis=0
    )
    norm, power, size = sums[:, 0:1], sums[:, 1:2], sums[:, 2:3]
    field = own[4:12]
    alpha = norm / power
    beta = (alpha * alpha * size - norm) / norm
    residual = field - alpha * image
    direction = residual + beta * field
    moved = (1.0 + beta) * image - alpha * twice
    parts = jnp.where(
        jnp.arange(LANES)[None] == 0,
        jnp.sum(residual * residual, axis=1, keepdims=True),
        jnp.sum(direction * moved, axis=1, keepdims=True),
    )
    both = lax.all_to_all(
        jnp.broadcast_to(parts[None], (tiles, 8, LANES)), "tiles", split_axis=0, concat_axis=0, tiled=True
    )
    return tuple(
        call(
            place_kernel,
            [((8, rows), f32)] * 2,
            [VMEM] * 6,
            [pltpu.VMEM((chunks, LANES), i32)] * 2 + [pltpu.VMEM((16, rows), f32)],
        )(own, both, jnp.broadcast_to(alpha, (8, LANES)), direction, residual, moved)
    )


def solution(mesh):
    both = ("groups", "tiles")
    placed = (P(None, both), P(both), P(both), P(None, both), P(both), P(both, None, None), P(both))
    return jax.shard_map(
        local,
        mesh=mesh,
        in_specs=placed,
        out_specs=(P(None, both), P(None, both)),
        check_vma=False,
    )
```

```python
import functools

import jax
import jax.numpy as jnp
from jax import lax
from jax.experimental import pallas as pl
from jax.experimental.pallas import tpu as pltpu
from jax.sharding import PartitionSpec as P

f32, bf16, i32 = jnp.float32, jnp.bfloat16, jnp.int32
LANES = 128
FIELDS = 16
BINS = 128
GROUP = 4
UNIT = 8
RING = 4
CACHED = 25
TRANSPOSED = (((1,), (1,)), ((), ()))
VMEM = pl.BlockSpec(memory_space=pltpu.VMEM)
SMEM = pl.BlockSpec(memory_space=pltpu.SMEM)
HBM = pl.BlockSpec(memory_space=pltpu.HBM)
LIMIT = 40 * 2**20


def iota(shape, axis):
    return lax.broadcasted_iota(i32, shape, axis)


def running_sum_weights():
    shape = (LANES, 2 * LANES)
    row, col = iota(shape, 0), iota(shape, 1)
    return jnp.where((row <= col) | (col >= LANES), 1.0, 0.0).astype(bf16)


def dot(a, b):
    return jnp.dot(a, b, preferred_element_type=f32)


def dot_t(a, b):
    return lax.dot_general(a, b, TRANSPOSED, preferred_element_type=f32)


def invert(places, count):
    chunk_rows, lane_rows, here_rows, low_rows = [], [], [], []
    for chunk, place in enumerate(places):
        high = jnp.right_shift(place, 7)
        here = jnp.where(high == iota((count, LANES), 0), 1.0, 0.0)
        here_rows.append(here.astype(bf16))
        chunk_rows.append((here * float(chunk)).astype(bf16))
        lane_rows.append((here * iota((count, LANES), 1).astype(f32)).astype(bf16))
        low = jnp.bitwise_and(place, LANES - 1)
        low_rows.append(jnp.where(low == iota((LANES, LANES), 0), 1.0, 0.0).astype(bf16))
    left = jnp.concatenate(
        [jnp.concatenate(rows, axis=1) for rows in (chunk_rows, lane_rows, here_rows)], axis=0
    )
    found = dot_t(left, jnp.concatenate(low_rows, axis=1))
    chunk = found[:count].astype(i32)
    lane = found[count : 2 * count].astype(i32)
    return chunk, lane, found[2 * count :] > 0.5


def pick(load, sources, chunk, lane, here):
    total = None
    for source in range(sources):
        value = load(source)
        index = jnp.broadcast_to(lane, value.shape)
        value = jnp.take_along_axis(value, index, axis=1)
        total = value if total is None else jnp.where(chunk == source, value, total)
    return jnp.where(here, total, 0.0)


def outbox_kernel(
    tiles,
    width,
    pos_ref,
    sd_ref,
    var_ref,
    innov_ref,
    target_ref,
    out_ref,
    fields,
    pos_scr,
    sd_scr,
    var_scr,
    innov_scr,
    target_scr,
    inv_chunk,
    inv_lane,
    inv_here,
    sems,
):
    rows = pos_ref.shape[1]
    chunks = rows // LANES
    copies = [
        pltpu.make_async_copy(source, target, sems.at[k])
        for k, (source, target) in enumerate(
            (
                (target_ref, target_scr),
                (pos_ref, pos_scr),
                (sd_ref, sd_scr),
                (var_ref, var_scr),
                (innov_ref, innov_scr),
            )
        )
    ]
    for copy in copies:
        copy.start()
    fields[...] = jnp.zeros_like(fields)
    for copy in copies:
        copy.wait()
    fields[0:2, :] = pos_scr[...]
    fields[2:3, :] = sd_scr[...]
    fields[3:4, :] = var_scr[...]
    target = target_scr[...]
    owner = target // rows
    fields[12:13, :] = (target - owner * rows + 1).astype(f32)
    fields[4:12, :] = innov_scr[...]
    mine = [
        jnp.where(owner[:, c * LANES : (c + 1) * LANES] == iota((tiles, LANES), 0), 1.0, 0.0)
        for c in range(chunks)
    ]
    sums = dot(jnp.concatenate([m.astype(bf16) for m in mine], axis=0), running_sum_weights())
    before = (iota((tiles, LANES), 0) * width - 1).astype(f32)
    places = []
    for c in range(chunks):
        part = sums[c * tiles : (c + 1) * tiles]
        place = jnp.sum(mine[c] * (part[:, :LANES] + before), axis=0, keepdims=True)
        places.append(place.astype(i32))
        before = before + part[:, LANES:]
    count = tiles * width // LANES
    chunk, lane, here = invert(places, count)
    inv_chunk[...] = chunk
    inv_lane[...] = lane
    inv_here[...] = jnp.where(here, 1, 0)
    per_tile = width // LANES
    for d in range(count):
        out_ref[d // per_tile, :, (d % per_tile) * LANES : (d % per_tile + 1) * LANES] = pick(
            lambda s: fields[:, s * LANES : (s + 1) * LANES],
            chunks,
            inv_chunk[d : d + 1, :],
            inv_lane[d : d + 1, :],
            inv_here[d : d + 1, :] > 0,
        )


def sort_kernel(in_ref, count_ref, share_ref, own_ref, inv_chunk, inv_lane, rank_scr):
    tiles, _, width = in_ref.shape
    rows = own_ref.shape[1]
    chunks = rows // LANES
    per_tile = width // LANES
    sources = tiles * per_tile

    def load(s):
        return in_ref[s // per_tile, :, (s % per_tile) * LANES : (s % per_tile + 1) * LANES]

    weights = running_sum_weights()
    before = jnp.full((BINS, LANES), -1.0, f32)
    for s in range(sources):
        data = load(s)
        bins = jnp.clip((data[1:2] * (BINS / 8.0)).astype(i32), 0, BINS - 1)
        bins = jnp.where(data[12:13] > 0.5, bins, -1)
        member = jnp.where(bins == iota((BINS, LANES), 0), 1.0, 0.0)
        part = dot(member.astype(bf16), weights)
        rank_scr[s] = member * (part[:, :LANES] + before)
        before = before + part[:, LANES:]
    totals = before + 1.0
    high = jnp.floor(totals * (1.0 / 64.0))
    low = totals - 64.0 * high
    earlier = jnp.where(iota((BINS, BINS), 1) < iota((BINS, BINS), 0), 1.0, 0.0).astype(bf16)
    base = 64.0 * dot(earlier, high.astype(bf16)) + dot(earlier, low.astype(bf16))
    places = []
    for s in range(sources):
        data = load(s)
        bins = jnp.clip((data[1:2] * (BINS / 8.0)).astype(i32), 0, BINS - 1)
        here = data[12:13] > 0.5
        member = jnp.where(bins == iota((BINS, LANES), 0), base, 0.0)
        place = jnp.sum(member + rank_scr[s], axis=0, keepdims=True).astype(i32)
        places.append(jnp.where(here, place, -1))
    chunk, lane, here = invert(places, chunks)
    inv_chunk[...] = chunk
    inv_lane[...] = lane
    for d in range(chunks):
        own_ref[:, d * LANES : (d + 1) * LANES] = pick(
            load, sources, inv_chunk[d : d + 1, :], inv_lane[d : d + 1, :], inv_lane[d : d + 1, :] >= 0
        )
    share_ref[...] = jnp.zeros_like(share_ref)
    share_ref[0:8, :] = own_ref[4:12, :] * (own_ref[2:3, :] * (1.0 / 256.0))
    share_ref[8:10, :] = own_ref[0:2, :] * 4.0
    stat = jnp.zeros((1, LANES), f32)
    for axis in range(2):
        wide = jnp.concatenate(
            [share_ref[8 + axis : 9 + axis, c * LANES : (c + 1) * LANES] for c in range(chunks)], axis=0
        )
        for which, value in ((0, jnp.min(wide, axis=1, keepdims=True)), (1, jnp.max(wide, axis=1, keepdims=True))):
            lanes = iota((chunks, LANES), 1) - chunks * (2 * axis + which)
            stat = stat + jnp.sum(
                jnp.where(lanes == iota((chunks, LANES), 0), value, 0.0), axis=0, keepdims=True
            )
    stat = jnp.where(iota((1, LANES), 1) == 4 * chunks, count_ref[0].astype(f32), stat)
    share_ref[10:11, 0:LANES] = stat


def make_list(hops, tile_ref, shares, list_ref):
    chunks = list_ref.shape[0]
    my_tile = tile_ref[0]
    own = shares[hops][10:11, 0:LANES]
    lane, sub = iota((chunks, LANES), 1), iota((chunks, LANES), 0)
    x_low, x_high, y_low, y_high = [
        jnp.sum(jnp.where(lane == sub + chunks * q, own, 0.0), axis=1, keepdims=True) for q in range(4)
    ]
    own_count = own[:, 4 * chunks : 4 * chunks + 1]
    need = jnp.zeros((chunks, LANES), f32)
    for nb in range(2 * hops + 1):
        hop = nb - hops
        other = shares[nb][10:11, 0:LANES]
        at = [pltpu.roll(other, (nb * chunks - q * chunks) % LANES, 1) for q in range(4)]
        gap_x = jnp.maximum(jnp.maximum(at[0] - x_high, x_low - at[1]), 0.0)
        gap_y = jnp.maximum(jnp.maximum(at[2] - y_high, y_low - at[3]), 0.0)
        near = gap_x * gap_x + gap_y * gap_y < 16.001
        count = own_count if hop >= 0 else other[:, 4 * chunks : 4 * chunks + 1]
        listed = (count > abs(hop) + 0.5) & (my_tile + hop >= 0)
        inside = (lane >= nb * chunks) & (lane < (nb + 1) * chunks)
        need = need + jnp.where(near & listed & inside, 1.0, 0.0)
    total = dot(need.astype(bf16), running_sum_weights())
    slot = jnp.where(need > 0.5, total[:, :LANES] - 1.0, -1.0)
    numbers = jnp.broadcast_to(iota((8, LANES), 1).astype(f32), (8, LANES)).astype(bf16)
    for r in range(chunks):
        match = jnp.where(slot[r : r + 1] == iota((LANES, LANES), 0).astype(f32), 1.0, 0.0)
        found = dot_t(numbers, match.astype(bf16))[0:1]
        amount = total[r : r + 1, LANES:]
        row = jnp.where(iota((1, LANES), 1).astype(f32) < amount, found, float((2 * hops + 1) * chunks))
        row = jnp.where(iota((1, LANES), 1) == LANES - 1, amount, row)
        list_ref[r : r + 1, :] = row.astype(i32)


def load_where(hops, shares, where_scr):
    chunks = shares[0].shape[1] // LANES
    for nb in range(2 * hops + 1):
        for c in range(chunks):
            where_scr[nb * chunks + c] = shares[nb][8:16, c * LANES : (c + 1) * LANES]
    where_scr[(2 * hops + 1) * chunks] = jnp.zeros((8, LANES), f32)


def load_vectors(hops, vectors, vec_scr):
    chunks = vectors[0].shape[1] // LANES
    for nb in range(2 * hops + 1):
        for c in range(chunks):
            value = vectors[nb][0:8, c * LANES : (c + 1) * LANES]
            high = value.astype(bf16)
            low = (value - high.astype(f32)).astype(bf16)
            vec_scr[nb * chunks + c] = jnp.concatenate([high, low], axis=0)
    vec_scr[(2 * hops + 1) * chunks] = jnp.zeros((16, LANES), bf16)


def block(x_col, y_col, x_row, y_row):
    dx = x_col - x_row
    dy = y_col - y_row
    square = jnp.maximum(dx * dx + dy * dy, 1e-30)
    distance = square * lax.rsqrt(square)
    inside = jnp.maximum(4.0 - distance, 0.0)
    inside = inside * inside
    corr = inside * inside * (distance + 1.0)
    high = corr.astype(bf16)
    return high, (corr - high.astype(f32)).astype(bf16)


def multiply(total, high, low, vec):
    both = jnp.concatenate([high, low], axis=1)
    return total + dot_t(jnp.concatenate([vec, vec], axis=1), both)


def flatten(list_smem, flat, chunks):
    def chunk_rows(r, number):
        def one(g, number):
            flat[number] = r * LANES + g * GROUP
            return number + 1

        return lax.fori_loop(0, (list_smem[r, LANES - 1] + (GROUP - 1)) // GROUP, one, number)

    number = lax.fori_loop(0, chunks, chunk_rows, 0)
    for k in range(UNIT):
        flat[number + k] = LANES - 2 * GROUP
    return (number + UNIT - 1) // UNIT


def own_columns(hops, chunks, where_scr, columns):
    for r in range(chunks):
        column = where_scr[hops * chunks + r].T
        for k in range(2):
            columns[k, r] = jnp.broadcast_to(column[:, k : k + 1], (LANES, LANES))


def ring_slot(stage, unit):
    return stage.at[unit % RING]


def group(list_smem, where_scr, vec_scr, columns, entry, total, keep):
    r, start = entry // LANES, entry % LANES
    x_col, y_col = columns[0, r], columns[1, r]
    for j in range(GROUP):
        c = list_smem[r, start + j]
        high, low = block(x_col, y_col, where_scr[c, 0:1, :], where_scr[c, 1:2, :])
        total = multiply(total, high, low, vec_scr[c])
        keep.append((high, low))
    return total


def add_rows(sums, entry, total):
    r = entry // LANES
    sums[r] = sums[r] + (total[0:8] + total[8:16])


def put_rows(out_ref, sums):
    for r in range(sums.shape[0]):
        out_ref[:, r * LANES : (r + 1) * LANES] = sums[r]


def product(list_smem, flat, where_scr, vec_scr, columns, sums, cache_ref, stage, sems):
    room = cache_ref.shape[0] - 1
    blank = jnp.zeros((16, LANES), f32)
    sums[...] = jnp.zeros_like(sums)
    units = flatten(list_smem, flat, sums.shape[0])

    def save(unit):
        return pltpu.make_async_copy(
            ring_slot(stage, unit), cache_ref.at[jnp.minimum(unit, room)], sems.at[unit % RING]
        )

    def one_unit(unit, _):
        pl.when(unit >= RING)(lambda: save(unit - RING).wait())
        slot = unit % RING
        entries = [flat[unit * UNIT + g] for g in range(UNIT)]
        kept, totals = [], []
        for entry in entries:
            totals.append(group(list_smem, where_scr, vec_scr, columns, entry, blank, kept))
        for k, (high, low) in enumerate(kept):
            stage[slot, 2 * k] = high
            stage[slot, 2 * k + 1] = low
        for entry, total in zip(entries, totals):
            add_rows(sums, entry, total)
        save(unit).start()
        return 0

    lax.fori_loop(0, units, one_unit, 0)
    for k in range(RING):
        last = units - 1 - (units - 1 - k) % RING
        pl.when(units > k)(lambda last=last: save(last).wait())


def product_again(list_smem, flat, where_scr, vec_scr, columns, sums, cache_ref, stage, sems, load):
    room = cache_ref.shape[0] - 1
    blank = jnp.zeros((16, LANES), f32)
    sums[...] = jnp.zeros_like(sums)
    units = flatten(list_smem, flat, sums.shape[0])
    ready = jnp.minimum(units, room)

    def fetch(unit):
        return pltpu.make_async_copy(cache_ref.at[unit], ring_slot(stage, unit), sems.at[unit % RING])

    for k in range(RING):
        pl.when(k < ready)(lambda k=k: fetch(k).start())
    load(units > ready)

    def one_unit(unit, _):
        fetch(unit).wait()
        slot = unit % RING
        entries = [flat[unit * UNIT + g] for g in range(UNIT)]
        totals = []
        for g, entry in enumerate(entries):
            r, start = entry // LANES, entry % LANES
            total = blank
            for j in range(GROUP):
                k = g * GROUP + j
                vec = vec_scr[list_smem[r, start + j]]
                total = multiply(total, stage[slot, 2 * k], stage[slot, 2 * k + 1], vec)
            totals.append(total)
        for entry, total in zip(entries, totals):
            add_rows(sums, entry, total)
        pl.when(unit + RING < ready)(lambda: fetch(unit + RING).start())
        return 0

    lax.fori_loop(0, ready, one_unit, 0)

    def fresh(number, _):
        entry = flat[number]
        add_rows(sums, entry, group(list_smem, where_scr, vec_scr, columns, entry, blank, []))
        return 0

    lax.fori_loop(ready * UNIT, units * UNIT, fresh, 0)


def first_kernel(hops, tile_ref, own_ref, *refs):
    shares = refs[: 2 * hops + 1]
    image_ref, share_ref, dots_ref, list_ref, cache_ref = refs[2 * hops + 1 : 2 * hops + 6]
    list_smem, flat, where_scr, vec_scr, columns, sums, stage, sems, sem = refs[2 * hops + 6 :]
    make_list(hops, tile_ref, shares, list_ref)
    copy = pltpu.make_async_copy(list_ref, list_smem, sem)
    copy.start()
    load_where(hops, shares, where_scr)
    load_vectors(hops, shares, vec_scr)
    own_columns(hops, own_ref.shape[1] // LANES, where_scr, columns)
    copy.wait()
    product(list_smem, flat, where_scr, vec_scr, columns, sums, cache_ref, stage, sems)
    put_rows(image_ref, sums)
    field = own_ref[4:12, :]
    image = own_ref[3:4, :] * field + own_ref[2:3, :] * image_ref[...]
    image_ref[...] = image
    share_ref[...] = image * (own_ref[2:3, :] * (1.0 / 256.0))
    lane = iota((8, LANES), 1)
    dots = jnp.where(
        lane == 0,
        jnp.sum(field * field, axis=1, keepdims=True),
        jnp.where(
            lane == 1,
            jnp.sum(field * image, axis=1, keepdims=True),
            jnp.sum(image * image, axis=1, keepdims=True),
        ),
    )
    dots_ref[...] = jnp.broadcast_to(dots[None], dots_ref.shape)


def second_kernel(hops, list_smem, own_ref, image_ref, cache_ref, *refs):
    n = 2 * hops + 1
    shares, vectors = refs[:n], refs[n : 2 * n]
    twice_ref, flat, where_scr, vec_scr, columns, sums, stage, sems = refs[2 * n :]

    def load(needed):
        load_vectors(hops, vectors, vec_scr)


        @pl.when(needed)
        def _():
            load_where(hops, shares, where_scr)
            own_columns(hops, own_ref.shape[1] // LANES, where_scr, columns)

    product_again(list_smem, flat, where_scr, vec_scr, columns, sums, cache_ref, stage, sems, load)
    put_rows(twice_ref, sums)
    twice_ref[...] = own_ref[3:4, :] * image_ref[...] + own_ref[2:3, :] * twice_ref[...]


def place_kernel(
    own_ref, both_ref, alpha_ref, direction_ref, residual_ref, moved_ref, field_out, residual_out, inv_chunk, inv_lane, data_scr
):
    chunks = own_ref.shape[1] // LANES
    sums = both_ref[0]
    for t in range(1, both_ref.shape[0]):
        sums = sums + both_ref[t]
    alpha_next = sums[:, 0:1] / sums[:, 1:2]
    data_scr[0:8, :] = alpha_ref[:, 0:1] * own_ref[4:12, :] + alpha_next * direction_ref[...]
    data_scr[8:16, :] = residual_ref[...] - alpha_next * moved_ref[...]
    places = [own_ref[12:13, c * LANES : (c + 1) * LANES].astype(i32) - 1 for c in range(chunks)]
    chunk, lane, _ = invert(places, chunks)
    inv_chunk[...] = chunk
    inv_lane[...] = lane
    for d in range(chunks):
        value = pick(
            lambda s: data_scr[:, s * LANES : (s + 1) * LANES],
            chunks,
            inv_chunk[d : d + 1, :],
            inv_lane[d : d + 1, :],
            inv_lane[d : d + 1, :] >= 0,
        )
        field_out[:, d * LANES : (d + 1) * LANES] = value[0:8]
        residual_out[:, d * LANES : (d + 1) * LANES] = value[8:16]


def call(kernel, outs, ins, scratch=(), limit=LIMIT):
    return pl.pallas_call(
        kernel,
        out_shape=[jax.ShapeDtypeStruct(shape, kind) for shape, kind in outs],
        in_specs=ins,
        out_specs=[VMEM if len(shape) < 3 or kind != bf16 else HBM for shape, kind in outs],
        scratch_shapes=list(scratch),
        compiler_params=pltpu.CompilerParams(vmem_limit_bytes=limit),
    )


def around(value, hops, tiles):
    got = {0: value}
    for hop in range(1, hops + 1):
        for sign in (1, -1):
            pairs = [(i, (i - sign * hop) % tiles) for i in range(tiles)]
            got[sign * hop] = lax.ppermute(value, "tiles", pairs)
    return [got[hop] for hop in range(-hops, hops + 1)]


def local(obs_position, obs_sd, obs_var, innovations, obs_target, pair_table, pair_count):
    tiles = lax.axis_size("tiles")
    my_tile = lax.axis_index("tiles").astype(i32)
    rows = obs_sd.shape[0]
    chunks = rows // LANES
    hops = pair_table.shape[1] - 1
    held = (2 * hops + 1) * chunks
    capacity = 3 * rows // (2 * tiles)
    width = -(-capacity // LANES) * LANES
    boxes = tiles * width // LANES

    (outbox,) = call(
        functools.partial(outbox_kernel, tiles, width),
        [((tiles, FIELDS, width), f32)],
        [HBM] * 5,
        [
            pltpu.VMEM((FIELDS, rows), f32),
            pltpu.VMEM((2, rows), f32),
            pltpu.VMEM((1, rows), f32),
            pltpu.VMEM((1, rows), f32),
            pltpu.VMEM((8, rows), f32),
            pltpu.VMEM((1, rows), i32),
        ]
        + [pltpu.VMEM((boxes, LANES), i32)] * 3
        + [pltpu.SemaphoreType.DMA((5,))],
        64 * 2**20 - 2**16,
    )(obs_position, obs_sd[None], obs_var[None], innovations, obs_target[None])
    inbox = lax.all_to_all(outbox, "tiles", split_axis=0, concat_axis=0, tiled=True)
    share, own = call(
        sort_kernel,
        [((FIELDS, rows), f32), ((FIELDS, rows), f32)],
        [VMEM, SMEM],
        [pltpu.VMEM((chunks, LANES), i32)] * 2 + [pltpu.VMEM((boxes, BINS, LANES), f32)],
    )(inbox, pair_count)
    shares = around(share, hops, tiles)
    operands = [
        pltpu.SMEM((held * chunks // GROUP + UNIT,), i32),
        pltpu.VMEM((held + 1, 8, LANES), f32),
        pltpu.VMEM((held + 1, 16, LANES), bf16),
        pltpu.VMEM((2, chunks, LANES, LANES), f32),
        pltpu.VMEM((chunks, 8, LANES), f32),
        pltpu.VMEM((RING, UNIT * 2 * GROUP, LANES, LANES), bf16),
        pltpu.SemaphoreType.DMA((RING,)),
    ]
    kept = (min(CACHED, held * chunks // (GROUP * UNIT)) + 1, UNIT * 2 * GROUP, LANES, LANES)
    image, image_share, dots, near, cache = call(
        functools.partial(first_kernel, hops),
        [((8, rows), f32), ((8, rows), f32), ((tiles, 8, LANES), f32), ((chunks, LANES), i32), (kept, bf16)],
        [SMEM] + [VMEM] * (2 * hops + 2),
        [pltpu.SMEM((chunks, LANES), i32)] + operands + [pltpu.SemaphoreType.DMA],
    )(my_tile[None], own, *shares)
    vectors = around(image_share, hops, tiles)
    (twice,) = call(
        functools.partial(second_kernel, hops),
        [((8, rows), f32)],
        [SMEM] + [VMEM] * 2 + [HBM] + [VMEM] * (4 * hops + 2),
        operands,
    )(near, own, image, cache, *shares, *vectors)

    sums = jnp.sum(
        lax.all_to_all(dots, "tiles", split_axis=0, concat_axis=0, tiled=True), axis=0
    )
    norm, power, size = sums[:, 0:1], sums[:, 1:2], sums[:, 2:3]
    field = own[4:12]
    alpha = norm / power
    beta = (alpha * alpha * size - norm) / norm
    residual = field - alpha * image
    direction = residual + beta * field
    moved = (1.0 + beta) * image - alpha * twice
    parts = jnp.where(
        jnp.arange(LANES)[None] == 0,
        jnp.sum(residual * residual, axis=1, keepdims=True),
        jnp.sum(direction * moved, axis=1, keepdims=True),
    )
    both = lax.all_to_all(
        jnp.broadcast_to(parts[None], (tiles, 8, LANES)), "tiles", split_axis=0, concat_axis=0, tiled=True
    )
    return tuple(
        call(
            place_kernel,
            [((8, rows), f32)] * 2,
            [VMEM] * 6,
            [pltpu.VMEM((chunks, LANES), i32)] * 2 + [pltpu.VMEM((16, rows), f32)],
        )(own, both, jnp.broadcast_to(alpha, (8, LANES)), direction, residual, moved)
    )


def solution(mesh):
    both = ("groups", "tiles")
    placed = (P(None, both), P(both), P(both), P(None, both), P(both), P(both, None, None), P(both))
    return jax.shard_map(
        local,
        mesh=mesh,
        in_specs=placed,
        out_specs=(P(None, both), P(None, both)),
        check_vma=False,
    )
```

```python
import functools

import jax
import jax.numpy as jnp
from jax import lax
from jax.experimental import pallas as pl
from jax.experimental.pallas import tpu as pltpu
from jax.sharding import PartitionSpec as P

f32, bf16, i32 = jnp.float32, jnp.bfloat16, jnp.int32
LANES = 128
FIELDS = 16
BINS = 128
GROUP = 4
UNIT = 8
RING = 4
INNER = 8
OUTER = 18
TRANSPOSED = (((1,), (1,)), ((), ()))
VMEM = pl.BlockSpec(memory_space=pltpu.VMEM)
SMEM = pl.BlockSpec(memory_space=pltpu.SMEM)
HBM = pl.BlockSpec(memory_space=pltpu.HBM)
LIMIT = 40 * 2**20


def iota(shape, axis):
    return lax.broadcasted_iota(i32, shape, axis)


def running_sum_weights():
    shape = (LANES, 2 * LANES)
    row, col = iota(shape, 0), iota(shape, 1)
    return jnp.where((row <= col) | (col >= LANES), 1.0, 0.0).astype(bf16)


def dot(a, b):
    return jnp.dot(a, b, preferred_element_type=f32)


def dot_t(a, b):
    return lax.dot_general(a, b, TRANSPOSED, preferred_element_type=f32)


def invert(places, count):
    chunk_rows, lane_rows, here_rows, low_rows = [], [], [], []
    for chunk, place in enumerate(places):
        high = jnp.right_shift(place, 7)
        here = jnp.where(high == iota((count, LANES), 0), 1.0, 0.0)
        here_rows.append(here.astype(bf16))
        chunk_rows.append((here * float(chunk)).astype(bf16))
        lane_rows.append((here * iota((count, LANES), 1).astype(f32)).astype(bf16))
        low = jnp.bitwise_and(place, LANES - 1)
        low_rows.append(jnp.where(low == iota((LANES, LANES), 0), 1.0, 0.0).astype(bf16))
    left = jnp.concatenate(
        [jnp.concatenate(rows, axis=1) for rows in (chunk_rows, lane_rows, here_rows)], axis=0
    )
    found = dot_t(left, jnp.concatenate(low_rows, axis=1))
    chunk = found[:count].astype(i32)
    lane = found[count : 2 * count].astype(i32)
    return chunk, lane, found[2 * count :] > 0.5


def pick(load, sources, chunk, lane, here):
    total = None
    for source in range(sources):
        value = load(source)
        index = jnp.broadcast_to(lane, value.shape)
        value = jnp.take_along_axis(value, index, axis=1)
        total = value if total is None else jnp.where(chunk == source, value, total)
    return jnp.where(here, total, 0.0)


def outbox_kernel(
    tiles,
    width,
    pos_ref,
    sd_ref,
    var_ref,
    innov_ref,
    target_ref,
    out_ref,
    fields,
    pos_scr,
    sd_scr,
    var_scr,
    innov_scr,
    target_scr,
    inv_chunk,
    inv_lane,
    inv_here,
    sems,
):
    rows = pos_ref.shape[1]
    chunks = rows // LANES
    copies = [
        pltpu.make_async_copy(source, target, sems.at[k])
        for k, (source, target) in enumerate(
            (
                (target_ref, target_scr),
                (pos_ref, pos_scr),
                (sd_ref, sd_scr),
                (var_ref, var_scr),
                (innov_ref, innov_scr),
            )
        )
    ]
    for copy in copies:
        copy.start()
    fields[...] = jnp.zeros_like(fields)
    for copy in copies:
        copy.wait()
    fields[0:2, :] = pos_scr[...]
    fields[2:3, :] = sd_scr[...]
    fields[3:4, :] = var_scr[...]
    target = target_scr[...]
    owner = target // rows
    fields[12:13, :] = (target - owner * rows + 1).astype(f32)
    fields[4:12, :] = innov_scr[...]
    mine = [
        jnp.where(owner[:, c * LANES : (c + 1) * LANES] == iota((tiles, LANES), 0), 1.0, 0.0)
        for c in range(chunks)
    ]
    sums = dot(jnp.concatenate([m.astype(bf16) for m in mine], axis=0), running_sum_weights())
    before = (iota((tiles, LANES), 0) * width - 1).astype(f32)
    places = []
    for c in range(chunks):
        part = sums[c * tiles : (c + 1) * tiles]
        place = jnp.sum(mine[c] * (part[:, :LANES] + before), axis=0, keepdims=True)
        places.append(place.astype(i32))
        before = before + part[:, LANES:]
    count = tiles * width // LANES
    chunk, lane, here = invert(places, count)
    inv_chunk[...] = chunk
    inv_lane[...] = lane
    inv_here[...] = jnp.where(here, 1, 0)
    per_tile = width // LANES
    for d in range(count):
        out_ref[d // per_tile, :, (d % per_tile) * LANES : (d % per_tile + 1) * LANES] = pick(
            lambda s: fields[:, s * LANES : (s + 1) * LANES],
            chunks,
            inv_chunk[d : d + 1, :],
            inv_lane[d : d + 1, :],
            inv_here[d : d + 1, :] > 0,
        )


def sort_kernel(in_ref, count_ref, share_ref, own_ref, inv_chunk, inv_lane, rank_scr):
    tiles, _, width = in_ref.shape
    rows = own_ref.shape[1]
    chunks = rows // LANES
    per_tile = width // LANES
    sources = tiles * per_tile

    def load(s):
        return in_ref[s // per_tile, :, (s % per_tile) * LANES : (s % per_tile + 1) * LANES]

    weights = running_sum_weights()
    before = jnp.full((BINS, LANES), -1.0, f32)
    for s in range(sources):
        data = load(s)
        bins = jnp.clip((data[1:2] * (BINS / 8.0)).astype(i32), 0, BINS - 1)
        bins = jnp.where(data[12:13] > 0.5, bins, -1)
        member = jnp.where(bins == iota((BINS, LANES), 0), 1.0, 0.0)
        part = dot(member.astype(bf16), weights)
        rank_scr[s] = member * (part[:, :LANES] + before)
        before = before + part[:, LANES:]
    totals = before + 1.0
    high = jnp.floor(totals * (1.0 / 64.0))
    low = totals - 64.0 * high
    earlier = jnp.where(iota((BINS, BINS), 1) < iota((BINS, BINS), 0), 1.0, 0.0).astype(bf16)
    base = 64.0 * dot(earlier, high.astype(bf16)) + dot(earlier, low.astype(bf16))
    places = []
    for s in range(sources):
        data = load(s)
        bins = jnp.clip((data[1:2] * (BINS / 8.0)).astype(i32), 0, BINS - 1)
        here = data[12:13] > 0.5
        member = jnp.where(bins == iota((BINS, LANES), 0), base, 0.0)
        place = jnp.sum(member + rank_scr[s], axis=0, keepdims=True).astype(i32)
        places.append(jnp.where(here, place, -1))
    chunk, lane, here = invert(places, chunks)
    inv_chunk[...] = chunk
    inv_lane[...] = lane
    for d in range(chunks):
        own_ref[:, d * LANES : (d + 1) * LANES] = pick(
            load, sources, inv_chunk[d : d + 1, :], inv_lane[d : d + 1, :], inv_lane[d : d + 1, :] >= 0
        )
    share_ref[...] = jnp.zeros_like(share_ref)
    share_ref[0:8, :] = own_ref[4:12, :] * (own_ref[2:3, :] * (1.0 / 256.0))
    share_ref[8:10, :] = own_ref[0:2, :] * 4.0
    stat = jnp.zeros((1, LANES), f32)
    for axis in range(2):
        wide = jnp.concatenate(
            [share_ref[8 + axis : 9 + axis, c * LANES : (c + 1) * LANES] for c in range(chunks)], axis=0
        )
        for which, value in ((0, jnp.min(wide, axis=1, keepdims=True)), (1, jnp.max(wide, axis=1, keepdims=True))):
            lanes = iota((chunks, LANES), 1) - chunks * (2 * axis + which)
            stat = stat + jnp.sum(
                jnp.where(lanes == iota((chunks, LANES), 0), value, 0.0), axis=0, keepdims=True
            )
    stat = jnp.where(iota((1, LANES), 1) == 4 * chunks, count_ref[0].astype(f32), stat)
    share_ref[10:11, 0:LANES] = stat


def make_list(hops, tile_ref, own_share, shares, list_ref):
    chunks = list_ref.shape[0]
    my_tile = tile_ref[0]
    own = own_share[10:11, 0:LANES]
    lane, sub = iota((chunks, LANES), 1), iota((chunks, LANES), 0)
    x_low, x_high, y_low, y_high = [
        jnp.sum(jnp.where(lane == sub + chunks * q, own, 0.0), axis=1, keepdims=True) for q in range(4)
    ]
    own_count = own[:, 4 * chunks : 4 * chunks + 1]
    need = jnp.zeros((chunks, LANES), f32)
    for nb, hop in enumerate(hops):
        other = shares[nb][10:11, 0:LANES]
        at = [pltpu.roll(other, (nb * chunks - q * chunks) % LANES, 1) for q in range(4)]
        gap_x = jnp.maximum(jnp.maximum(at[0] - x_high, x_low - at[1]), 0.0)
        gap_y = jnp.maximum(jnp.maximum(at[2] - y_high, y_low - at[3]), 0.0)
        near = gap_x * gap_x + gap_y * gap_y < 16.001
        count = own_count if hop >= 0 else other[:, 4 * chunks : 4 * chunks + 1]
        listed = (count > abs(hop) + 0.5) & (my_tile + hop >= 0)
        inside = (lane >= nb * chunks) & (lane < (nb + 1) * chunks)
        need = need + jnp.where(near & listed & inside, 1.0, 0.0)
    total = dot(need.astype(bf16), running_sum_weights())
    slot = jnp.where(need > 0.5, total[:, :LANES] - 1.0, -1.0)
    numbers = jnp.broadcast_to(iota((8, LANES), 1).astype(f32), (8, LANES)).astype(bf16)
    for r in range(chunks):
        match = jnp.where(slot[r : r + 1] == iota((LANES, LANES), 0).astype(f32), 1.0, 0.0)
        found = dot_t(numbers, match.astype(bf16))[0:1]
        amount = total[r : r + 1, LANES:]
        row = jnp.where(iota((1, LANES), 1).astype(f32) < amount, found, float(len(hops) * chunks))
        row = jnp.where(iota((1, LANES), 1) == LANES - 1, amount, row)
        list_ref[r : r + 1, :] = row.astype(i32)


def load_where(shares, where_scr):
    chunks = shares[0].shape[1] // LANES
    for nb, share in enumerate(shares):
        for c in range(chunks):
            where_scr[nb * chunks + c] = share[8:16, c * LANES : (c + 1) * LANES]
    where_scr[len(shares) * chunks] = jnp.zeros((8, LANES), f32)


def load_vectors(vectors, vec_scr):
    chunks = vectors[0].shape[1] // LANES
    for nb, vector in enumerate(vectors):
        for c in range(chunks):
            value = vector[0:8, c * LANES : (c + 1) * LANES]
            high = value.astype(bf16)
            low = (value - high.astype(f32)).astype(bf16)
            vec_scr[nb * chunks + c] = jnp.concatenate([high, low], axis=0)
    vec_scr[len(vectors) * chunks] = jnp.zeros((16, LANES), bf16)


def block(x_col, y_col, x_row, y_row):
    dx = x_col - x_row
    dy = y_col - y_row
    square = jnp.maximum(dx * dx + dy * dy, 1e-30)
    distance = square * lax.rsqrt(square)
    inside = jnp.maximum(4.0 - distance, 0.0)
    inside = inside * inside
    corr = inside * inside * (distance + 1.0)
    high = corr.astype(bf16)
    return high, (corr - high.astype(f32)).astype(bf16)


def multiply(total, high, low, vec):
    both = jnp.concatenate([high, low], axis=1)
    return total + dot_t(jnp.concatenate([vec, vec], axis=1), both)


def flatten(list_smem, flat, chunks):
    def chunk_rows(r, number):
        def one(g, number):
            flat[number] = r * LANES + g * GROUP
            return number + 1

        return lax.fori_loop(0, (list_smem[r, LANES - 1] + (GROUP - 1)) // GROUP, one, number)

    number = lax.fori_loop(0, chunks, chunk_rows, 0)
    for k in range(UNIT):
        flat[number + k] = LANES - 2 * GROUP
    return (number + UNIT - 1) // UNIT


def own_columns(own_share, columns):
    for r in range(columns.shape[1]):
        column = own_share[8:16, r * LANES : (r + 1) * LANES].T
        for k in range(2):
            columns[k, r] = jnp.broadcast_to(column[:, k : k + 1], (LANES, LANES))


def ring_slot(stage, unit):
    return stage.at[unit % RING]


def group(list_smem, where_scr, vec_scr, columns, entry, total, keep):
    r, start = entry // LANES, entry % LANES
    x_col, y_col = columns[0, r], columns[1, r]
    for j in range(GROUP):
        c = list_smem[r, start + j]
        high, low = block(x_col, y_col, where_scr[c, 0:1, :], where_scr[c, 1:2, :])
        total = multiply(total, high, low, vec_scr[c])
        keep.append((high, low))
    return total


def add_rows(sums, entry, total):
    r = entry // LANES
    sums[r] = sums[r] + (total[0:8] + total[8:16])


def put_rows(out_ref, sums):
    for r in range(sums.shape[0]):
        out_ref[:, r * LANES : (r + 1) * LANES] = sums[r]


def product(list_smem, flat, where_scr, vec_scr, columns, sums, cache_ref, stage, sems):
    room = cache_ref.shape[0] - 1
    blank = jnp.zeros((16, LANES), f32)
    sums[...] = jnp.zeros_like(sums)
    units = flatten(list_smem, flat, sums.shape[0])

    def save(unit):
        return pltpu.make_async_copy(
            ring_slot(stage, unit), cache_ref.at[jnp.minimum(unit, room)], sems.at[unit % RING]
        )

    def one_unit(unit, _):
        pl.when(unit >= RING)(lambda: save(unit - RING).wait())
        slot = unit % RING
        entries = [flat[unit * UNIT + g] for g in range(UNIT)]
        kept, totals = [], []
        for entry in entries:
            totals.append(group(list_smem, where_scr, vec_scr, columns, entry, blank, kept))
        for k, (high, low) in enumerate(kept):
            stage[slot, 2 * k] = high
            stage[slot, 2 * k + 1] = low
        for entry, total in zip(entries, totals):
            add_rows(sums, entry, total)
        save(unit).start()
        return 0

    lax.fori_loop(0, units, one_unit, 0)
    for k in range(RING):
        last = units - 1 - (units - 1 - k) % RING
        pl.when(units > k)(lambda last=last: save(last).wait())


def product_again(list_smem, flat, where_scr, vec_scr, columns, sums, cache_ref, stage, sems, load):
    room = cache_ref.shape[0] - 1
    blank = jnp.zeros((16, LANES), f32)
    sums[...] = jnp.zeros_like(sums)
    units = flatten(list_smem, flat, sums.shape[0])
    ready = jnp.minimum(units, room)

    def fetch(unit):
        return pltpu.make_async_copy(cache_ref.at[unit], ring_slot(stage, unit), sems.at[unit % RING])

    for k in range(RING):
        pl.when(k < ready)(lambda k=k: fetch(k).start())
    load(units > ready)

    def one_unit(unit, _):
        fetch(unit).wait()
        slot = unit % RING
        entries = [flat[unit * UNIT + g] for g in range(UNIT)]
        totals = []
        for g, entry in enumerate(entries):
            r, start = entry // LANES, entry % LANES
            total = blank
            for j in range(GROUP):
                k = g * GROUP + j
                vec = vec_scr[list_smem[r, start + j]]
                total = multiply(total, stage[slot, 2 * k], stage[slot, 2 * k + 1], vec)
            totals.append(total)
        for entry, total in zip(entries, totals):
            add_rows(sums, entry, total)
        pl.when(unit + RING < ready)(lambda: fetch(unit + RING).start())
        return 0

    lax.fori_loop(0, ready, one_unit, 0)

    def fresh(number, _):
        entry = flat[number]
        add_rows(sums, entry, group(list_smem, where_scr, vec_scr, columns, entry, blank, []))
        return 0

    lax.fori_loop(ready * UNIT, units * UNIT, fresh, 0)


def first_sums(hops, tile_ref, own_share, shares, list_ref, cache_ref, scratch):
    list_smem, sem, flat, where_scr, vec_scr, columns, sums, stage, sems = scratch
    make_list(hops, tile_ref, own_share, shares, list_ref)
    copy = pltpu.make_async_copy(list_ref, list_smem, sem)
    copy.start()
    load_where(shares, where_scr)
    load_vectors(shares, vec_scr)
    own_columns(own_share, columns)
    copy.wait()
    product(list_smem, flat, where_scr, vec_scr, columns, sums, cache_ref, stage, sems)
    return sums


def second_sums(list_smem, own_share, shares, vectors, cache_ref, scratch):
    flat, where_scr, vec_scr, columns, sums, stage, sems = scratch

    def load(needed):
        load_vectors(vectors, vec_scr)

        @pl.when(needed)
        def _():
            load_where(shares, where_scr)
            own_columns(own_share, columns)

    product_again(list_smem, flat, where_scr, vec_scr, columns, sums, cache_ref, stage, sems, load)
    return sums


def first_inner_kernel(tile_ref, own_share, out_ref, list_ref, cache_ref, *scratch):
    put_rows(out_ref, first_sums([0], tile_ref, own_share, [own_share], list_ref, cache_ref, scratch))


def first_outer_kernel(hops, tile_ref, own_ref, inner_ref, own_share, *refs):
    n = len(hops)
    shares = refs[:n]
    image_ref, share_ref, list_ref, cache_ref = refs[n : n + 4]
    put_rows(image_ref, first_sums(hops, tile_ref, own_share, shares, list_ref, cache_ref, refs[n + 4 :]))
    field = own_ref[4:12, :]
    image = own_ref[3:4, :] * field + own_ref[2:3, :] * (inner_ref[...] + image_ref[...])
    image_ref[...] = image
    share_ref[...] = image * (own_ref[2:3, :] * (1.0 / 256.0))


def second_inner_kernel(list_smem, own_share, vector, cache_ref, out_ref, *scratch):
    put_rows(out_ref, second_sums(list_smem, own_share, [own_share], [vector], cache_ref, scratch))


def two_sum(a, b):
    total = a + b
    back = total - a
    return total, (a - (total - back)) + (b - back)


def halves(a):
    scaled = a * 4097.0
    high = scaled - (scaled - a)
    return high, a - high


def two_product(a, b):
    total = a * b
    (a_high, a_low), (b_high, b_low) = halves(a), halves(b)
    error = ((a_high * b_high - total) + a_high * b_low + a_low * b_high) + a_low * b_low
    return total, error


def pair_sum(a, b):
    total, rest = two_sum(a[0], b[0])
    rest = rest + (a[1] + b[1])
    high = total + rest
    return high, rest - (high - total)


def pair_product(a, b):
    total, rest = two_product(a[0], b[0])
    rest = rest + (a[0] * b[1] + a[1] * b[0])
    high = total + rest
    return high, rest - (high - total)


def lane_sums(left, right):
    total = (jnp.zeros((8, LANES), f32), jnp.zeros((8, LANES), f32))
    for c in range(left.shape[1] // LANES):
        lanes = slice(c * LANES, (c + 1) * LANES)
        value, error = two_sum(total[0], left[:, lanes] * right[:, lanes])
        total = (value, total[1] + error)
    shift = LANES // 2
    while shift:
        total = pair_sum(total, tuple(pltpu.roll(part, shift, 1) for part in total))
        shift //= 2
    return total


def second_outer_kernel(n, list_smem, own_ref, image_ref, inner_ref, cache_ref, own_share, *refs):
    shares, vectors, twice_ref, dots_ref = refs[:n], refs[n : 2 * n], refs[2 * n], refs[2 * n + 1]
    put_rows(twice_ref, second_sums(list_smem, own_share, shares, vectors, cache_ref, refs[2 * n + 2 :]))
    image = image_ref[...]
    twice = own_ref[3:4, :] * image + own_ref[2:3, :] * (inner_ref[...] + twice_ref[...])
    twice_ref[...] = twice
    field = own_ref[4:12, :]
    lane = iota((8, LANES), 1)
    dots = jnp.zeros((8, LANES), f32)
    pairs = ((field, field), (field, image), (image, image), (field, twice), (image, twice))
    for k, (left, right) in enumerate(pairs):
        value, rest = lane_sums(left, right)
        dots = jnp.where(lane == 2 * k, value, jnp.where(lane == 2 * k + 1, rest, dots))
    dots_ref[...] = jnp.broadcast_to(dots[None], dots_ref.shape)


def place_kernel(own_ref, image_ref, twice_ref, dots_ref, field_out, residual_out, inv_chunk, inv_lane, data_scr):
    chunks = own_ref.shape[1] // LANES

    def held(t):
        part = dots_ref[t]
        return part, pltpu.roll(part, LANES - 1, 1)

    sums = held(0)
    for t in range(1, dots_ref.shape[0]):
        sums = pair_sum(sums, held(t))
    pp, pq, qq, pz, qz = [tuple(part[:, 2 * k : 2 * k + 1] for part in sums) for k in range(5)]
    alpha = pp[0] / pq[0]
    zero = jnp.zeros_like(alpha)
    first = (alpha, zero)
    minus = (-alpha, zero)
    square = pair_product(first, first)
    norm = pair_sum(pair_sum(pp, pair_product((-2.0 * alpha, zero), pq)), pair_product(square, qq))
    beta = norm[0] / pp[0]
    grown = two_sum(jnp.ones_like(beta), beta)
    power = pair_sum(
        pair_product(grown, pair_sum(pair_product(grown, pq), pair_product(minus, pair_sum(qq, pz)))),
        pair_product(square, qz),
    )
    alpha_next = norm[0] / power[0]
    field, image = own_ref[4:12, :], image_ref[...]
    residual = field - alpha * image
    data_scr[0:8, :] = alpha * field + alpha_next * (residual + beta * field)
    data_scr[8:16, :] = residual - alpha_next * ((image - alpha * twice_ref[...]) + beta * image)
    places = [own_ref[12:13, c * LANES : (c + 1) * LANES].astype(i32) - 1 for c in range(chunks)]
    chunk, lane, _ = invert(places, chunks)
    inv_chunk[...] = chunk
    inv_lane[...] = lane
    for d in range(chunks):
        value = pick(
            lambda s: data_scr[:, s * LANES : (s + 1) * LANES],
            chunks,
            inv_chunk[d : d + 1, :],
            inv_lane[d : d + 1, :],
            inv_lane[d : d + 1, :] >= 0,
        )
        field_out[:, d * LANES : (d + 1) * LANES] = value[0:8]
        residual_out[:, d * LANES : (d + 1) * LANES] = value[8:16]


def call(kernel, outs, ins, scratch=(), limit=LIMIT, cost=None):
    return pl.pallas_call(
        kernel,
        out_shape=[jax.ShapeDtypeStruct(shape, kind) for shape, kind in outs],
        in_specs=ins,
        out_specs=[VMEM if len(shape) < 3 or kind != bf16 else HBM for shape, kind in outs],
        scratch_shapes=list(scratch),
        compiler_params=pltpu.CompilerParams(vmem_limit_bytes=limit),
        cost_estimate=cost,
    )


def cost(parts):
    return pl.CostEstimate(flops=parts * 2 * 10**9, bytes_accessed=parts * 10**7, transcendentals=0)


def around(value, hops, tiles):
    return [lax.ppermute(value, "tiles", [(i, (i - hop) % tiles) for i in range(tiles)]) for hop in hops]


def local(obs_position, obs_sd, obs_var, innovations, obs_target, pair_table, pair_count):
    tiles = lax.axis_size("tiles")
    my_tile = lax.axis_index("tiles").astype(i32)
    rows = obs_sd.shape[0]
    chunks = rows // LANES
    hops = [sign * hop for hop in range(1, pair_table.shape[1]) for sign in (1, -1)]
    n = len(hops)
    capacity = 3 * rows // (2 * tiles)
    width = -(-capacity // LANES) * LANES
    boxes = tiles * width // LANES

    (outbox,) = call(
        functools.partial(outbox_kernel, tiles, width),
        [((tiles, FIELDS, width), f32)],
        [HBM] * 5,
        [
            pltpu.VMEM((FIELDS, rows), f32),
            pltpu.VMEM((2, rows), f32),
            pltpu.VMEM((1, rows), f32),
            pltpu.VMEM((1, rows), f32),
            pltpu.VMEM((8, rows), f32),
            pltpu.VMEM((1, rows), i32),
        ]
        + [pltpu.VMEM((boxes, LANES), i32)] * 3
        + [pltpu.SemaphoreType.DMA((5,))],
        64 * 2**20 - 2**16,
    )(obs_position, obs_sd[None], obs_var[None], innovations, obs_target[None])
    inbox = lax.all_to_all(outbox, "tiles", split_axis=0, concat_axis=0, tiled=True)
    share, own = call(
        sort_kernel,
        [((FIELDS, rows), f32), ((FIELDS, rows), f32)],
        [VMEM, SMEM],
        [pltpu.VMEM((chunks, LANES), i32)] * 2 + [pltpu.VMEM((boxes, BINS, LANES), f32)],
    )(inbox, pair_count)
    shares = around(share, hops, tiles)
    tile = my_tile[None]

    def operands(held):
        return [
            pltpu.SMEM((held * chunks // GROUP + UNIT,), i32),
            pltpu.VMEM((held + 1, 8, LANES), f32),
            pltpu.VMEM((held + 1, 16, LANES), bf16),
            pltpu.VMEM((2, chunks, LANES, LANES), f32),
            pltpu.VMEM((chunks, 8, LANES), f32),
            pltpu.VMEM((RING, UNIT * 2 * GROUP, LANES, LANES), bf16),
            pltpu.SemaphoreType.DMA((RING,)),
        ]

    def kept(held, most):
        units = min(most, -(-held * chunks // (GROUP * UNIT)))
        return (units + 1, UNIT * 2 * GROUP, LANES, LANES)

    listing = [pltpu.SMEM((chunks, LANES), i32), pltpu.SemaphoreType.DMA]
    field_kind = ((8, rows), f32)
    list_kind = ((chunks, LANES), i32)
    held = n * chunks
    inner, near, near_cache = call(
        first_inner_kernel,
        [field_kind, list_kind, (kept(chunks, INNER), bf16)],
        [SMEM, VMEM],
        listing + operands(chunks),
        cost=cost(1),
    )(tile, share)
    image, image_share, far, far_cache = call(
        functools.partial(first_outer_kernel, hops),
        [field_kind, field_kind, list_kind, (kept(held, OUTER), bf16)],
        [SMEM] + [VMEM] * (n + 3),
        listing + operands(held),
        cost=cost(4),
    )(tile, own, inner, share, *shares)
    vectors = around(image_share, hops, tiles)
    (inner_again,) = call(
        second_inner_kernel,
        [field_kind],
        [SMEM, VMEM, VMEM, HBM],
        operands(chunks),
        cost=cost(1),
    )(near, share, image_share, near_cache)
    twice, dots = call(
        functools.partial(second_outer_kernel, n),
        [field_kind, ((tiles, 8, LANES), f32)],
        [SMEM] + [VMEM] * 3 + [HBM] + [VMEM] * (2 * n + 1),
        operands(held),
        cost=cost(3),
    )(far, own, image, inner_again, far_cache, share, *shares, *vectors)
    dots = lax.all_to_all(dots, "tiles", split_axis=0, concat_axis=0, tiled=True)
    return tuple(
        call(
            place_kernel,
            [field_kind] * 2,
            [VMEM] * 4,
            [pltpu.VMEM((chunks, LANES), i32)] * 2 + [pltpu.VMEM((16, rows), f32)],
        )(own, image, twice, dots)
    )


def solution(mesh):
    both = ("groups", "tiles")
    placed = (P(None, both), P(both), P(both), P(None, both), P(both), P(both, None, None), P(both))
    return jax.shard_map(
        local,
        mesh=mesh,
        in_specs=placed,
        out_specs=(P(None, both), P(None, both)),
        check_vma=False,
    )
```

```python
import functools

import jax
import jax.numpy as jnp
from jax import lax
from jax.experimental import pallas as pl
from jax.experimental.pallas import tpu as pltpu
from jax.sharding import PartitionSpec as P

f32, bf16, i32 = jnp.float32, jnp.bfloat16, jnp.int32
LANES = 128
FIELDS = 16
BINS = 128
GROUP = 4
UNIT = 8
RING = 4
INNER = 8
OUTER = 18
TRANSPOSED = (((1,), (1,)), ((), ()))
VMEM = pl.BlockSpec(memory_space=pltpu.VMEM)
SMEM = pl.BlockSpec(memory_space=pltpu.SMEM)
HBM = pl.BlockSpec(memory_space=pltpu.HBM)
LIMIT = 40 * 2**20


def iota(shape, axis):
    return lax.broadcasted_iota(i32, shape, axis)


def running_sum_weights():
    shape = (LANES, 2 * LANES)
    row, col = iota(shape, 0), iota(shape, 1)
    return jnp.where((row <= col) | (col >= LANES), 1.0, 0.0).astype(bf16)


def dot(a, b):
    return jnp.dot(a, b, preferred_element_type=f32)


def dot_t(a, b):
    return lax.dot_general(a, b, TRANSPOSED, preferred_element_type=f32)


def invert(places, count):
    chunk_rows, lane_rows, here_rows, low_rows = [], [], [], []
    for chunk, place in enumerate(places):
        high = jnp.right_shift(place, 7)
        here = jnp.where(high == iota((count, LANES), 0), 1.0, 0.0)
        here_rows.append(here.astype(bf16))
        chunk_rows.append((here * float(chunk)).astype(bf16))
        lane_rows.append((here * iota((count, LANES), 1).astype(f32)).astype(bf16))
        low = jnp.bitwise_and(place, LANES - 1)
        low_rows.append(jnp.where(low == iota((LANES, LANES), 0), 1.0, 0.0).astype(bf16))
    left = jnp.concatenate(
        [jnp.concatenate(rows, axis=1) for rows in (chunk_rows, lane_rows, here_rows)], axis=0
    )
    found = dot_t(left, jnp.concatenate(low_rows, axis=1))
    chunk = found[:count].astype(i32)
    lane = found[count : 2 * count].astype(i32)
    return chunk, lane, found[2 * count :] > 0.5


def pick(load, sources, chunk, lane, here):
    total = None
    for source in range(sources):
        value = load(source)
        index = jnp.broadcast_to(lane, value.shape)
        value = jnp.take_along_axis(value, index, axis=1)
        total = value if total is None else jnp.where(chunk == source, value, total)
    return jnp.where(here, total, 0.0)


def outbox_kernel(
    tiles,
    width,
    pos_ref,
    sd_ref,
    var_ref,
    innov_ref,
    target_ref,
    out_ref,
    fields,
    pos_scr,
    sd_scr,
    var_scr,
    innov_scr,
    target_scr,
    inv_chunk,
    inv_lane,
    inv_here,
    sems,
):
    rows = pos_ref.shape[1]
    chunks = rows // LANES
    copies = [
        pltpu.make_async_copy(source, target, sems.at[k])
        for k, (source, target) in enumerate(
            (
                (target_ref, target_scr),
                (pos_ref, pos_scr),
                (sd_ref, sd_scr),
                (var_ref, var_scr),
                (innov_ref, innov_scr),
            )
        )
    ]
    for copy in copies:
        copy.start()
    fields[...] = jnp.zeros_like(fields)
    for copy in copies:
        copy.wait()
    fields[0:2, :] = pos_scr[...]
    fields[2:3, :] = sd_scr[...]
    fields[3:4, :] = var_scr[...]
    target = target_scr[...]
    owner = target // rows
    fields[12:13, :] = (target - owner * rows + 1).astype(f32)
    fields[4:12, :] = innov_scr[...]
    mine = [
        jnp.where(owner[:, c * LANES : (c + 1) * LANES] == iota((tiles, LANES), 0), 1.0, 0.0)
        for c in range(chunks)
    ]
    sums = dot(jnp.concatenate([m.astype(bf16) for m in mine], axis=0), running_sum_weights())
    before = (iota((tiles, LANES), 0) * width - 1).astype(f32)
    places = []
    for c in range(chunks):
        part = sums[c * tiles : (c + 1) * tiles]
        place = jnp.sum(mine[c] * (part[:, :LANES] + before), axis=0, keepdims=True)
        places.append(place.astype(i32))
        before = before + part[:, LANES:]
    count = tiles * width // LANES
    chunk, lane, here = invert(places, count)
    inv_chunk[...] = chunk
    inv_lane[...] = lane
    inv_here[...] = jnp.where(here, 1, 0)
    per_tile = width // LANES
    for d in range(count):
        value = pick(
            lambda s: fields[:, s * LANES : (s + 1) * LANES],
            chunks,
            inv_chunk[d : d + 1, :],
            inv_lane[d : d + 1, :],
            inv_here[d : d + 1, :] > 0,
        )
        first = d % per_tile * FIELDS
        if first + FIELDS <= out_ref.shape[1]:
            out_ref[d // per_tile, first : first + FIELDS, :] = value
        else:
            left = iota((FIELDS // 2, LANES), 1) < LANES // 2
            other = pltpu.roll(value[FIELDS // 2 :], LANES // 2, 1)
            out_ref[d // per_tile, first:, :] = jnp.where(left, value[: FIELDS // 2], other)


def sort_kernel(in_ref, count_ref, share_ref, own_ref, inv_chunk, inv_lane, rank_scr):
    tiles, depth, _ = in_ref.shape
    rows = own_ref.shape[1]
    chunks = rows // LANES
    whole = depth // FIELDS
    half = depth % FIELDS
    sources = tiles * whole + (tiles // 2 if half else 0)

    def load(s):
        if s < tiles * whole:
            first = s % whole * FIELDS
            return in_ref[s // whole, first : first + FIELDS, :]
        pair = 2 * (s - tiles * whole)
        one, two = in_ref[pair, whole * FIELDS :, :], in_ref[pair + 1, whole * FIELDS :, :]
        left = iota((half, LANES), 1) < LANES // 2
        return jnp.concatenate(
            [
                jnp.where(left, one, pltpu.roll(two, LANES // 2, 1)),
                jnp.where(left, pltpu.roll(one, LANES // 2, 1), two),
            ],
            axis=0,
        )

    weights = running_sum_weights()
    before = jnp.full((BINS, LANES), -1.0, f32)
    for s in range(sources):
        data = load(s)
        bins = jnp.clip((data[1:2] * (BINS / 8.0)).astype(i32), 0, BINS - 1)
        bins = jnp.where(data[12:13] > 0.5, bins, -1)
        member = jnp.where(bins == iota((BINS, LANES), 0), 1.0, 0.0)
        part = dot(member.astype(bf16), weights)
        rank_scr[s] = member * (part[:, :LANES] + before)
        before = before + part[:, LANES:]
    totals = before + 1.0
    high = jnp.floor(totals * (1.0 / 64.0))
    low = totals - 64.0 * high
    earlier = jnp.where(iota((BINS, BINS), 1) < iota((BINS, BINS), 0), 1.0, 0.0).astype(bf16)
    base = 64.0 * dot(earlier, high.astype(bf16)) + dot(earlier, low.astype(bf16))
    places = []
    for s in range(sources):
        data = load(s)
        bins = jnp.clip((data[1:2] * (BINS / 8.0)).astype(i32), 0, BINS - 1)
        here = data[12:13] > 0.5
        member = jnp.where(bins == iota((BINS, LANES), 0), base, 0.0)
        place = jnp.sum(member + rank_scr[s], axis=0, keepdims=True).astype(i32)
        places.append(jnp.where(here, place, -1))
    chunk, lane, here = invert(places, chunks)
    inv_chunk[...] = chunk
    inv_lane[...] = lane
    for d in range(chunks):
        own_ref[:, d * LANES : (d + 1) * LANES] = pick(
            load, sources, inv_chunk[d : d + 1, :], inv_lane[d : d + 1, :], inv_lane[d : d + 1, :] >= 0
        )
    share_ref[...] = jnp.zeros_like(share_ref)
    share_ref[0:8, :] = own_ref[4:12, :] * (own_ref[2:3, :] * (1.0 / 256.0))
    share_ref[8:10, :] = own_ref[0:2, :] * 4.0
    stat = jnp.zeros((1, LANES), f32)
    for axis in range(2):
        wide = jnp.concatenate(
            [share_ref[8 + axis : 9 + axis, c * LANES : (c + 1) * LANES] for c in range(chunks)], axis=0
        )
        for which, value in ((0, jnp.min(wide, axis=1, keepdims=True)), (1, jnp.max(wide, axis=1, keepdims=True))):
            lanes = iota((chunks, LANES), 1) - chunks * (2 * axis + which)
            stat = stat + jnp.sum(
                jnp.where(lanes == iota((chunks, LANES), 0), value, 0.0), axis=0, keepdims=True
            )
    stat = jnp.where(iota((1, LANES), 1) == 4 * chunks, count_ref[0].astype(f32), stat)
    share_ref[10:11, 0:LANES] = stat


def make_list(hops, tile_ref, own_share, shares, list_ref):
    chunks = list_ref.shape[0]
    my_tile = tile_ref[0]
    own = own_share[10:11, 0:LANES]
    lane, sub = iota((chunks, LANES), 1), iota((chunks, LANES), 0)
    x_low, x_high, y_low, y_high = [
        jnp.sum(jnp.where(lane == sub + chunks * q, own, 0.0), axis=1, keepdims=True) for q in range(4)
    ]
    own_count = own[:, 4 * chunks : 4 * chunks + 1]
    need = jnp.zeros((chunks, LANES), f32)
    for nb, hop in enumerate(hops):
        other = shares[nb][10:11, 0:LANES]
        at = [pltpu.roll(other, (nb * chunks - q * chunks) % LANES, 1) for q in range(4)]
        gap_x = jnp.maximum(jnp.maximum(at[0] - x_high, x_low - at[1]), 0.0)
        gap_y = jnp.maximum(jnp.maximum(at[2] - y_high, y_low - at[3]), 0.0)
        near = gap_x * gap_x + gap_y * gap_y < 16.001
        count = own_count if hop >= 0 else other[:, 4 * chunks : 4 * chunks + 1]
        listed = (count > abs(hop) + 0.5) & (my_tile + hop >= 0)
        inside = (lane >= nb * chunks) & (lane < (nb + 1) * chunks)
        need = need + jnp.where(near & listed & inside, 1.0, 0.0)
    total = dot(need.astype(bf16), running_sum_weights())
    slot = jnp.where(need > 0.5, total[:, :LANES] - 1.0, -1.0)
    numbers = jnp.broadcast_to(iota((8, LANES), 1).astype(f32), (8, LANES)).astype(bf16)
    for r in range(chunks):
        match = jnp.where(slot[r : r + 1] == iota((LANES, LANES), 0).astype(f32), 1.0, 0.0)
        found = dot_t(numbers, match.astype(bf16))[0:1]
        amount = total[r : r + 1, LANES:]
        row = jnp.where(iota((1, LANES), 1).astype(f32) < amount, found, float(len(hops) * chunks))
        row = jnp.where(iota((1, LANES), 1) == LANES - 1, amount, row)
        list_ref[r : r + 1, :] = row.astype(i32)


def load_where(shares, where_scr):
    chunks = shares[0].shape[1] // LANES
    for nb, share in enumerate(shares):
        for c in range(chunks):
            where_scr[nb * chunks + c] = share[8:16, c * LANES : (c + 1) * LANES]
    where_scr[len(shares) * chunks] = jnp.zeros((8, LANES), f32)


def load_vectors(vectors, vec_scr):
    chunks = vectors[0].shape[1] // LANES
    for nb, vector in enumerate(vectors):
        for c in range(chunks):
            value = vector[0:8, c * LANES : (c + 1) * LANES]
            high = value.astype(bf16)
            low = (value - high.astype(f32)).astype(bf16)
            vec_scr[nb * chunks + c] = jnp.concatenate([high, low], axis=0)
    vec_scr[len(vectors) * chunks] = jnp.zeros((16, LANES), bf16)


def block(x_col, y_col, x_row, y_row):
    dx = x_col - x_row
    dy = y_col - y_row
    square = jnp.maximum(dx * dx + dy * dy, 1e-30)
    distance = square * lax.rsqrt(square)
    inside = jnp.maximum(4.0 - distance, 0.0)
    inside = inside * inside
    corr = inside * inside * (distance + 1.0)
    high = corr.astype(bf16)
    return high, (corr - high.astype(f32)).astype(bf16)


def multiply(total, high, low, vec):
    both = jnp.concatenate([high, low], axis=1)
    return total + dot_t(jnp.concatenate([vec, vec], axis=1), both)


def flatten(list_smem, flat, chunks):
    def chunk_rows(r, number):
        def one(g, number):
            flat[number] = r * LANES + g * GROUP
            return number + 1

        return lax.fori_loop(0, (list_smem[r, LANES - 1] + (GROUP - 1)) // GROUP, one, number)

    number = lax.fori_loop(0, chunks, chunk_rows, 0)
    for k in range(UNIT):
        flat[number + k] = LANES - 2 * GROUP
    return (number + UNIT - 1) // UNIT


def own_columns(own_share, columns):
    for r in range(columns.shape[1]):
        column = own_share[8:16, r * LANES : (r + 1) * LANES].T
        for k in range(2):
            columns[k, r] = jnp.broadcast_to(column[:, k : k + 1], (LANES, LANES))


def ring_slot(stage, unit):
    return stage.at[unit % RING]


def group(list_smem, where_scr, vec_scr, columns, entry, total, keep):
    r, start = entry // LANES, entry % LANES
    x_col, y_col = columns[0, r], columns[1, r]
    for j in range(GROUP):
        c = list_smem[r, start + j]
        high, low = block(x_col, y_col, where_scr[c, 0:1, :], where_scr[c, 1:2, :])
        total = multiply(total, high, low, vec_scr[c])
        keep.append((high, low))
    return total


def add_rows(sums, entry, total):
    r = entry // LANES
    sums[r] = sums[r] + (total[0:8] + total[8:16])


def put_rows(out_ref, sums):
    for r in range(sums.shape[0]):
        out_ref[:, r * LANES : (r + 1) * LANES] = sums[r]


def product(list_smem, flat, where_scr, vec_scr, columns, sums, cache_ref, stage, sems):
    room = cache_ref.shape[0] - 1
    blank = jnp.zeros((16, LANES), f32)
    sums[...] = jnp.zeros_like(sums)
    units = flatten(list_smem, flat, sums.shape[0])

    def save(unit):
        return pltpu.make_async_copy(
            ring_slot(stage, unit), cache_ref.at[jnp.minimum(unit, room)], sems.at[unit % RING]
        )

    def one_unit(unit, _):
        pl.when(unit >= RING)(lambda: save(unit - RING).wait())
        slot = unit % RING
        entries = [flat[unit * UNIT + g] for g in range(UNIT)]
        kept, totals = [], []
        for entry in entries:
            totals.append(group(list_smem, where_scr, vec_scr, columns, entry, blank, kept))
        for k, (high, low) in enumerate(kept):
            stage[slot, 2 * k] = high
            stage[slot, 2 * k + 1] = low
        for entry, total in zip(entries, totals):
            add_rows(sums, entry, total)
        save(unit).start()
        return 0

    lax.fori_loop(0, units, one_unit, 0)
    for k in range(RING):
        last = units - 1 - (units - 1 - k) % RING
        pl.when(units > k)(lambda last=last: save(last).wait())


def product_again(list_smem, flat, where_scr, vec_scr, columns, sums, cache_ref, stage, sems, load):
    room = cache_ref.shape[0] - 1
    blank = jnp.zeros((16, LANES), f32)
    sums[...] = jnp.zeros_like(sums)
    units = flatten(list_smem, flat, sums.shape[0])
    ready = jnp.minimum(units, room)

    def fetch(unit):
        return pltpu.make_async_copy(cache_ref.at[unit], ring_slot(stage, unit), sems.at[unit % RING])

    for k in range(RING):
        pl.when(k < ready)(lambda k=k: fetch(k).start())
    load(units > ready)

    def one_unit(unit, _):
        fetch(unit).wait()
        slot = unit % RING
        entries = [flat[unit * UNIT + g] for g in range(UNIT)]
        totals = []
        for g, entry in enumerate(entries):
            r, start = entry // LANES, entry % LANES
            total = blank
            for j in range(GROUP):
                k = g * GROUP + j
                vec = vec_scr[list_smem[r, start + j]]
                total = multiply(total, stage[slot, 2 * k], stage[slot, 2 * k + 1], vec)
            totals.append(total)
        for entry, total in zip(entries, totals):
            add_rows(sums, entry, total)
        pl.when(unit + RING < ready)(lambda: fetch(unit + RING).start())
        return 0

    lax.fori_loop(0, ready, one_unit, 0)

    def fresh(number, _):
        entry = flat[number]
        add_rows(sums, entry, group(list_smem, where_scr, vec_scr, columns, entry, blank, []))
        return 0

    lax.fori_loop(ready * UNIT, units * UNIT, fresh, 0)


def first_sums(hops, tile_ref, own_share, shares, list_ref, cache_ref, scratch):
    list_smem, sem, flat, where_scr, vec_scr, columns, sums, stage, sems = scratch
    make_list(hops, tile_ref, own_share, shares, list_ref)
    copy = pltpu.make_async_copy(list_ref, list_smem, sem)
    copy.start()
    load_where(shares, where_scr)
    load_vectors(shares, vec_scr)
    own_columns(own_share, columns)
    copy.wait()
    product(list_smem, flat, where_scr, vec_scr, columns, sums, cache_ref, stage, sems)
    return sums


def second_sums(list_smem, own_share, shares, vectors, cache_ref, scratch):
    flat, where_scr, vec_scr, columns, sums, stage, sems = scratch

    def load(needed):
        load_vectors(vectors, vec_scr)

        @pl.when(needed)
        def _():
            load_where(shares, where_scr)
            own_columns(own_share, columns)

    product_again(list_smem, flat, where_scr, vec_scr, columns, sums, cache_ref, stage, sems, load)
    return sums


def first_inner_kernel(tile_ref, own_share, out_ref, list_ref, cache_ref, *scratch):
    put_rows(out_ref, first_sums([0], tile_ref, own_share, [own_share], list_ref, cache_ref, scratch))


def first_outer_kernel(hops, tile_ref, own_ref, inner_ref, own_share, *refs):
    n = len(hops)
    shares = refs[:n]
    image_ref, share_ref, list_ref, cache_ref = refs[n : n + 4]
    put_rows(image_ref, first_sums(hops, tile_ref, own_share, shares, list_ref, cache_ref, refs[n + 4 :]))
    field = own_ref[4:12, :]
    image = own_ref[3:4, :] * field + own_ref[2:3, :] * (inner_ref[...] + image_ref[...])
    image_ref[...] = image
    share_ref[...] = image * (own_ref[2:3, :] * (1.0 / 256.0))


def second_inner_kernel(list_smem, own_share, vector, cache_ref, out_ref, *scratch):
    put_rows(out_ref, second_sums(list_smem, own_share, [own_share], [vector], cache_ref, scratch))


def two_sum(a, b):
    total = a + b
    back = total - a
    return total, (a - (total - back)) + (b - back)


def halves(a):
    scaled = a * 4097.0
    high = scaled - (scaled - a)
    return high, a - high


def two_product(a, b):
    total = a * b
    (a_high, a_low), (b_high, b_low) = halves(a), halves(b)
    error = ((a_high * b_high - total) + a_high * b_low + a_low * b_high) + a_low * b_low
    return total, error


def pair_sum(a, b):
    total, rest = two_sum(a[0], b[0])
    rest = rest + (a[1] + b[1])
    high = total + rest
    return high, rest - (high - total)


def pair_product(a, b):
    total, rest = two_product(a[0], b[0])
    rest = rest + (a[0] * b[1] + a[1] * b[0])
    high = total + rest
    return high, rest - (high - total)


def lane_sums(left, right):
    total = (jnp.zeros((8, LANES), f32), jnp.zeros((8, LANES), f32))
    for c in range(left.shape[1] // LANES):
        lanes = slice(c * LANES, (c + 1) * LANES)
        value, error = two_sum(total[0], left[:, lanes] * right[:, lanes])
        total = (value, total[1] + error)
    shift = LANES // 2
    while shift:
        total = pair_sum(total, tuple(pltpu.roll(part, shift, 1) for part in total))
        shift //= 2
    return total


def second_outer_kernel(n, list_smem, own_ref, image_ref, inner_ref, cache_ref, own_share, *refs):
    shares, vectors, twice_ref, dots_ref = refs[:n], refs[n : 2 * n], refs[2 * n], refs[2 * n + 1]
    put_rows(twice_ref, second_sums(list_smem, own_share, shares, vectors, cache_ref, refs[2 * n + 2 :]))
    image = image_ref[...]
    twice = own_ref[3:4, :] * image + own_ref[2:3, :] * (inner_ref[...] + twice_ref[...])
    twice_ref[...] = twice
    field = own_ref[4:12, :]
    lane = iota((8, LANES), 1)
    dots = jnp.zeros((8, LANES), f32)
    pairs = ((field, field), (field, image), (image, image), (field, twice), (image, twice))
    for k, (left, right) in enumerate(pairs):
        value, rest = lane_sums(left, right)
        dots = jnp.where(lane == 2 * k, value, jnp.where(lane == 2 * k + 1, rest, dots))
    dots_ref[...] = jnp.broadcast_to(dots[None], dots_ref.shape)


def place_kernel(own_ref, image_ref, twice_ref, dots_ref, field_out, residual_out, inv_chunk, inv_lane, data_scr):
    chunks = own_ref.shape[1] // LANES

    def held(t):
        part = dots_ref[t]
        return part, pltpu.roll(part, LANES - 1, 1)

    sums = held(0)
    for t in range(1, dots_ref.shape[0]):
        sums = pair_sum(sums, held(t))
    pp, pq, qq, pz, qz = [tuple(part[:, 2 * k : 2 * k + 1] for part in sums) for k in range(5)]
    alpha = pp[0] / pq[0]
    zero = jnp.zeros_like(alpha)
    first = (alpha, zero)
    minus = (-alpha, zero)
    square = pair_product(first, first)
    norm = pair_sum(pair_sum(pp, pair_product((-2.0 * alpha, zero), pq)), pair_product(square, qq))
    beta = norm[0] / pp[0]
    grown = two_sum(jnp.ones_like(beta), beta)
    power = pair_sum(
        pair_product(grown, pair_sum(pair_product(grown, pq), pair_product(minus, pair_sum(qq, pz)))),
        pair_product(square, qz),
    )
    alpha_next = norm[0] / power[0]
    field, image = own_ref[4:12, :], image_ref[...]
    residual = field - alpha * image
    data_scr[0:8, :] = alpha * field + alpha_next * (residual + beta * field)
    data_scr[8:16, :] = residual - alpha_next * ((image - alpha * twice_ref[...]) + beta * image)
    places = [own_ref[12:13, c * LANES : (c + 1) * LANES].astype(i32) - 1 for c in range(chunks)]
    chunk, lane, _ = invert(places, chunks)
    inv_chunk[...] = chunk
    inv_lane[...] = lane
    for d in range(chunks):
        value = pick(
            lambda s: data_scr[:, s * LANES : (s + 1) * LANES],
            chunks,
            inv_chunk[d : d + 1, :],
            inv_lane[d : d + 1, :],
            inv_lane[d : d + 1, :] >= 0,
        )
        field_out[:, d * LANES : (d + 1) * LANES] = value[0:8]
        residual_out[:, d * LANES : (d + 1) * LANES] = value[8:16]


def call(kernel, outs, ins, scratch=(), limit=LIMIT, cost=None):
    return pl.pallas_call(
        kernel,
        out_shape=[jax.ShapeDtypeStruct(shape, kind) for shape, kind in outs],
        in_specs=ins,
        out_specs=[VMEM if len(shape) < 3 or kind != bf16 else HBM for shape, kind in outs],
        scratch_shapes=list(scratch),
        compiler_params=pltpu.CompilerParams(vmem_limit_bytes=limit),
        cost_estimate=cost,
    )


def cost(parts):
    return pl.CostEstimate(flops=parts * 2 * 10**9, bytes_accessed=parts * 10**7, transcendentals=0)


def around(value, hops, tiles):
    return [lax.ppermute(value, "tiles", [(i, (i - hop) % tiles) for i in range(tiles)]) for hop in hops]


def local(obs_position, obs_sd, obs_var, innovations, obs_target, pair_table, pair_count):
    tiles = lax.axis_size("tiles")
    my_tile = lax.axis_index("tiles").astype(i32)
    rows = obs_sd.shape[0]
    chunks = rows // LANES
    hops = [sign * hop for hop in range(1, pair_table.shape[1]) for sign in (1, -1)]
    n = len(hops)
    capacity = 3 * rows // (2 * tiles)
    width = -(-capacity // LANES) * LANES
    boxes = tiles * width // LANES
    folded = capacity > LANES and 0 < capacity % LANES <= LANES // 2 and tiles % 2 == 0
    depth = width // LANES * FIELDS - (FIELDS // 2 if folded else 0)
    arrivals = tiles * (depth // FIELDS) + (tiles // 2 if folded else 0)

    (outbox,) = call(
        functools.partial(outbox_kernel, tiles, width),
        [((tiles, depth, LANES), f32)],
        [HBM] * 5,
        [
            pltpu.VMEM((FIELDS, rows), f32),
            pltpu.VMEM((2, rows), f32),
            pltpu.VMEM((1, rows), f32),
            pltpu.VMEM((1, rows), f32),
            pltpu.VMEM((8, rows), f32),
            pltpu.VMEM((1, rows), i32),
        ]
        + [pltpu.VMEM((boxes, LANES), i32)] * 3
        + [pltpu.SemaphoreType.DMA((5,))],
        64 * 2**20 - 2**16,
    )(obs_position, obs_sd[None], obs_var[None], innovations, obs_target[None])
    inbox = lax.all_to_all(outbox, "tiles", split_axis=0, concat_axis=0, tiled=True)
    share, own = call(
        sort_kernel,
        [((FIELDS, rows), f32), ((FIELDS, rows), f32)],
        [VMEM, SMEM],
        [pltpu.VMEM((chunks, LANES), i32)] * 2 + [pltpu.VMEM((arrivals, BINS, LANES), f32)],
    )(inbox, pair_count)
    shares = around(share, hops, tiles)
    tile = my_tile[None]

    def operands(held):
        return [
            pltpu.SMEM((held * chunks // GROUP + UNIT,), i32),
            pltpu.VMEM((held + 1, 8, LANES), f32),
            pltpu.VMEM((held + 1, 16, LANES), bf16),
            pltpu.VMEM((2, chunks, LANES, LANES), f32),
            pltpu.VMEM((chunks, 8, LANES), f32),
            pltpu.VMEM((RING, UNIT * 2 * GROUP, LANES, LANES), bf16),
            pltpu.SemaphoreType.DMA((RING,)),
        ]

    def kept(held, most):
        units = min(most, -(-held * chunks // (GROUP * UNIT)))
        return (units + 1, UNIT * 2 * GROUP, LANES, LANES)

    listing = [pltpu.SMEM((chunks, LANES), i32), pltpu.SemaphoreType.DMA]
    field_kind = ((8, rows), f32)
    list_kind = ((chunks, LANES), i32)
    held = n * chunks
    inner, near, near_cache = call(
        first_inner_kernel,
        [field_kind, list_kind, (kept(chunks, INNER), bf16)],
        [SMEM, VMEM],
        listing + operands(chunks),
        cost=cost(1),
    )(tile, share)
    image, image_share, far, far_cache = call(
        functools.partial(first_outer_kernel, hops),
        [field_kind, field_kind, list_kind, (kept(held, OUTER), bf16)],
        [SMEM] + [VMEM] * (n + 3),
        listing + operands(held),
        cost=cost(4),
    )(tile, own, inner, share, *shares)
    vectors = around(image_share, hops, tiles)
    (inner_again,) = call(
        second_inner_kernel,
        [field_kind],
        [SMEM, VMEM, VMEM, HBM],
        operands(chunks),
        cost=cost(1),
    )(near, share, image_share, near_cache)
    twice, dots = call(
        functools.partial(second_outer_kernel, n),
        [field_kind, ((tiles, 8, LANES), f32)],
        [SMEM] + [VMEM] * 3 + [HBM] + [VMEM] * (2 * n + 1),
        operands(held),
        cost=cost(3),
    )(far, own, image, inner_again, far_cache, share, *shares, *vectors)
    dots = lax.all_to_all(dots, "tiles", split_axis=0, concat_axis=0, tiled=True)
    return tuple(
        call(
            place_kernel,
            [field_kind] * 2,
            [VMEM] * 4,
            [pltpu.VMEM((chunks, LANES), i32)] * 2 + [pltpu.VMEM((16, rows), f32)],
        )(own, image, twice, dots)
    )


def solution(mesh):
    both = ("groups", "tiles")
    placed = (P(None, both), P(both), P(both), P(None, both), P(both), P(both, None, None), P(both))
    return jax.shard_map(
        local,
        mesh=mesh,
        in_specs=placed,
        out_specs=(P(None, both), P(None, both)),
        check_vma=False,
    )
```

```python
import functools

import jax
import jax.numpy as jnp
from jax import lax
from jax.experimental import pallas as pl
from jax.experimental.pallas import tpu as pltpu
from jax.sharding import PartitionSpec as P

f32, bf16, i32 = jnp.float32, jnp.bfloat16, jnp.int32
LANES = 128
FIELDS = 16
BINS = 128
INNER_GROUP = 2
OUTER_GROUP = 4
UNIT = 32
RING = 4
INNER = 8
OUTER = 18
TRANSPOSED = (((1,), (1,)), ((), ()))
VMEM = pl.BlockSpec(memory_space=pltpu.VMEM)
SMEM = pl.BlockSpec(memory_space=pltpu.SMEM)
HBM = pl.BlockSpec(memory_space=pltpu.HBM)
LIMIT = 40 * 2**20


def iota(shape, axis):
    return lax.broadcasted_iota(i32, shape, axis)


def running_sum_weights():
    shape = (LANES, 2 * LANES)
    row, col = iota(shape, 0), iota(shape, 1)
    return jnp.where((row <= col) | (col >= LANES), 1.0, 0.0).astype(bf16)


def dot(a, b):
    return jnp.dot(a, b, preferred_element_type=f32)


def dot_t(a, b):
    return lax.dot_general(a, b, TRANSPOSED, preferred_element_type=f32)


def invert(places, count):
    chunk_rows, lane_rows, here_rows, low_rows = [], [], [], []
    for chunk, place in enumerate(places):
        high = jnp.right_shift(place, 7)
        here = jnp.where(high == iota((count, LANES), 0), 1.0, 0.0)
        here_rows.append(here.astype(bf16))
        chunk_rows.append((here * float(chunk)).astype(bf16))
        lane_rows.append((here * iota((count, LANES), 1).astype(f32)).astype(bf16))
        low = jnp.bitwise_and(place, LANES - 1)
        low_rows.append(jnp.where(low == iota((LANES, LANES), 0), 1.0, 0.0).astype(bf16))
    left = jnp.concatenate(
        [jnp.concatenate(rows, axis=1) for rows in (chunk_rows, lane_rows, here_rows)], axis=0
    )
    found = dot_t(left, jnp.concatenate(low_rows, axis=1))
    chunk = found[:count].astype(i32)
    lane = found[count : 2 * count].astype(i32)
    return chunk, lane, found[2 * count :] > 0.5


def pick(load, sources, chunk, lane, here):
    total = None
    for source in range(sources):
        value = load(source)
        index = jnp.broadcast_to(lane, value.shape)
        value = jnp.take_along_axis(value, index, axis=1)
        total = value if total is None else jnp.where(chunk == source, value, total)
    return jnp.where(here, total, 0.0)


def outbox_kernel(
    tiles,
    width,
    pos_ref,
    sd_ref,
    var_ref,
    innov_ref,
    target_ref,
    out_ref,
    fields,
    pos_scr,
    sd_scr,
    var_scr,
    innov_scr,
    target_scr,
    inv_chunk,
    inv_lane,
    inv_here,
    sems,
):
    rows = pos_ref.shape[1]
    chunks = rows // LANES
    copies = [
        pltpu.make_async_copy(source, target, sems.at[k])
        for k, (source, target) in enumerate(
            (
                (target_ref, target_scr),
                (pos_ref, pos_scr),
                (sd_ref, sd_scr),
                (var_ref, var_scr),
                (innov_ref, innov_scr),
            )
        )
    ]
    for copy in copies:
        copy.start()
    fields[...] = jnp.zeros_like(fields)
    for copy in copies:
        copy.wait()
    fields[0:2, :] = pos_scr[...]
    fields[2:3, :] = sd_scr[...]
    fields[3:4, :] = var_scr[...]
    target = target_scr[...]
    owner = target // rows
    fields[12:13, :] = (target - owner * rows + 1).astype(f32)
    fields[4:12, :] = innov_scr[...]
    mine = [
        jnp.where(owner[:, c * LANES : (c + 1) * LANES] == iota((tiles, LANES), 0), 1.0, 0.0)
        for c in range(chunks)
    ]
    sums = dot(jnp.concatenate([m.astype(bf16) for m in mine], axis=0), running_sum_weights())
    before = (iota((tiles, LANES), 0) * width - 1).astype(f32)
    places = []
    for c in range(chunks):
        part = sums[c * tiles : (c + 1) * tiles]
        place = jnp.sum(mine[c] * (part[:, :LANES] + before), axis=0, keepdims=True)
        places.append(place.astype(i32))
        before = before + part[:, LANES:]
    count = tiles * width // LANES
    chunk, lane, here = invert(places, count)
    inv_chunk[...] = chunk
    inv_lane[...] = lane
    inv_here[...] = jnp.where(here, 1, 0)
    per_tile = width // LANES
    for d in range(count):
        value = pick(
            lambda s: fields[:, s * LANES : (s + 1) * LANES],
            chunks,
            inv_chunk[d : d + 1, :],
            inv_lane[d : d + 1, :],
            inv_here[d : d + 1, :] > 0,
        )
        first = d % per_tile * FIELDS
        if first + FIELDS <= out_ref.shape[1]:
            out_ref[d // per_tile, first : first + FIELDS, :] = value
        else:
            left = iota((FIELDS // 2, LANES), 1) < LANES // 2
            other = pltpu.roll(value[FIELDS // 2 :], LANES // 2, 1)
            out_ref[d // per_tile, first:, :] = jnp.where(left, value[: FIELDS // 2], other)


def sort_kernel(in_ref, count_ref, share_ref, own_ref, inv_chunk, inv_lane, rank_scr):
    tiles, depth, _ = in_ref.shape
    rows = own_ref.shape[1]
    chunks = rows // LANES
    whole = depth // FIELDS
    half = depth % FIELDS
    sources = tiles * whole + (tiles // 2 if half else 0)

    def load(s):
        if s < tiles * whole:
            first = s % whole * FIELDS
            return in_ref[s // whole, first : first + FIELDS, :]
        pair = 2 * (s - tiles * whole)
        one, two = in_ref[pair, whole * FIELDS :, :], in_ref[pair + 1, whole * FIELDS :, :]
        left = iota((half, LANES), 1) < LANES // 2
        return jnp.concatenate(
            [
                jnp.where(left, one, pltpu.roll(two, LANES // 2, 1)),
                jnp.where(left, pltpu.roll(one, LANES // 2, 1), two),
            ],
            axis=0,
        )

    weights = running_sum_weights()
    before = jnp.full((BINS, LANES), -1.0, f32)
    for s in range(sources):
        data = load(s)
        bins = jnp.clip((data[1:2] * (BINS / 8.0)).astype(i32), 0, BINS - 1)
        bins = jnp.where(data[12:13] > 0.5, bins, -1)
        member = jnp.where(bins == iota((BINS, LANES), 0), 1.0, 0.0)
        part = dot(member.astype(bf16), weights)
        rank_scr[s] = member * (part[:, :LANES] + before)
        before = before + part[:, LANES:]
    totals = before + 1.0
    high = jnp.floor(totals * (1.0 / 64.0))
    low = totals - 64.0 * high
    earlier = jnp.where(iota((BINS, BINS), 1) < iota((BINS, BINS), 0), 1.0, 0.0).astype(bf16)
    base = 64.0 * dot(earlier, high.astype(bf16)) + dot(earlier, low.astype(bf16))
    places = []
    for s in range(sources):
        data = load(s)
        bins = jnp.clip((data[1:2] * (BINS / 8.0)).astype(i32), 0, BINS - 1)
        here = data[12:13] > 0.5
        member = jnp.where(bins == iota((BINS, LANES), 0), base, 0.0)
        place = jnp.sum(member + rank_scr[s], axis=0, keepdims=True).astype(i32)
        places.append(jnp.where(here, place, -1))
    chunk, lane, here = invert(places, chunks)
    inv_chunk[...] = chunk
    inv_lane[...] = lane
    for d in range(chunks):
        own_ref[:, d * LANES : (d + 1) * LANES] = pick(
            load, sources, inv_chunk[d : d + 1, :], inv_lane[d : d + 1, :], inv_lane[d : d + 1, :] >= 0
        )
    share_ref[...] = jnp.zeros_like(share_ref)
    share_ref[0:8, :] = own_ref[4:12, :] * (own_ref[2:3, :] * (1.0 / 256.0))
    share_ref[8:10, :] = own_ref[0:2, :] * 4.0
    stat = jnp.zeros((1, LANES), f32)
    for axis in range(2):
        wide = jnp.concatenate(
            [share_ref[8 + axis : 9 + axis, c * LANES : (c + 1) * LANES] for c in range(chunks)], axis=0
        )
        for which, value in ((0, jnp.min(wide, axis=1, keepdims=True)), (1, jnp.max(wide, axis=1, keepdims=True))):
            lanes = iota((chunks, LANES), 1) - chunks * (2 * axis + which)
            stat = stat + jnp.sum(
                jnp.where(lanes == iota((chunks, LANES), 0), value, 0.0), axis=0, keepdims=True
            )
    stat = jnp.where(iota((1, LANES), 1) == 4 * chunks, count_ref[0].astype(f32), stat)
    share_ref[10:11, 0:LANES] = stat


def make_list(hops, tile_ref, own_share, shares, list_ref):
    chunks = list_ref.shape[0]
    my_tile = tile_ref[0]
    own = own_share[10:11, 0:LANES]
    lane, sub = iota((chunks, LANES), 1), iota((chunks, LANES), 0)
    x_low, x_high, y_low, y_high = [
        jnp.sum(jnp.where(lane == sub + chunks * q, own, 0.0), axis=1, keepdims=True) for q in range(4)
    ]
    own_count = own[:, 4 * chunks : 4 * chunks + 1]
    need = jnp.zeros((chunks, LANES), f32)
    for nb, hop in enumerate(hops):
        other = shares[nb][10:11, 0:LANES]
        at = [pltpu.roll(other, (nb * chunks - q * chunks) % LANES, 1) for q in range(4)]
        gap_x = jnp.maximum(jnp.maximum(at[0] - x_high, x_low - at[1]), 0.0)
        gap_y = jnp.maximum(jnp.maximum(at[2] - y_high, y_low - at[3]), 0.0)
        near = gap_x * gap_x + gap_y * gap_y < 16.001
        count = own_count if hop >= 0 else other[:, 4 * chunks : 4 * chunks + 1]
        listed = (count > abs(hop) + 0.5) & (my_tile + hop >= 0)
        inside = (lane >= nb * chunks) & (lane < (nb + 1) * chunks)
        need = need + jnp.where(near & listed & inside, 1.0, 0.0)
    total = dot(need.astype(bf16), running_sum_weights())
    slot = jnp.where(need > 0.5, total[:, :LANES] - 1.0, -1.0)
    numbers = jnp.broadcast_to(iota((8, LANES), 1).astype(f32), (8, LANES)).astype(bf16)
    for r in range(chunks):
        match = jnp.where(slot[r : r + 1] == iota((LANES, LANES), 0).astype(f32), 1.0, 0.0)
        found = dot_t(numbers, match.astype(bf16))[0:1]
        amount = total[r : r + 1, LANES:]
        row = jnp.where(iota((1, LANES), 1).astype(f32) < amount, found, float(len(hops) * chunks))
        row = jnp.where(iota((1, LANES), 1) == LANES - 1, amount, row)
        list_ref[r : r + 1, :] = row.astype(i32)


def load_where(shares, where_scr):
    chunks = shares[0].shape[1] // LANES
    for nb, share in enumerate(shares):
        for c in range(chunks):
            where_scr[nb * chunks + c] = share[8:16, c * LANES : (c + 1) * LANES]
    where_scr[len(shares) * chunks] = jnp.zeros((8, LANES), f32)


def load_vectors(vectors, vec_scr):
    chunks = vectors[0].shape[1] // LANES
    for nb, vector in enumerate(vectors):
        for c in range(chunks):
            value = vector[0:8, c * LANES : (c + 1) * LANES]
            high = value.astype(bf16)
            low = (value - high.astype(f32)).astype(bf16)
            vec_scr[nb * chunks + c] = jnp.concatenate([high, low], axis=0)
    vec_scr[len(vectors) * chunks] = jnp.zeros((16, LANES), bf16)


def block(x_col, y_col, x_row, y_row):
    dx = x_col - x_row
    dy = y_col - y_row
    square = jnp.maximum(dx * dx + dy * dy, 1e-30)
    distance = square * lax.rsqrt(square)
    inside = jnp.maximum(4.0 - distance, 0.0)
    inside = inside * inside
    corr = inside * inside * (distance + 1.0)
    high = corr.astype(bf16)
    return high, (corr - high.astype(f32)).astype(bf16)


def multiply(total, high, low, vec):
    both = jnp.concatenate([high, low], axis=1)
    return total + dot_t(jnp.concatenate([vec, vec], axis=1), both)


def flatten(size, list_smem, flat, chunks):
    def chunk_rows(r, number):
        def one(g, number):
            flat[number] = r * LANES + g * size
            return number + 1

        return lax.fori_loop(0, (list_smem[r, LANES - 1] + (size - 1)) // size, one, number)

    number = lax.fori_loop(0, chunks, chunk_rows, 0)
    groups = UNIT // size
    for k in range(groups):
        flat[number + k] = LANES - 2 * size
    return (number + groups // 2 - 1) // groups, (number + groups - 1) // groups


def own_columns(own_share, columns):
    for r in range(columns.shape[1]):
        column = own_share[8:16, r * LANES : (r + 1) * LANES].T
        for k in range(2):
            columns[k, r] = jnp.broadcast_to(column[:, k : k + 1], (LANES, LANES))


def ring_slot(stage, unit):
    return stage.at[unit % RING]


def group(size, list_smem, where_scr, vec_scr, columns, entry, total, keep):
    r, start = entry // LANES, entry % LANES
    x_col, y_col = columns[0, r], columns[1, r]
    for j in range(size):
        c = list_smem[r, start + j]
        high, low = block(x_col, y_col, where_scr[c, 0:1, :], where_scr[c, 1:2, :])
        total = multiply(total, high, low, vec_scr[c])
        keep.append((high, low))
    return total


def add_rows(sums, entry, total):
    r = entry // LANES
    sums[r] = sums[r] + (total[0:8] + total[8:16])


def put_rows(out_ref, sums):
    for r in range(sums.shape[0]):
        out_ref[:, r * LANES : (r + 1) * LANES] = sums[r]


def product(size, list_smem, flat, where_scr, vec_scr, columns, sums, cache_ref, stage, sems):
    room = cache_ref.shape[0] - 1
    blank = jnp.zeros((16, LANES), f32)
    sums[...] = jnp.zeros_like(sums)
    whole, units = flatten(size, list_smem, flat, sums.shape[0])
    groups = UNIT // size

    def save(unit):
        return pltpu.make_async_copy(
            ring_slot(stage, unit), cache_ref.at[jnp.minimum(unit, room)], sems.at[unit % RING]
        )

    def one_unit(unit, count):
        pl.when(unit >= RING)(lambda: save(unit - RING).wait())
        slot = unit % RING
        entries = [flat[unit * groups + g] for g in range(count)]
        kept, totals = [], []
        for entry in entries:
            totals.append(group(size, list_smem, where_scr, vec_scr, columns, entry, blank, kept))
        for k, (high, low) in enumerate(kept):
            stage[slot, 2 * k] = high
            stage[slot, 2 * k + 1] = low
        for entry, total in zip(entries, totals):
            add_rows(sums, entry, total)
        save(unit).start()
    def loop(unit, _):
        one_unit(unit, groups)
        return 0

    lax.fori_loop(0, whole, loop, 0)
    pl.when(units > whole)(lambda: one_unit(whole, groups // 2))
    for k in range(RING):
        last = units - 1 - (units - 1 - k) % RING
        pl.when(units > k)(lambda last=last: save(last).wait())


def product_again(size, list_smem, flat, where_scr, vec_scr, columns, sums, cache_ref, stage, sems, load):
    room = cache_ref.shape[0] - 1
    blank = jnp.zeros((16, LANES), f32)
    sums[...] = jnp.zeros_like(sums)
    whole, units = flatten(size, list_smem, flat, sums.shape[0])
    groups = UNIT // size
    ready = jnp.minimum(units, room)

    def fetch(unit):
        return pltpu.make_async_copy(cache_ref.at[unit], ring_slot(stage, unit), sems.at[unit % RING])

    for k in range(RING):
        pl.when(k < ready)(lambda k=k: fetch(k).start())
    load(units > ready)

    def one_unit(unit, count):
        fetch(unit).wait()
        slot = unit % RING
        entries = [flat[unit * groups + g] for g in range(count)]
        totals = []
        for g, entry in enumerate(entries):
            r, start = entry // LANES, entry % LANES
            total = blank
            for j in range(size):
                k = g * size + j
                vec = vec_scr[list_smem[r, start + j]]
                total = multiply(total, stage[slot, 2 * k], stage[slot, 2 * k + 1], vec)
            totals.append(total)
        for entry, total in zip(entries, totals):
            add_rows(sums, entry, total)
        pl.when(unit + RING < ready)(lambda: fetch(unit + RING).start())
    def loop(unit, _):
        one_unit(unit, groups)
        return 0

    lax.fori_loop(0, jnp.minimum(whole, ready), loop, 0)
    pl.when((units > whole) & (units == ready))(lambda: one_unit(whole, groups // 2))

    def fresh(number, _):
        entry = flat[number]
        add_rows(sums, entry, group(size, list_smem, where_scr, vec_scr, columns, entry, blank, []))
        return 0

    lax.fori_loop(ready * groups, units * groups, fresh, 0)


def first_sums(size, hops, tile_ref, own_share, shares, list_ref, cache_ref, scratch):
    list_smem, sem, flat, where_scr, vec_scr, columns, sums, stage, sems = scratch
    make_list(hops, tile_ref, own_share, shares, list_ref)
    copy = pltpu.make_async_copy(list_ref, list_smem, sem)
    copy.start()
    load_where(shares, where_scr)
    load_vectors(shares, vec_scr)
    own_columns(own_share, columns)
    copy.wait()
    product(size, list_smem, flat, where_scr, vec_scr, columns, sums, cache_ref, stage, sems)
    return sums


def second_sums(size, list_smem, own_share, shares, vectors, cache_ref, scratch):
    flat, where_scr, vec_scr, columns, sums, stage, sems = scratch

    def load(needed):
        load_vectors(vectors, vec_scr)

        @pl.when(needed)
        def _():
            load_where(shares, where_scr)
            own_columns(own_share, columns)

    product_again(size, list_smem, flat, where_scr, vec_scr, columns, sums, cache_ref, stage, sems, load)
    return sums


def first_inner_kernel(tile_ref, own_share, out_ref, list_ref, cache_ref, *scratch):
    put_rows(out_ref, first_sums(INNER_GROUP, [0], tile_ref, own_share, [own_share], list_ref, cache_ref, scratch))


def first_outer_kernel(hops, tile_ref, own_ref, inner_ref, own_share, *refs):
    n = len(hops)
    shares = refs[:n]
    image_ref, share_ref, list_ref, cache_ref = refs[n : n + 4]
    put_rows(image_ref, first_sums(OUTER_GROUP, hops, tile_ref, own_share, shares, list_ref, cache_ref, refs[n + 4 :]))
    field = own_ref[4:12, :]
    image = own_ref[3:4, :] * field + own_ref[2:3, :] * (inner_ref[...] + image_ref[...])
    image_ref[...] = image
    share_ref[...] = image * (own_ref[2:3, :] * (1.0 / 256.0))


def second_inner_kernel(list_smem, own_share, vector, cache_ref, out_ref, *scratch):
    put_rows(out_ref, second_sums(INNER_GROUP, list_smem, own_share, [own_share], [vector], cache_ref, scratch))


def two_sum(a, b):
    total = a + b
    back = total - a
    return total, (a - (total - back)) + (b - back)


def halves(a):
    scaled = a * 4097.0
    high = scaled - (scaled - a)
    return high, a - high


def two_product(a, b):
    total = a * b
    (a_high, a_low), (b_high, b_low) = halves(a), halves(b)
    error = ((a_high * b_high - total) + a_high * b_low + a_low * b_high) + a_low * b_low
    return total, error


def pair_sum(a, b):
    total, rest = two_sum(a[0], b[0])
    rest = rest + (a[1] + b[1])
    high = total + rest
    return high, rest - (high - total)


def pair_product(a, b):
    total, rest = two_product(a[0], b[0])
    rest = rest + (a[0] * b[1] + a[1] * b[0])
    high = total + rest
    return high, rest - (high - total)


def lane_sums(left, right):
    total = (jnp.zeros((8, LANES), f32), jnp.zeros((8, LANES), f32))
    for c in range(left.shape[1] // LANES):
        lanes = slice(c * LANES, (c + 1) * LANES)
        value, error = two_sum(total[0], left[:, lanes] * right[:, lanes])
        total = (value, total[1] + error)
    shift = LANES // 2
    while shift:
        total = pair_sum(total, tuple(pltpu.roll(part, shift, 1) for part in total))
        shift //= 2
    return total


def second_outer_kernel(n, list_smem, own_ref, image_ref, inner_ref, cache_ref, own_share, *refs):
    shares, vectors, twice_ref, dots_ref = refs[:n], refs[n : 2 * n], refs[2 * n], refs[2 * n + 1]
    put_rows(twice_ref, second_sums(OUTER_GROUP, list_smem, own_share, shares, vectors, cache_ref, refs[2 * n + 2 :]))
    image = image_ref[...]
    twice = own_ref[3:4, :] * image + own_ref[2:3, :] * (inner_ref[...] + twice_ref[...])
    twice_ref[...] = twice
    field = own_ref[4:12, :]
    lane = iota((8, LANES), 1)
    dots = jnp.zeros((8, LANES), f32)
    pairs = ((field, field), (field, image), (image, image), (field, twice), (image, twice))
    for k, (left, right) in enumerate(pairs):
        value, rest = lane_sums(left, right)
        dots = jnp.where(lane == 2 * k, value, jnp.where(lane == 2 * k + 1, rest, dots))
    dots_ref[...] = jnp.broadcast_to(dots[None], dots_ref.shape)


def place_kernel(own_ref, image_ref, twice_ref, dots_ref, field_out, residual_out, inv_chunk, inv_lane, data_scr):
    chunks = own_ref.shape[1] // LANES

    def held(t):
        part = dots_ref[t]
        return part, pltpu.roll(part, LANES - 1, 1)

    sums = held(0)
    for t in range(1, dots_ref.shape[0]):
        sums = pair_sum(sums, held(t))
    pp, pq, qq, pz, qz = [tuple(part[:, 2 * k : 2 * k + 1] for part in sums) for k in range(5)]
    alpha = pp[0] / pq[0]
    zero = jnp.zeros_like(alpha)
    first = (alpha, zero)
    minus = (-alpha, zero)
    square = pair_product(first, first)
    norm = pair_sum(pair_sum(pp, pair_product((-2.0 * alpha, zero), pq)), pair_product(square, qq))
    beta = norm[0] / pp[0]
    grown = two_sum(jnp.ones_like(beta), beta)
    power = pair_sum(
        pair_product(grown, pair_sum(pair_product(grown, pq), pair_product(minus, pair_sum(qq, pz)))),
        pair_product(square, qz),
    )
    alpha_next = norm[0] / power[0]
    field, image = own_ref[4:12, :], image_ref[...]
    residual = field - alpha * image
    data_scr[0:8, :] = alpha * field + alpha_next * (residual + beta * field)
    data_scr[8:16, :] = residual - alpha_next * ((image - alpha * twice_ref[...]) + beta * image)
    places = [own_ref[12:13, c * LANES : (c + 1) * LANES].astype(i32) - 1 for c in range(chunks)]
    chunk, lane, _ = invert(places, chunks)
    inv_chunk[...] = chunk
    inv_lane[...] = lane
    for d in range(chunks):
        value = pick(
            lambda s: data_scr[:, s * LANES : (s + 1) * LANES],
            chunks,
            inv_chunk[d : d + 1, :],
            inv_lane[d : d + 1, :],
            inv_lane[d : d + 1, :] >= 0,
        )
        field_out[:, d * LANES : (d + 1) * LANES] = value[0:8]
        residual_out[:, d * LANES : (d + 1) * LANES] = value[8:16]


def call(kernel, outs, ins, scratch=(), limit=LIMIT, cost=None):
    return pl.pallas_call(
        kernel,
        out_shape=[jax.ShapeDtypeStruct(shape, kind) for shape, kind in outs],
        in_specs=ins,
        out_specs=[VMEM if len(shape) < 3 or kind != bf16 else HBM for shape, kind in outs],
        scratch_shapes=list(scratch),
        compiler_params=pltpu.CompilerParams(vmem_limit_bytes=limit),
        cost_estimate=cost,
    )


def cost(parts):
    return pl.CostEstimate(flops=parts * 2 * 10**9, bytes_accessed=parts * 10**7, transcendentals=0)


def around(value, hops, tiles):
    return [lax.ppermute(value, "tiles", [(i, (i - hop) % tiles) for i in range(tiles)]) for hop in hops]


def local(obs_position, obs_sd, obs_var, innovations, obs_target, pair_table, pair_count):
    tiles = lax.axis_size("tiles")
    my_tile = lax.axis_index("tiles").astype(i32)
    rows = obs_sd.shape[0]
    chunks = rows // LANES
    hops = [sign * hop for hop in range(1, pair_table.shape[1]) for sign in (1, -1)]
    n = len(hops)
    capacity = 3 * rows // (2 * tiles)
    width = -(-capacity // LANES) * LANES
    boxes = tiles * width // LANES
    folded = capacity > LANES and 0 < capacity % LANES <= LANES // 2 and tiles % 2 == 0
    depth = width // LANES * FIELDS - (FIELDS // 2 if folded else 0)
    arrivals = tiles * (depth // FIELDS) + (tiles // 2 if folded else 0)

    (outbox,) = call(
        functools.partial(outbox_kernel, tiles, width),
        [((tiles, depth, LANES), f32)],
        [HBM] * 5,
        [
            pltpu.VMEM((FIELDS, rows), f32),
            pltpu.VMEM((2, rows), f32),
            pltpu.VMEM((1, rows), f32),
            pltpu.VMEM((1, rows), f32),
            pltpu.VMEM((8, rows), f32),
            pltpu.VMEM((1, rows), i32),
        ]
        + [pltpu.VMEM((boxes, LANES), i32)] * 3
        + [pltpu.SemaphoreType.DMA((5,))],
        64 * 2**20 - 2**16,
    )(obs_position, obs_sd[None], obs_var[None], innovations, obs_target[None])
    inbox = lax.all_to_all(outbox, "tiles", split_axis=0, concat_axis=0, tiled=True)
    share, own = call(
        sort_kernel,
        [((FIELDS, rows), f32), ((FIELDS, rows), f32)],
        [VMEM, SMEM],
        [pltpu.VMEM((chunks, LANES), i32)] * 2 + [pltpu.VMEM((arrivals, BINS, LANES), f32)],
    )(inbox, pair_count)
    shares = around(share, hops, tiles)
    tile = my_tile[None]

    def operands(held, size):
        return [
            pltpu.SMEM((held * chunks // size + UNIT,), i32),
            pltpu.VMEM((held + 1, 8, LANES), f32),
            pltpu.VMEM((held + 1, 16, LANES), bf16),
            pltpu.VMEM((2, chunks, LANES, LANES), f32),
            pltpu.VMEM((chunks, 8, LANES), f32),
            pltpu.VMEM((RING, 2 * UNIT, LANES, LANES), bf16),
            pltpu.SemaphoreType.DMA((RING,)),
        ]

    def kept(held, most):
        units = min(most, -(-held * chunks // UNIT))
        return (units + 1, 2 * UNIT, LANES, LANES)

    listing = [pltpu.SMEM((chunks, LANES), i32), pltpu.SemaphoreType.DMA]
    field_kind = ((8, rows), f32)
    list_kind = ((chunks, LANES), i32)
    held = n * chunks
    inner, near, near_cache = call(
        first_inner_kernel,
        [field_kind, list_kind, (kept(chunks, INNER), bf16)],
        [SMEM, VMEM],
        listing + operands(chunks, INNER_GROUP),
        cost=cost(1),
    )(tile, share)
    image, image_share, far, far_cache = call(
        functools.partial(first_outer_kernel, hops),
        [field_kind, field_kind, list_kind, (kept(held, OUTER), bf16)],
        [SMEM] + [VMEM] * (n + 3),
        listing + operands(held, OUTER_GROUP),
        cost=cost(4),
    )(tile, own, inner, share, *shares)
    vectors = around(image_share, hops, tiles)
    (inner_again,) = call(
        second_inner_kernel,
        [field_kind],
        [SMEM, VMEM, VMEM, HBM],
        operands(chunks, INNER_GROUP),
        cost=cost(1),
    )(near, share, image_share, near_cache)
    twice, dots = call(
        functools.partial(second_outer_kernel, n),
        [field_kind, ((tiles, 8, LANES), f32)],
        [SMEM] + [VMEM] * 3 + [HBM] + [VMEM] * (2 * n + 1),
        operands(held, OUTER_GROUP),
        cost=cost(3),
    )(far, own, image, inner_again, far_cache, share, *shares, *vectors)
    dots = lax.all_to_all(dots, "tiles", split_axis=0, concat_axis=0, tiled=True)
    return tuple(
        call(
            place_kernel,
            [field_kind] * 2,
            [VMEM] * 4,
            [pltpu.VMEM((chunks, LANES), i32)] * 2 + [pltpu.VMEM((16, rows), f32)],
        )(own, image, twice, dots)
    )


def solution(mesh):
    both = ("groups", "tiles")
    placed = (P(None, both), P(both), P(both), P(None, both), P(both), P(both, None, None), P(both))
    return jax.shard_map(
        local,
        mesh=mesh,
        in_specs=placed,
        out_specs=(P(None, both), P(None, both)),
        check_vma=False,
    )
```

```python
import functools

import jax
import jax.numpy as jnp
from jax import lax
from jax.experimental import pallas as pl
from jax.experimental.pallas import tpu as pltpu
from jax.sharding import PartitionSpec as P

f32, bf16, i32 = jnp.float32, jnp.bfloat16, jnp.int32
LANES = 128
FIELDS = 16
BINS = 128
INNER_GROUP = 2
OUTER_GROUP = 4
UNIT = 32
RING = 4
SPAN = 16
INNER = 8
OUTER = 18
TRANSPOSED = (((1,), (1,)), ((), ()))
VMEM = pl.BlockSpec(memory_space=pltpu.VMEM)
SMEM = pl.BlockSpec(memory_space=pltpu.SMEM)
HBM = pl.BlockSpec(memory_space=pltpu.HBM)
LIMIT = 40 * 2**20


def iota(shape, axis):
    return lax.broadcasted_iota(i32, shape, axis)


def running_sum_weights():
    shape = (LANES, 2 * LANES)
    row, col = iota(shape, 0), iota(shape, 1)
    return jnp.where((row <= col) | (col >= LANES), 1.0, 0.0).astype(bf16)


def dot(a, b):
    return jnp.dot(a, b, preferred_element_type=f32)


def dot_t(a, b):
    return lax.dot_general(a, b, TRANSPOSED, preferred_element_type=f32)


def invert(places, count):
    chunk_rows, lane_rows, here_rows, low_rows = [], [], [], []
    for chunk, place in enumerate(places):
        high = jnp.right_shift(place, 7)
        here = jnp.where(high == iota((count, LANES), 0), 1.0, 0.0)
        here_rows.append(here.astype(bf16))
        chunk_rows.append((here * float(chunk)).astype(bf16))
        lane_rows.append((here * iota((count, LANES), 1).astype(f32)).astype(bf16))
        low = jnp.bitwise_and(place, LANES - 1)
        low_rows.append(jnp.where(low == iota((LANES, LANES), 0), 1.0, 0.0).astype(bf16))
    left = jnp.concatenate(
        [jnp.concatenate(rows, axis=1) for rows in (chunk_rows, lane_rows, here_rows)], axis=0
    )
    found = dot_t(left, jnp.concatenate(low_rows, axis=1))
    chunk = found[:count].astype(i32)
    lane = found[count : 2 * count].astype(i32)
    return chunk, lane, found[2 * count :] > 0.5


def pick(load, sources, chunk, lane, here):
    total = None
    for source in range(sources):
        value = load(source)
        index = jnp.broadcast_to(lane, value.shape)
        value = jnp.take_along_axis(value, index, axis=1)
        total = value if total is None else jnp.where(chunk == source, value, total)
    return jnp.where(here, total, 0.0)


def outbox_kernel(
    tiles,
    width,
    pos_ref,
    sd_ref,
    var_ref,
    innov_ref,
    target_ref,
    out_ref,
    fields,
    pos_scr,
    sd_scr,
    var_scr,
    innov_scr,
    target_scr,
    inv_chunk,
    inv_lane,
    inv_here,
    sems,
):
    rows = pos_ref.shape[1]
    chunks = rows // LANES
    copies = [
        pltpu.make_async_copy(source, target, sems.at[k])
        for k, (source, target) in enumerate(
            (
                (target_ref, target_scr),
                (pos_ref, pos_scr),
                (sd_ref, sd_scr),
                (var_ref, var_scr),
                (innov_ref, innov_scr),
            )
        )
    ]
    for copy in copies:
        copy.start()
    fields[...] = jnp.zeros_like(fields)
    for copy in copies:
        copy.wait()
    fields[0:2, :] = pos_scr[...]
    fields[2:3, :] = sd_scr[...]
    fields[3:4, :] = var_scr[...]
    target = target_scr[...]
    owner = target // rows
    fields[12:13, :] = (target - owner * rows + 1).astype(f32)
    fields[4:12, :] = innov_scr[...]
    mine = [
        jnp.where(owner[:, c * LANES : (c + 1) * LANES] == iota((tiles, LANES), 0), 1.0, 0.0)
        for c in range(chunks)
    ]
    sums = dot(jnp.concatenate([m.astype(bf16) for m in mine], axis=0), running_sum_weights())
    before = (iota((tiles, LANES), 0) * width - 1).astype(f32)
    places = []
    for c in range(chunks):
        part = sums[c * tiles : (c + 1) * tiles]
        place = jnp.sum(mine[c] * (part[:, :LANES] + before), axis=0, keepdims=True)
        places.append(place.astype(i32))
        before = before + part[:, LANES:]
    count = tiles * width // LANES
    chunk, lane, here = invert(places, count)
    inv_chunk[...] = chunk
    inv_lane[...] = lane
    inv_here[...] = jnp.where(here, 1, 0)
    per_tile = width // LANES
    for d in range(count):
        value = pick(
            lambda s: fields[:, s * LANES : (s + 1) * LANES],
            chunks,
            inv_chunk[d : d + 1, :],
            inv_lane[d : d + 1, :],
            inv_here[d : d + 1, :] > 0,
        )
        first = d % per_tile * FIELDS
        if first + FIELDS <= out_ref.shape[1]:
            out_ref[d // per_tile, first : first + FIELDS, :] = value
        else:
            left = iota((FIELDS // 2, LANES), 1) < LANES // 2
            other = pltpu.roll(value[FIELDS // 2 :], LANES // 2, 1)
            out_ref[d // per_tile, first:, :] = jnp.where(left, value[: FIELDS // 2], other)


def sort_kernel(in_ref, count_ref, share_ref, own_ref, inv_chunk, inv_lane, rank_scr):
    tiles, depth, _ = in_ref.shape
    rows = own_ref.shape[1]
    chunks = rows // LANES
    whole = depth // FIELDS
    half = depth % FIELDS
    sources = tiles * whole + (tiles // 2 if half else 0)

    def load(s):
        if s < tiles * whole:
            first = s % whole * FIELDS
            return in_ref[s // whole, first : first + FIELDS, :]
        pair = 2 * (s - tiles * whole)
        one, two = in_ref[pair, whole * FIELDS :, :], in_ref[pair + 1, whole * FIELDS :, :]
        left = iota((half, LANES), 1) < LANES // 2
        return jnp.concatenate(
            [
                jnp.where(left, one, pltpu.roll(two, LANES // 2, 1)),
                jnp.where(left, pltpu.roll(one, LANES // 2, 1), two),
            ],
            axis=0,
        )

    weights = running_sum_weights()
    before = jnp.full((BINS, LANES), -1.0, f32)
    for s in range(sources):
        data = load(s)
        bins = jnp.clip((data[1:2] * (BINS / 8.0)).astype(i32), 0, BINS - 1)
        bins = jnp.where(data[12:13] > 0.5, bins, -1)
        member = jnp.where(bins == iota((BINS, LANES), 0), 1.0, 0.0)
        part = dot(member.astype(bf16), weights)
        rank_scr[s] = member * (part[:, :LANES] + before)
        before = before + part[:, LANES:]
    totals = before + 1.0
    high = jnp.floor(totals * (1.0 / 64.0))
    low = totals - 64.0 * high
    earlier = jnp.where(iota((BINS, BINS), 1) < iota((BINS, BINS), 0), 1.0, 0.0).astype(bf16)
    base = 64.0 * dot(earlier, high.astype(bf16)) + dot(earlier, low.astype(bf16))
    places = []
    for s in range(sources):
        data = load(s)
        bins = jnp.clip((data[1:2] * (BINS / 8.0)).astype(i32), 0, BINS - 1)
        here = data[12:13] > 0.5
        member = jnp.where(bins == iota((BINS, LANES), 0), base, 0.0)
        place = jnp.sum(member + rank_scr[s], axis=0, keepdims=True).astype(i32)
        places.append(jnp.where(here, place, -1))
    chunk, lane, here = invert(places, chunks)
    inv_chunk[...] = chunk
    inv_lane[...] = lane
    for d in range(chunks):
        own_ref[:, d * LANES : (d + 1) * LANES] = pick(
            load, sources, inv_chunk[d : d + 1, :], inv_lane[d : d + 1, :], inv_lane[d : d + 1, :] >= 0
        )
    share_ref[...] = jnp.zeros_like(share_ref)
    share_ref[0:8, :] = own_ref[4:12, :] * (own_ref[2:3, :] * (1.0 / 256.0))
    share_ref[8:10, :] = own_ref[0:2, :] * 4.0
    stat = jnp.zeros((1, LANES), f32)
    for axis in range(2):
        wide = jnp.concatenate(
            [share_ref[8 + axis : 9 + axis, c * LANES : (c + 1) * LANES] for c in range(chunks)], axis=0
        )
        for which, value in ((0, jnp.min(wide, axis=1, keepdims=True)), (1, jnp.max(wide, axis=1, keepdims=True))):
            lanes = iota((chunks, LANES), 1) - chunks * (2 * axis + which)
            stat = stat + jnp.sum(
                jnp.where(lanes == iota((chunks, LANES), 0), value, 0.0), axis=0, keepdims=True
            )
    stat = jnp.where(iota((1, LANES), 1) == 4 * chunks, count_ref[0].astype(f32), stat)
    share_ref[10:11, 0:LANES] = stat


def make_list(hops, tile_ref, own_share, shares, list_ref):
    chunks = list_ref.shape[0]
    my_tile = tile_ref[0]
    own = own_share[10:11, 0:LANES]
    lane, sub = iota((chunks, LANES), 1), iota((chunks, LANES), 0)
    x_low, x_high, y_low, y_high = [
        jnp.sum(jnp.where(lane == sub + chunks * q, own, 0.0), axis=1, keepdims=True) for q in range(4)
    ]
    own_count = own[:, 4 * chunks : 4 * chunks + 1]
    need = jnp.zeros((chunks, LANES), f32)
    for nb, hop in enumerate(hops):
        other = shares[nb][10:11, 0:LANES]
        at = [pltpu.roll(other, (nb * chunks - q * chunks) % LANES, 1) for q in range(4)]
        gap_x = jnp.maximum(jnp.maximum(at[0] - x_high, x_low - at[1]), 0.0)
        gap_y = jnp.maximum(jnp.maximum(at[2] - y_high, y_low - at[3]), 0.0)
        near = gap_x * gap_x + gap_y * gap_y < 16.001
        count = own_count if hop >= 0 else other[:, 4 * chunks : 4 * chunks + 1]
        listed = (count > abs(hop) + 0.5) & (my_tile + hop >= 0)
        inside = (lane >= nb * chunks) & (lane < (nb + 1) * chunks)
        need = need + jnp.where(near & listed & inside, 1.0, 0.0)
    total = dot(need.astype(bf16), running_sum_weights())
    slot = jnp.where(need > 0.5, total[:, :LANES] - 1.0, -1.0)
    numbers = jnp.broadcast_to(iota((8, LANES), 1).astype(f32), (8, LANES)).astype(bf16)
    for r in range(chunks):
        match = jnp.where(slot[r : r + 1] == iota((LANES, LANES), 0).astype(f32), 1.0, 0.0)
        found = dot_t(numbers, match.astype(bf16))[0:1]
        amount = total[r : r + 1, LANES:]
        row = jnp.where(iota((1, LANES), 1).astype(f32) < amount, found, float(len(hops) * chunks))
        row = jnp.where(iota((1, LANES), 1) == LANES - 1, amount, row)
        list_ref[r : r + 1, :] = row.astype(i32)


def load_where(shares, where_scr):
    chunks = shares[0].shape[1] // LANES
    for nb, share in enumerate(shares):
        for c in range(chunks):
            where_scr[nb * chunks + c] = share[8:16, c * LANES : (c + 1) * LANES]
    where_scr[len(shares) * chunks] = jnp.zeros((8, LANES), f32)


def load_vectors(vectors, vec_scr):
    chunks = vectors[0].shape[1] // LANES
    for nb, vector in enumerate(vectors):
        for c in range(chunks):
            value = vector[0:8, c * LANES : (c + 1) * LANES]
            high = value.astype(bf16)
            low = (value - high.astype(f32)).astype(bf16)
            vec_scr[nb * chunks + c] = jnp.concatenate([high, low], axis=0)
    vec_scr[len(vectors) * chunks] = jnp.zeros((16, LANES), bf16)


def block(x_col, y_col, x_row, y_row):
    dx = x_col - x_row
    dy = y_col - y_row
    square = jnp.maximum(dx * dx + dy * dy, 1e-30)
    distance = square * lax.rsqrt(square)
    inside = jnp.maximum(4.0 - distance, 0.0)
    inside = inside * inside
    corr = inside * inside * (distance + 1.0)
    high = corr.astype(bf16)
    return high, (corr - high.astype(f32)).astype(bf16)


def multiply(total, high, low, vec):
    both = jnp.concatenate([high, low], axis=1)
    return total + dot_t(jnp.concatenate([vec, vec], axis=1), both)


def flatten(size, list_smem, flat, chunks):
    def chunk_rows(r, number):
        amount = (list_smem[r, LANES - 1] + (size - 1)) // size

        def four(q, _):
            for g in range(4):
                flat[number + 4 * q + g] = r * LANES + (4 * q + g) * size
            return 0

        lax.fori_loop(0, (amount + 3) // 4, four, 0)
        return number + amount

    number = lax.fori_loop(0, chunks, chunk_rows, 0)
    groups = UNIT // size
    for k in range(groups):
        flat[number + k] = LANES - 2 * size
    return (number + groups // 2 - 1) // groups, (number + groups - 1) // groups


def own_columns(own_share, columns):
    for r in range(columns.shape[1]):
        column = own_share[8:16, r * LANES : (r + 1) * LANES].T
        for k in range(2):
            columns[k, r] = jnp.broadcast_to(column[:, k : k + 1], (LANES, LANES))


def ring_slot(stage, unit):
    return stage.at[unit % RING]


def group(size, list_smem, where_scr, vec_scr, columns, entry, total, keep):
    r, start = entry // LANES, entry % LANES
    x_col, y_col = columns[0, r], columns[1, r]
    for j in range(size):
        c = list_smem[r, start + j]
        high, low = block(x_col, y_col, where_scr[c, 0:1, :], where_scr[c, 1:2, :])
        total = multiply(total, high, low, vec_scr[c])
        keep.append((high, low))
    return total


def add_rows(sums, entry, total):
    r = entry // LANES
    sums[r] = sums[r] + (total[0:8] + total[8:16])


def put_rows(out_ref, sums):
    for r in range(sums.shape[0]):
        out_ref[:, r * LANES : (r + 1) * LANES] = sums[r]


def product(size, list_smem, flat, where_scr, vec_scr, columns, sums, cache_ref, stage, sems):
    room = cache_ref.shape[0] - 1
    blank = jnp.zeros((16, LANES), f32)
    sums[...] = jnp.zeros_like(sums)
    whole, units = flatten(size, list_smem, flat, sums.shape[0])
    groups = UNIT // size

    def save(unit):
        return pltpu.make_async_copy(
            ring_slot(stage, unit), cache_ref.at[jnp.minimum(unit, room)], sems.at[unit % RING]
        )

    def one_unit(unit, count):
        pl.when(unit >= RING)(lambda: save(unit - RING).wait())
        slot = unit % RING
        entries = [flat[unit * groups + g] for g in range(count)]
        kept, totals = [], []
        for entry in entries:
            totals.append(group(size, list_smem, where_scr, vec_scr, columns, entry, blank, kept))
        for k, (high, low) in enumerate(kept):
            stage[slot, 2 * k] = high
            stage[slot, 2 * k + 1] = low
        for entry, total in zip(entries, totals):
            add_rows(sums, entry, total)
        save(unit).start()
    def loop(unit, _):
        one_unit(unit, groups)
        return 0

    lax.fori_loop(0, whole, loop, 0)
    pl.when(units > whole)(lambda: one_unit(whole, groups // 2))
    for k in range(RING):
        last = units - 1 - (units - 1 - k) % RING
        pl.when(units > k)(lambda last=last: save(last).wait())


def product_again(size, list_smem, flat, where_scr, vec_scr, columns, sums, cache_ref, stage, sems, load):
    room = cache_ref.shape[0] - 1
    blank = jnp.zeros((16, LANES), f32)
    sums[...] = jnp.zeros_like(sums)
    whole, units = flatten(size, list_smem, flat, sums.shape[0])
    groups = UNIT // size
    ready = jnp.minimum(units, room)

    def fetch(unit):
        return pltpu.make_async_copy(cache_ref.at[unit], ring_slot(stage, unit), sems.at[unit % RING])

    for k in range(RING):
        pl.when(k < ready)(lambda k=k: fetch(k).start())
    load(units > ready)

    def one_unit(unit, count):
        fetch(unit).wait()
        slot = unit % RING
        entries = [flat[unit * groups + g] for g in range(count)]
        totals = []
        for g, entry in enumerate(entries):
            r, start = entry // LANES, entry % LANES
            total = blank
            for j in range(size):
                k = g * size + j
                vec = vec_scr[list_smem[r, start + j]]
                total = multiply(total, stage[slot, 2 * k], stage[slot, 2 * k + 1], vec)
            totals.append(total)
        for entry, total in zip(entries, totals):
            add_rows(sums, entry, total)
        pl.when(unit + RING < ready)(lambda: fetch(unit + RING).start())
    def loop(unit, _):
        one_unit(unit, groups)
        return 0

    lax.fori_loop(0, jnp.minimum(whole, ready), loop, 0)
    pl.when((units > whole) & (units == ready))(lambda: one_unit(whole, groups // 2))

    def fresh(number, _):
        entry = flat[number]
        add_rows(sums, entry, group(size, list_smem, where_scr, vec_scr, columns, entry, blank, []))
        return 0

    lax.fori_loop(ready * groups, units * groups, fresh, 0)


def first_sums(size, hops, tile_ref, own_share, shares, list_ref, cache_ref, scratch):
    list_smem, sem, flat, where_scr, vec_scr, columns, sums, stage, sems = scratch
    make_list(hops, tile_ref, own_share, shares, list_ref)
    copy = pltpu.make_async_copy(list_ref, list_smem, sem)
    copy.start()
    load_where(shares, where_scr)
    load_vectors(shares, vec_scr)
    own_columns(own_share, columns)
    copy.wait()
    product(size, list_smem, flat, where_scr, vec_scr, columns, sums, cache_ref, stage, sems)
    return sums


def second_sums(size, list_smem, own_share, shares, vectors, cache_ref, scratch):
    flat, where_scr, vec_scr, columns, sums, stage, sems = scratch

    def load(needed):
        load_vectors(vectors, vec_scr)

        @pl.when(needed)
        def _():
            load_where(shares, where_scr)
            own_columns(own_share, columns)

    product_again(size, list_smem, flat, where_scr, vec_scr, columns, sums, cache_ref, stage, sems, load)
    return sums


def first_inner_kernel(tile_ref, own_share, out_ref, list_ref, cache_ref, *scratch):
    put_rows(out_ref, first_sums(INNER_GROUP, [0], tile_ref, own_share, [own_share], list_ref, cache_ref, scratch))


def first_outer_kernel(hops, tile_ref, own_ref, inner_ref, own_share, *refs):
    n = len(hops)
    shares = refs[:n]
    image_ref, share_ref, list_ref, cache_ref = refs[n : n + 4]
    put_rows(image_ref, first_sums(OUTER_GROUP, hops, tile_ref, own_share, shares, list_ref, cache_ref, refs[n + 4 :]))
    field = own_ref[4:12, :]
    image = own_ref[3:4, :] * field + own_ref[2:3, :] * (inner_ref[...] + image_ref[...])
    image_ref[...] = image
    share_ref[...] = image * (own_ref[2:3, :] * (1.0 / 256.0))


def second_inner_kernel(list_smem, own_share, vector, cache_ref, out_ref, *scratch):
    put_rows(out_ref, second_sums(INNER_GROUP, list_smem, own_share, [own_share], [vector], cache_ref, scratch))


def two_sum(a, b):
    total = a + b
    back = total - a
    return total, (a - (total - back)) + (b - back)


def halves(a):
    scaled = a * 4097.0
    high = scaled - (scaled - a)
    return high, a - high


def two_product(a, b):
    total = a * b
    (a_high, a_low), (b_high, b_low) = halves(a), halves(b)
    error = ((a_high * b_high - total) + a_high * b_low + a_low * b_high) + a_low * b_low
    return total, error


def pair_sum(a, b):
    total, rest = two_sum(a[0], b[0])
    rest = rest + (a[1] + b[1])
    high = total + rest
    return high, rest - (high - total)


def pair_product(a, b):
    total, rest = two_product(a[0], b[0])
    rest = rest + (a[0] * b[1] + a[1] * b[0])
    high = total + rest
    return high, rest - (high - total)


def lane_sums(left, right):
    total = (jnp.zeros((8, LANES), f32), jnp.zeros((8, LANES), f32))
    for c in range(left.shape[1] // LANES):
        lanes = slice(c * LANES, (c + 1) * LANES)
        value, error = two_sum(total[0], left[:, lanes] * right[:, lanes])
        total = (value, total[1] + error)
    shift = LANES // 2
    while shift:
        total = pair_sum(total, tuple(pltpu.roll(part, shift, 1) for part in total))
        shift //= 2
    return total


def second_outer_kernel(n, list_smem, own_ref, image_ref, inner_ref, cache_ref, own_share, *refs):
    shares, vectors, twice_ref, dots_ref = refs[:n], refs[n : 2 * n], refs[2 * n], refs[2 * n + 1]
    put_rows(twice_ref, second_sums(OUTER_GROUP, list_smem, own_share, shares, vectors, cache_ref, refs[2 * n + 2 :]))
    image = image_ref[...]
    twice = own_ref[3:4, :] * image + own_ref[2:3, :] * (inner_ref[...] + twice_ref[...])
    twice_ref[...] = twice
    field = own_ref[4:12, :]
    lane = iota((8, LANES), 1)
    dots = jnp.zeros((8, LANES), f32)
    pairs = ((field, field), (field, image), (image, image), (field, twice), (image, twice))
    for k, (left, right) in enumerate(pairs):
        value, rest = lane_sums(left, right)
        dots = jnp.where(lane == 2 * k, value, jnp.where(lane == 2 * k + 1, rest, dots))
    row = dots[0:1]
    for r in range(1, 8):
        row = row + pltpu.roll(dots[r : r + 1], SPAN * r, 1)
    dots_ref[...] = jnp.broadcast_to(row[None], dots_ref.shape)


def place_kernel(own_ref, image_ref, twice_ref, dots_ref, field_out, residual_out, inv_chunk, inv_lane, data_scr):
    chunks = own_ref.shape[1] // LANES

    def held(t):
        part = dots_ref[t]
        return part, pltpu.roll(part, LANES - 1, 1)

    sums = held(0)
    for t in range(1, dots_ref.shape[0]):
        sums = pair_sum(sums, held(t))
    sums = [
        jnp.concatenate([part] + [pltpu.roll(part, LANES - SPAN * r, 1) for r in range(1, 8)], axis=0)
        for part in sums
    ]
    pp, pq, qq, pz, qz = [tuple(part[:, 2 * k : 2 * k + 1] for part in sums) for k in range(5)]
    alpha = pp[0] / pq[0]
    zero = jnp.zeros_like(alpha)
    first = (alpha, zero)
    minus = (-alpha, zero)
    square = pair_product(first, first)
    norm = pair_sum(pair_sum(pp, pair_product((-2.0 * alpha, zero), pq)), pair_product(square, qq))
    beta = norm[0] / pp[0]
    grown = two_sum(jnp.ones_like(beta), beta)
    power = pair_sum(
        pair_product(grown, pair_sum(pair_product(grown, pq), pair_product(minus, pair_sum(qq, pz)))),
        pair_product(square, qz),
    )
    alpha_next = norm[0] / power[0]
    field, image = own_ref[4:12, :], image_ref[...]
    residual = field - alpha * image
    data_scr[0:8, :] = alpha * field + alpha_next * (residual + beta * field)
    data_scr[8:16, :] = residual - alpha_next * ((image - alpha * twice_ref[...]) + beta * image)
    places = [own_ref[12:13, c * LANES : (c + 1) * LANES].astype(i32) - 1 for c in range(chunks)]
    chunk, lane, _ = invert(places, chunks)
    inv_chunk[...] = chunk
    inv_lane[...] = lane
    for d in range(chunks):
        value = pick(
            lambda s: data_scr[:, s * LANES : (s + 1) * LANES],
            chunks,
            inv_chunk[d : d + 1, :],
            inv_lane[d : d + 1, :],
            inv_lane[d : d + 1, :] >= 0,
        )
        field_out[:, d * LANES : (d + 1) * LANES] = value[0:8]
        residual_out[:, d * LANES : (d + 1) * LANES] = value[8:16]


def call(kernel, outs, ins, scratch=(), limit=LIMIT, cost=None):
    return pl.pallas_call(
        kernel,
        out_shape=[jax.ShapeDtypeStruct(shape, kind) for shape, kind in outs],
        in_specs=ins,
        out_specs=[VMEM if len(shape) < 3 or kind != bf16 else HBM for shape, kind in outs],
        scratch_shapes=list(scratch),
        compiler_params=pltpu.CompilerParams(vmem_limit_bytes=limit),
        cost_estimate=cost,
    )


def cost(parts):
    return pl.CostEstimate(flops=parts * 2 * 10**9, bytes_accessed=parts * 10**7, transcendentals=0)


def around(value, hops, tiles):
    return [lax.ppermute(value, "tiles", [(i, (i - hop) % tiles) for i in range(tiles)]) for hop in hops]


def local(obs_position, obs_sd, obs_var, innovations, obs_target, pair_table, pair_count):
    tiles = lax.axis_size("tiles")
    my_tile = lax.axis_index("tiles").astype(i32)
    rows = obs_sd.shape[0]
    chunks = rows // LANES
    hops = [sign * hop for hop in range(1, pair_table.shape[1]) for sign in (1, -1)]
    n = len(hops)
    capacity = 3 * rows // (2 * tiles)
    width = -(-capacity // LANES) * LANES
    boxes = tiles * width // LANES
    folded = capacity > LANES and 0 < capacity % LANES <= LANES // 2 and tiles % 2 == 0
    depth = width // LANES * FIELDS - (FIELDS // 2 if folded else 0)
    arrivals = tiles * (depth // FIELDS) + (tiles // 2 if folded else 0)

    (outbox,) = call(
        functools.partial(outbox_kernel, tiles, width),
        [((tiles, depth, LANES), f32)],
        [HBM] * 5,
        [
            pltpu.VMEM((FIELDS, rows), f32),
            pltpu.VMEM((2, rows), f32),
            pltpu.VMEM((1, rows), f32),
            pltpu.VMEM((1, rows), f32),
            pltpu.VMEM((8, rows), f32),
            pltpu.VMEM((1, rows), i32),
        ]
        + [pltpu.VMEM((boxes, LANES), i32)] * 3
        + [pltpu.SemaphoreType.DMA((5,))],
        64 * 2**20 - 2**16,
    )(obs_position, obs_sd[None], obs_var[None], innovations, obs_target[None])
    inbox = lax.all_to_all(outbox, "tiles", split_axis=0, concat_axis=0, tiled=True)
    share, own = call(
        sort_kernel,
        [((FIELDS, rows), f32), ((FIELDS, rows), f32)],
        [VMEM, SMEM],
        [pltpu.VMEM((chunks, LANES), i32)] * 2 + [pltpu.VMEM((arrivals, BINS, LANES), f32)],
    )(inbox, pair_count)
    shares = around(share, hops, tiles)
    tile = my_tile[None]

    def operands(held, size):
        return [
            pltpu.SMEM((held * chunks // size + UNIT,), i32),
            pltpu.VMEM((held + 1, 8, LANES), f32),
            pltpu.VMEM((held + 1, 16, LANES), bf16),
            pltpu.VMEM((2, chunks, LANES, LANES), f32),
            pltpu.VMEM((chunks, 8, LANES), f32),
            pltpu.VMEM((RING, 2 * UNIT, LANES, LANES), bf16),
            pltpu.SemaphoreType.DMA((RING,)),
        ]

    def kept(held, most):
        units = min(most, -(-held * chunks // UNIT))
        return (units + 1, 2 * UNIT, LANES, LANES)

    listing = [pltpu.SMEM((chunks, LANES), i32), pltpu.SemaphoreType.DMA]
    field_kind = ((8, rows), f32)
    list_kind = ((chunks, LANES), i32)
    held = n * chunks
    inner, near, near_cache = call(
        first_inner_kernel,
        [field_kind, list_kind, (kept(chunks, INNER), bf16)],
        [SMEM, VMEM],
        listing + operands(chunks, INNER_GROUP),
        cost=cost(1),
    )(tile, share)
    image, image_share, far, far_cache = call(
        functools.partial(first_outer_kernel, hops),
        [field_kind, field_kind, list_kind, (kept(held, OUTER), bf16)],
        [SMEM] + [VMEM] * (n + 3),
        listing + operands(held, OUTER_GROUP),
        cost=cost(4),
    )(tile, own, inner, share, *shares)
    vectors = around(image_share, hops, tiles)
    (inner_again,) = call(
        second_inner_kernel,
        [field_kind],
        [SMEM, VMEM, VMEM, HBM],
        operands(chunks, INNER_GROUP),
        cost=cost(1),
    )(near, share, image_share, near_cache)
    twice, dots = call(
        functools.partial(second_outer_kernel, n),
        [field_kind, ((tiles, 1, LANES), f32)],
        [SMEM] + [VMEM] * 3 + [HBM] + [VMEM] * (2 * n + 1),
        operands(held, OUTER_GROUP),
        cost=cost(3),
    )(far, own, image, inner_again, far_cache, share, *shares, *vectors)
    dots = lax.all_to_all(dots, "tiles", split_axis=0, concat_axis=0, tiled=True)
    return tuple(
        call(
            place_kernel,
            [field_kind] * 2,
            [VMEM] * 4,
            [pltpu.VMEM((chunks, LANES), i32)] * 2 + [pltpu.VMEM((16, rows), f32)],
        )(own, image, twice, dots)
    )


def solution(mesh):
    both = ("groups", "tiles")
    placed = (P(None, both), P(both), P(both), P(None, both), P(both), P(both, None, None), P(both))
    return jax.shard_map(
        local,
        mesh=mesh,
        in_specs=placed,
        out_specs=(P(None, both), P(None, both)),
        check_vma=False,
    )
```

```python
import functools

import jax
import jax.numpy as jnp
from jax import lax
from jax.experimental import pallas as pl
from jax.experimental.pallas import tpu as pltpu
from jax.sharding import PartitionSpec as P

f32, bf16, i32 = jnp.float32, jnp.bfloat16, jnp.int32
LANES = 128
FIELDS = 16
BINS = 128
INNER_GROUP = 2
OUTER_GROUP = 4
UNIT = 32
RING = 4
SPAN = 16
INNER = 8
OUTER = 18
TRANSPOSED = (((1,), (1,)), ((), ()))
VMEM = pl.BlockSpec(memory_space=pltpu.VMEM)
SMEM = pl.BlockSpec(memory_space=pltpu.SMEM)
HBM = pl.BlockSpec(memory_space=pltpu.HBM)
LIMIT = 40 * 2**20


def iota(shape, axis):
    return lax.broadcasted_iota(i32, shape, axis)


def running_sum_weights():
    shape = (LANES, 2 * LANES)
    row, col = iota(shape, 0), iota(shape, 1)
    return jnp.where((row <= col) | (col >= LANES), 1.0, 0.0).astype(bf16)


def dot(a, b):
    return jnp.dot(a, b, preferred_element_type=f32)


def dot_t(a, b):
    return lax.dot_general(a, b, TRANSPOSED, preferred_element_type=f32)


def invert(places, count):
    chunk_rows, lane_rows, here_rows, low_rows = [], [], [], []
    for chunk, place in enumerate(places):
        high = jnp.right_shift(place, 7)
        here = jnp.where(high == iota((count, LANES), 0), 1.0, 0.0)
        here_rows.append(here.astype(bf16))
        chunk_rows.append((here * float(chunk)).astype(bf16))
        lane_rows.append((here * iota((count, LANES), 1).astype(f32)).astype(bf16))
        low = jnp.bitwise_and(place, LANES - 1)
        low_rows.append(jnp.where(low == iota((LANES, LANES), 0), 1.0, 0.0).astype(bf16))
    left = jnp.concatenate(
        [jnp.concatenate(rows, axis=1) for rows in (chunk_rows, lane_rows, here_rows)], axis=0
    )
    found = dot_t(left, jnp.concatenate(low_rows, axis=1))
    chunk = found[:count].astype(i32)
    lane = found[count : 2 * count].astype(i32)
    return chunk, lane, found[2 * count :] > 0.5


def pick(load, sources, chunk, lane, here):
    total = None
    for source in range(sources):
        value = load(source)
        index = jnp.broadcast_to(lane, value.shape)
        value = jnp.take_along_axis(value, index, axis=1)
        total = value if total is None else jnp.where(chunk == source, value, total)
    return jnp.where(here, total, 0.0)


def outbox_kernel(
    tiles,
    width,
    pos_ref,
    sd_ref,
    var_ref,
    innov_ref,
    target_ref,
    out_ref,
    fields,
    pos_scr,
    sd_scr,
    var_scr,
    innov_scr,
    target_scr,
    inv_chunk,
    inv_lane,
    inv_here,
    sems,
):
    rows = pos_ref.shape[1]
    chunks = rows // LANES
    copies = [
        pltpu.make_async_copy(source, target, sems.at[k])
        for k, (source, target) in enumerate(
            (
                (target_ref, target_scr),
                (pos_ref, pos_scr),
                (sd_ref, sd_scr),
                (var_ref, var_scr),
                (innov_ref, innov_scr),
            )
        )
    ]
    for copy in copies:
        copy.start()
    fields[...] = jnp.zeros_like(fields)
    for copy in copies:
        copy.wait()
    fields[0:2, :] = pos_scr[...]
    fields[2:3, :] = sd_scr[...]
    fields[3:4, :] = var_scr[...]
    target = target_scr[...]
    owner = target // rows
    fields[12:13, :] = (target - owner * rows + 1).astype(f32)
    fields[4:12, :] = innov_scr[...]
    mine = [
        jnp.where(owner[:, c * LANES : (c + 1) * LANES] == iota((tiles, LANES), 0), 1.0, 0.0)
        for c in range(chunks)
    ]
    sums = dot(jnp.concatenate([m.astype(bf16) for m in mine], axis=0), running_sum_weights())
    before = (iota((tiles, LANES), 0) * width - 1).astype(f32)
    places = []
    for c in range(chunks):
        part = sums[c * tiles : (c + 1) * tiles]
        place = jnp.sum(mine[c] * (part[:, :LANES] + before), axis=0, keepdims=True)
        places.append(place.astype(i32))
        before = before + part[:, LANES:]
    count = tiles * width // LANES
    chunk, lane, here = invert(places, count)
    inv_chunk[...] = chunk
    inv_lane[...] = lane
    inv_here[...] = jnp.where(here, 1, 0)
    per_tile = width // LANES
    for d in range(count):
        value = pick(
            lambda s: fields[:, s * LANES : (s + 1) * LANES],
            chunks,
            inv_chunk[d : d + 1, :],
            inv_lane[d : d + 1, :],
            inv_here[d : d + 1, :] > 0,
        )
        first = d % per_tile * FIELDS
        if first + FIELDS <= out_ref.shape[1]:
            out_ref[d // per_tile, first : first + FIELDS, :] = value
        else:
            left = iota((FIELDS // 2, LANES), 1) < LANES // 2
            other = pltpu.roll(value[FIELDS // 2 :], LANES // 2, 1)
            out_ref[d // per_tile, first:, :] = jnp.where(left, value[: FIELDS // 2], other)


def sort_kernel(in_ref, count_ref, share_ref, own_ref, inv_chunk, inv_lane, rank_scr):
    tiles, depth, _ = in_ref.shape
    rows = own_ref.shape[1]
    chunks = rows // LANES
    whole = depth // FIELDS
    half = depth % FIELDS
    sources = tiles * whole + (tiles // 2 if half else 0)

    def load(s):
        if s < tiles * whole:
            first = s % whole * FIELDS
            return in_ref[s // whole, first : first + FIELDS, :]
        pair = 2 * (s - tiles * whole)
        one, two = in_ref[pair, whole * FIELDS :, :], in_ref[pair + 1, whole * FIELDS :, :]
        left = iota((half, LANES), 1) < LANES // 2
        return jnp.concatenate(
            [
                jnp.where(left, one, pltpu.roll(two, LANES // 2, 1)),
                jnp.where(left, pltpu.roll(one, LANES // 2, 1), two),
            ],
            axis=0,
        )

    weights = running_sum_weights()
    before = jnp.full((BINS, LANES), -1.0, f32)
    for s in range(sources):
        data = load(s)
        bins = jnp.clip((data[1:2] * (BINS / 8.0)).astype(i32), 0, BINS - 1)
        bins = jnp.where(data[12:13] > 0.5, bins, -1)
        member = jnp.where(bins == iota((BINS, LANES), 0), 1.0, 0.0)
        part = dot(member.astype(bf16), weights)
        rank_scr[s] = member * (part[:, :LANES] + before)
        before = before + part[:, LANES:]
    totals = before + 1.0
    high = jnp.floor(totals * (1.0 / 64.0))
    low = totals - 64.0 * high
    earlier = jnp.where(iota((BINS, BINS), 1) < iota((BINS, BINS), 0), 1.0, 0.0).astype(bf16)
    base = 64.0 * dot(earlier, high.astype(bf16)) + dot(earlier, low.astype(bf16))
    places = []
    for s in range(sources):
        data = load(s)
        bins = jnp.clip((data[1:2] * (BINS / 8.0)).astype(i32), 0, BINS - 1)
        here = data[12:13] > 0.5
        member = jnp.where(bins == iota((BINS, LANES), 0), base, 0.0)
        place = jnp.sum(member + rank_scr[s], axis=0, keepdims=True).astype(i32)
        places.append(jnp.where(here, place, -1))
    chunk, lane, here = invert(places, chunks)
    inv_chunk[...] = chunk
    inv_lane[...] = lane
    for d in range(chunks):
        own_ref[:, d * LANES : (d + 1) * LANES] = pick(
            load, sources, inv_chunk[d : d + 1, :], inv_lane[d : d + 1, :], inv_lane[d : d + 1, :] >= 0
        )
    share_ref[...] = jnp.zeros_like(share_ref)
    share_ref[0:8, :] = own_ref[4:12, :] * (own_ref[2:3, :] * (1.0 / 256.0))
    share_ref[8:10, :] = own_ref[0:2, :] * 4.0
    stat = jnp.zeros((1, LANES), f32)
    for axis in range(2):
        wide = jnp.concatenate(
            [share_ref[8 + axis : 9 + axis, c * LANES : (c + 1) * LANES] for c in range(chunks)], axis=0
        )
        for which, value in ((0, jnp.min(wide, axis=1, keepdims=True)), (1, jnp.max(wide, axis=1, keepdims=True))):
            lanes = iota((chunks, LANES), 1) - chunks * (2 * axis + which)
            stat = stat + jnp.sum(
                jnp.where(lanes == iota((chunks, LANES), 0), value, 0.0), axis=0, keepdims=True
            )
    stat = jnp.where(iota((1, LANES), 1) == 4 * chunks, count_ref[0].astype(f32), stat)
    share_ref[10:11, 0:LANES] = stat


def make_list(hops, tile_ref, own_share, shares, list_ref):
    chunks = list_ref.shape[0]
    my_tile = tile_ref[0]
    own = own_share[10:11, 0:LANES]
    lane, sub = iota((chunks, LANES), 1), iota((chunks, LANES), 0)
    x_low, x_high, y_low, y_high = [
        jnp.sum(jnp.where(lane == sub + chunks * q, own, 0.0), axis=1, keepdims=True) for q in range(4)
    ]
    own_count = own[:, 4 * chunks : 4 * chunks + 1]
    need = jnp.zeros((chunks, LANES), f32)
    for nb, hop in enumerate(hops):
        other = shares[nb][10:11, 0:LANES]
        at = [pltpu.roll(other, (nb * chunks - q * chunks) % LANES, 1) for q in range(4)]
        gap_x = jnp.maximum(jnp.maximum(at[0] - x_high, x_low - at[1]), 0.0)
        gap_y = jnp.maximum(jnp.maximum(at[2] - y_high, y_low - at[3]), 0.0)
        near = gap_x * gap_x + gap_y * gap_y < 16.001
        count = own_count if hop >= 0 else other[:, 4 * chunks : 4 * chunks + 1]
        listed = (count > abs(hop) + 0.5) & (my_tile + hop >= 0)
        inside = (lane >= nb * chunks) & (lane < (nb + 1) * chunks)
        need = need + jnp.where(near & listed & inside, 1.0, 0.0)
    total = dot(need.astype(bf16), running_sum_weights())
    slot = jnp.where(need > 0.5, total[:, :LANES] - 1.0, -1.0)
    numbers = jnp.broadcast_to(iota((8, LANES), 1).astype(f32), (8, LANES)).astype(bf16)
    for r in range(chunks):
        match = jnp.where(slot[r : r + 1] == iota((LANES, LANES), 0).astype(f32), 1.0, 0.0)
        found = dot_t(numbers, match.astype(bf16))[0:1]
        amount = total[r : r + 1, LANES:]
        row = jnp.where(iota((1, LANES), 1).astype(f32) < amount, found, float(len(hops) * chunks))
        row = jnp.where(iota((1, LANES), 1) == LANES - 1, amount, row)
        list_ref[r : r + 1, :] = row.astype(i32)


def load_where(shares, where_scr):
    chunks = shares[0].shape[1] // LANES
    for nb, share in enumerate(shares):
        for c in range(chunks):
            where_scr[nb * chunks + c] = share[8:16, c * LANES : (c + 1) * LANES]
    where_scr[len(shares) * chunks] = jnp.zeros((8, LANES), f32)


def load_vectors(vectors, vec_scr):
    chunks = vectors[0].shape[1] // LANES
    for nb, vector in enumerate(vectors):
        for c in range(chunks):
            value = vector[0:8, c * LANES : (c + 1) * LANES]
            high = value.astype(bf16)
            low = (value - high.astype(f32)).astype(bf16)
            vec_scr[nb * chunks + c] = jnp.concatenate([high, low], axis=0)
    vec_scr[len(vectors) * chunks] = jnp.zeros((16, LANES), bf16)


def block(x_col, y_col, x_row, y_row):
    dx = x_col - x_row
    dy = y_col - y_row
    square = jnp.maximum(dx * dx + dy * dy, 1e-30)
    distance = square * lax.rsqrt(square)
    inside = jnp.maximum(4.0 - distance, 0.0)
    inside = inside * inside
    corr = inside * inside * (distance + 1.0)
    high = corr.astype(bf16)
    return high, (corr - high.astype(f32)).astype(bf16)


def multiply(total, high, low, vec):
    both = jnp.concatenate([high, low], axis=1)
    return total + dot_t(jnp.concatenate([vec, vec], axis=1), both)


def flatten(size, list_smem, flat, chunks):
    def chunk_rows(r, number):
        amount = (list_smem[r, LANES - 1] + (size - 1)) // size

        def four(q, _):
            for g in range(4):
                flat[number + 4 * q + g] = r * LANES + (4 * q + g) * size
            return 0

        lax.fori_loop(0, (amount + 3) // 4, four, 0)
        return number + amount

    number = lax.fori_loop(0, chunks, chunk_rows, 0)
    groups = UNIT // size
    for k in range(groups):
        flat[number + k] = LANES - 2 * size
    return (number + groups // 2 - 1) // groups, (number + groups - 1) // groups


def own_columns(own_share, columns):
    for r in range(columns.shape[1]):
        column = own_share[8:16, r * LANES : (r + 1) * LANES].T
        for k in range(2):
            columns[k, r] = jnp.broadcast_to(column[:, k : k + 1], (LANES, LANES))


def ring_slot(stage, unit):
    return stage.at[unit % RING]


def group(size, list_smem, where_scr, vec_scr, columns, entry, total, keep):
    r, start = entry // LANES, entry % LANES
    x_col, y_col = columns[0, r], columns[1, r]
    for j in range(size):
        c = list_smem[r, start + j]
        high, low = block(x_col, y_col, where_scr[c, 0:1, :], where_scr[c, 1:2, :])
        total = multiply(total, high, low, vec_scr[c])
        keep.append((high, low))
    return total


def add_rows(sums, entry, total):
    r = entry // LANES
    sums[r] = sums[r] + (total[0:8] + total[8:16])


def put_rows(out_ref, sums):
    for r in range(sums.shape[0]):
        out_ref[:, r * LANES : (r + 1) * LANES] = sums[r]


def product(size, list_smem, flat, where_scr, vec_scr, columns, sums, cache_ref, stage, sems):
    room = cache_ref.shape[0] - 1
    blank = jnp.zeros((16, LANES), f32)
    sums[...] = jnp.zeros_like(sums)
    whole, units = flatten(size, list_smem, flat, sums.shape[0])
    groups = UNIT // size

    def save(unit):
        return pltpu.make_async_copy(
            ring_slot(stage, unit), cache_ref.at[jnp.minimum(unit, room)], sems.at[unit % RING]
        )

    def one_unit(unit, count):
        pl.when(unit >= RING)(lambda: save(unit - RING).wait())
        slot = unit % RING
        entries = [flat[unit * groups + g] for g in range(count)]
        kept, totals = [], []
        for entry in entries:
            totals.append(group(size, list_smem, where_scr, vec_scr, columns, entry, blank, kept))
        for k, (high, low) in enumerate(kept):
            stage[slot, 2 * k] = high
            stage[slot, 2 * k + 1] = low
        for entry, total in zip(entries, totals):
            add_rows(sums, entry, total)
        save(unit).start()
    def loop(unit, _):
        one_unit(unit, groups)
        return 0

    lax.fori_loop(0, whole, loop, 0)
    pl.when(units > whole)(lambda: one_unit(whole, groups // 2))
    for k in range(RING):
        last = units - 1 - (units - 1 - k) % RING
        pl.when(units > k)(lambda last=last: save(last).wait())


def product_again(size, list_smem, flat, where_scr, vec_scr, columns, sums, cache_ref, stage, sems, load):
    room = cache_ref.shape[0] - 1
    blank = jnp.zeros((16, LANES), f32)
    sums[...] = jnp.zeros_like(sums)
    whole, units = flatten(size, list_smem, flat, sums.shape[0])
    groups = UNIT // size
    ready = jnp.minimum(units, room)

    def fetch(unit):
        return pltpu.make_async_copy(cache_ref.at[unit], ring_slot(stage, unit), sems.at[unit % RING])

    for k in range(RING):
        pl.when(k < ready)(lambda k=k: fetch(k).start())
    load(units > ready)

    def one_unit(unit, count):
        fetch(unit).wait()
        slot = unit % RING
        entries = [flat[unit * groups + g] for g in range(count)]
        totals = []
        for g, entry in enumerate(entries):
            r, start = entry // LANES, entry % LANES
            total = blank
            for j in range(size):
                k = g * size + j
                vec = vec_scr[list_smem[r, start + j]]
                total = multiply(total, stage[slot, 2 * k], stage[slot, 2 * k + 1], vec)
            totals.append(total)
        for entry, total in zip(entries, totals):
            add_rows(sums, entry, total)
        pl.when(unit + RING < ready)(lambda: fetch(unit + RING).start())
    def loop(unit, _):
        one_unit(unit, groups)
        return 0

    lax.fori_loop(0, jnp.minimum(whole, ready), loop, 0)
    pl.when((units > whole) & (units == ready))(lambda: one_unit(whole, groups // 2))

    def fresh(number, _):
        entry = flat[number]
        add_rows(sums, entry, group(size, list_smem, where_scr, vec_scr, columns, entry, blank, []))
        return 0

    lax.fori_loop(ready * groups, units * groups, fresh, 0)


def first_sums(size, hops, tile_ref, own_share, shares, list_ref, cache_ref, scratch):
    list_smem, sem, flat, where_scr, vec_scr, columns, sums, stage, sems = scratch
    make_list(hops, tile_ref, own_share, shares, list_ref)
    copy = pltpu.make_async_copy(list_ref, list_smem, sem)
    copy.start()
    load_where(shares, where_scr)
    load_vectors(shares, vec_scr)
    own_columns(own_share, columns)
    copy.wait()
    product(size, list_smem, flat, where_scr, vec_scr, columns, sums, cache_ref, stage, sems)
    return sums


def second_sums(size, list_smem, own_share, shares, vectors, cache_ref, scratch):
    flat, where_scr, vec_scr, columns, sums, stage, sems = scratch

    def load(needed):
        load_vectors(vectors, vec_scr)

        @pl.when(needed)
        def _():
            load_where(shares, where_scr)
            own_columns(own_share, columns)

    product_again(size, list_smem, flat, where_scr, vec_scr, columns, sums, cache_ref, stage, sems, load)
    return sums


def first_inner_kernel(tile_ref, own_ref, own_share, out_ref, list_ref, inv_chunk, inv_lane, cache_ref, *scratch):
    chunks = own_ref.shape[1] // LANES
    places = [own_ref[12:13, c * LANES : (c + 1) * LANES].astype(i32) - 1 for c in range(chunks)]
    chunk, lane, _ = invert(places, chunks)
    inv_chunk[...] = chunk
    inv_lane[...] = lane
    put_rows(out_ref, first_sums(INNER_GROUP, [0], tile_ref, own_share, [own_share], list_ref, cache_ref, scratch))


def first_outer_kernel(hops, tile_ref, own_ref, inner_ref, own_share, *refs):
    n = len(hops)
    shares = refs[:n]
    image_ref, share_ref, list_ref, cache_ref = refs[n : n + 4]
    put_rows(image_ref, first_sums(OUTER_GROUP, hops, tile_ref, own_share, shares, list_ref, cache_ref, refs[n + 4 :]))
    field = own_ref[4:12, :]
    image = own_ref[3:4, :] * field + own_ref[2:3, :] * (inner_ref[...] + image_ref[...])
    image_ref[...] = image
    share_ref[...] = image * (own_ref[2:3, :] * (1.0 / 256.0))


def second_inner_kernel(list_smem, own_share, vector, cache_ref, out_ref, *scratch):
    put_rows(out_ref, second_sums(INNER_GROUP, list_smem, own_share, [own_share], [vector], cache_ref, scratch))


def two_sum(a, b):
    total = a + b
    back = total - a
    return total, (a - (total - back)) + (b - back)


def halves(a):
    scaled = a * 4097.0
    high = scaled - (scaled - a)
    return high, a - high


def two_product(a, b):
    total = a * b
    (a_high, a_low), (b_high, b_low) = halves(a), halves(b)
    error = ((a_high * b_high - total) + a_high * b_low + a_low * b_high) + a_low * b_low
    return total, error


def pair_sum(a, b):
    total, rest = two_sum(a[0], b[0])
    rest = rest + (a[1] + b[1])
    high = total + rest
    return high, rest - (high - total)


def pair_product(a, b):
    total, rest = two_product(a[0], b[0])
    rest = rest + (a[0] * b[1] + a[1] * b[0])
    high = total + rest
    return high, rest - (high - total)


def lane_sums(left, right):
    total = (jnp.zeros((8, LANES), f32), jnp.zeros((8, LANES), f32))
    for c in range(left.shape[1] // LANES):
        lanes = slice(c * LANES, (c + 1) * LANES)
        value, error = two_sum(total[0], left[:, lanes] * right[:, lanes])
        total = (value, total[1] + error)
    shift = LANES // 2
    while shift:
        total = pair_sum(total, tuple(pltpu.roll(part, shift, 1) for part in total))
        shift //= 2
    return total


def second_outer_kernel(n, list_smem, own_ref, image_ref, inner_ref, cache_ref, own_share, *refs):
    shares, vectors, twice_ref, dots_ref = refs[:n], refs[n : 2 * n], refs[2 * n], refs[2 * n + 1]
    put_rows(twice_ref, second_sums(OUTER_GROUP, list_smem, own_share, shares, vectors, cache_ref, refs[2 * n + 2 :]))
    image = image_ref[...]
    twice = own_ref[3:4, :] * image + own_ref[2:3, :] * (inner_ref[...] + twice_ref[...])
    twice_ref[...] = twice
    field = own_ref[4:12, :]
    lane = iota((8, LANES), 1)
    dots = jnp.zeros((8, LANES), f32)
    pairs = ((field, field), (field, image), (image, image), (field, twice), (image, twice))
    for k, (left, right) in enumerate(pairs):
        value, rest = lane_sums(left, right)
        dots = jnp.where(lane == 2 * k, value, jnp.where(lane == 2 * k + 1, rest, dots))
    row = dots[0:1]
    for r in range(1, 8):
        row = row + pltpu.roll(dots[r : r + 1], SPAN * r, 1)
    dots_ref[...] = jnp.broadcast_to(row[None], dots_ref.shape)


def place_kernel(own_ref, image_ref, twice_ref, dots_ref, inv_chunk, inv_lane, field_out, residual_out, data_scr):
    chunks = own_ref.shape[1] // LANES

    def held(t):
        part = dots_ref[t]
        return part, pltpu.roll(part, LANES - 1, 1)

    parts = [held(t) for t in range(dots_ref.shape[0])]
    while len(parts) > 1:
        odd = parts[len(parts) // 2 * 2 :]
        parts = [pair_sum(one, two) for one, two in zip(parts[::2], parts[1::2])] + odd
    sums = parts[0]
    sums = [
        jnp.concatenate([part] + [pltpu.roll(part, LANES - SPAN * r, 1) for r in range(1, 8)], axis=0)
        for part in sums
    ]
    pp, pq, qq, pz, qz = [tuple(part[:, 2 * k : 2 * k + 1] for part in sums) for k in range(5)]
    alpha = pp[0] / pq[0]
    zero = jnp.zeros_like(alpha)
    first = (alpha, zero)
    minus = (-alpha, zero)
    square = pair_product(first, first)
    norm = pair_sum(pair_sum(pp, pair_product((-2.0 * alpha, zero), pq)), pair_product(square, qq))
    beta = norm[0] / pp[0]
    grown = two_sum(jnp.ones_like(beta), beta)
    power = pair_sum(
        pair_product(grown, pair_sum(pair_product(grown, pq), pair_product(minus, pair_sum(qq, pz)))),
        pair_product(square, qz),
    )
    alpha_next = norm[0] / power[0]
    field, image = own_ref[4:12, :], image_ref[...]
    residual = field - alpha * image
    data_scr[0:8, :] = alpha * field + alpha_next * (residual + beta * field)
    data_scr[8:16, :] = residual - alpha_next * ((image - alpha * twice_ref[...]) + beta * image)
    for d in range(chunks):
        value = pick(
            lambda s: data_scr[:, s * LANES : (s + 1) * LANES],
            chunks,
            inv_chunk[d : d + 1, :],
            inv_lane[d : d + 1, :],
            inv_lane[d : d + 1, :] >= 0,
        )
        field_out[:, d * LANES : (d + 1) * LANES] = value[0:8]
        residual_out[:, d * LANES : (d + 1) * LANES] = value[8:16]


def call(kernel, outs, ins, scratch=(), limit=LIMIT, cost=None):
    return pl.pallas_call(
        kernel,
        out_shape=[jax.ShapeDtypeStruct(shape, kind) for shape, kind in outs],
        in_specs=ins,
        out_specs=[VMEM if len(shape) < 3 or kind != bf16 else HBM for shape, kind in outs],
        scratch_shapes=list(scratch),
        compiler_params=pltpu.CompilerParams(vmem_limit_bytes=limit),
        cost_estimate=cost,
    )


def cost(parts):
    return pl.CostEstimate(flops=parts * 2 * 10**9, bytes_accessed=parts * 10**7, transcendentals=0)


def around(value, hops, tiles):
    return [lax.ppermute(value, "tiles", [(i, (i - hop) % tiles) for i in range(tiles)]) for hop in hops]


def local(obs_position, obs_sd, obs_var, innovations, obs_target, pair_table, pair_count):
    tiles = lax.axis_size("tiles")
    my_tile = lax.axis_index("tiles").astype(i32)
    rows = obs_sd.shape[0]
    chunks = rows // LANES
    hops = [sign * hop for hop in range(1, pair_table.shape[1]) for sign in (1, -1)]
    n = len(hops)
    capacity = 3 * rows // (2 * tiles)
    width = -(-capacity // LANES) * LANES
    boxes = tiles * width // LANES
    folded = capacity > LANES and 0 < capacity % LANES <= LANES // 2 and tiles % 2 == 0
    depth = width // LANES * FIELDS - (FIELDS // 2 if folded else 0)
    arrivals = tiles * (depth // FIELDS) + (tiles // 2 if folded else 0)

    (outbox,) = call(
        functools.partial(outbox_kernel, tiles, width),
        [((tiles, depth, LANES), f32)],
        [HBM] * 5,
        [
            pltpu.VMEM((FIELDS, rows), f32),
            pltpu.VMEM((2, rows), f32),
            pltpu.VMEM((1, rows), f32),
            pltpu.VMEM((1, rows), f32),
            pltpu.VMEM((8, rows), f32),
            pltpu.VMEM((1, rows), i32),
        ]
        + [pltpu.VMEM((boxes, LANES), i32)] * 3
        + [pltpu.SemaphoreType.DMA((5,))],
        64 * 2**20 - 2**16,
    )(obs_position, obs_sd[None], obs_var[None], innovations, obs_target[None])
    inbox = lax.all_to_all(outbox, "tiles", split_axis=0, concat_axis=0, tiled=True)
    share, own = call(
        sort_kernel,
        [((FIELDS, rows), f32), ((FIELDS, rows), f32)],
        [VMEM, SMEM],
        [pltpu.VMEM((chunks, LANES), i32)] * 2 + [pltpu.VMEM((arrivals, BINS, LANES), f32)],
    )(inbox, pair_count)
    shares = around(share, hops, tiles)
    tile = my_tile[None]

    def operands(held, size):
        return [
            pltpu.SMEM((held * chunks // size + UNIT,), i32),
            pltpu.VMEM((held + 1, 8, LANES), f32),
            pltpu.VMEM((held + 1, 16, LANES), bf16),
            pltpu.VMEM((2, chunks, LANES, LANES), f32),
            pltpu.VMEM((chunks, 8, LANES), f32),
            pltpu.VMEM((RING, 2 * UNIT, LANES, LANES), bf16),
            pltpu.SemaphoreType.DMA((RING,)),
        ]

    def kept(held, most):
        units = min(most, -(-held * chunks // UNIT))
        return (units + 1, 2 * UNIT, LANES, LANES)

    listing = [pltpu.SMEM((chunks, LANES), i32), pltpu.SemaphoreType.DMA]
    field_kind = ((8, rows), f32)
    list_kind = ((chunks, LANES), i32)
    held = n * chunks
    inner, near, inv_chunk, inv_lane, near_cache = call(
        first_inner_kernel,
        [field_kind, list_kind, list_kind, list_kind, (kept(chunks, INNER), bf16)],
        [SMEM, VMEM, VMEM],
        listing + operands(chunks, INNER_GROUP),
        cost=cost(1),
    )(tile, own, share)
    image, image_share, far, far_cache = call(
        functools.partial(first_outer_kernel, hops),
        [field_kind, field_kind, list_kind, (kept(held, OUTER), bf16)],
        [SMEM] + [VMEM] * (n + 3),
        listing + operands(held, OUTER_GROUP),
        cost=cost(4),
    )(tile, own, inner, share, *shares)
    vectors = around(image_share, hops, tiles)
    (inner_again,) = call(
        second_inner_kernel,
        [field_kind],
        [SMEM, VMEM, VMEM, HBM],
        operands(chunks, INNER_GROUP),
        cost=cost(1),
    )(near, share, image_share, near_cache)
    twice, dots = call(
        functools.partial(second_outer_kernel, n),
        [field_kind, ((tiles, 1, LANES), f32)],
        [SMEM] + [VMEM] * 3 + [HBM] + [VMEM] * (2 * n + 1),
        operands(held, OUTER_GROUP),
        cost=cost(3),
    )(far, own, image, inner_again, far_cache, share, *shares, *vectors)
    dots = lax.all_to_all(dots, "tiles", split_axis=0, concat_axis=0, tiled=True)
    return tuple(
        call(
            place_kernel,
            [field_kind] * 2,
            [VMEM] * 6,
            [pltpu.VMEM((16, rows), f32)],
        )(own, image, twice, dots, inv_chunk, inv_lane)
    )


def solution(mesh):
    both = ("groups", "tiles")
    placed = (P(None, both), P(both), P(both), P(None, both), P(both), P(both, None, None), P(both))
    return jax.shard_map(
        local,
        mesh=mesh,
        in_specs=placed,
        out_specs=(P(None, both), P(None, both)),
        check_vma=False,
    )
```
